32 devices in a mesh: dp: 8 (over y, x, core), tensor: 4 (over z).
Axes of the slice: x: 2, y: 2, z: 4, core: 2. Of those that a mesh axis runs over, the one named last changes fastest.
Arguments:
- tokens_in: bfloat16 [12288, 1024], P(('dp', 'tensor')), may hold values from -6 to 6
- lm_grad: bfloat16 [12288, 1024], P(('dp', 'tensor')), may hold values from -6 to 6
- lm_logprob: float32 [12288], P(('dp', 'tensor')), may hold values from -4 to -0.5
- targets: int32 [12288], P(('dp', 'tensor')), may hold values from 0 to 8191
- neighbor_ids: int32 [12288, 1024], P(('dp', 'tensor')), may hold values from 0 to 8191
- nearby_entry_gaps: float32 [12288, 1024], P(('dp', 'tensor')), may hold values from 0.5 to 6.5
- seq_lengths: int32 [8, 3], P('dp'), may hold values from 0 to 1536, as said below
- attn_weights: float32 [4, 1024, 1024], P(None, 'dp', 'tensor')
- ffn_weights: float32 [2, 1024, 4096], P(None, 'dp', 'tensor')
- attn_left: float32 [4, 1024, 1024], P(None, 'dp', 'tensor'), as said below
- attn_right: float32 [4, 1024, 1024], P(None, 'tensor', 'dp'), as said below
- ffn_left: float32 [2, 1024, 1024], P(None, 'dp', 'tensor'), as said below
- ffn_right: float32 [2, 4096, 4096], P(None, 'tensor', 'dp'), as said below
- attn_left_root: float32 [4, 1024, 1024], P(None, 'dp'), as said below
- attn_right_root: float32 [4, 1024, 1024], P(None, None, 'tensor'), as said below
- ffn_left_root: float32 [2, 1024, 1024], P(None, 'dp'), as said below
- ffn_right_root: float32 [2, 4096, 4096], P(None, None, 'tensor'), as said below
- norm_params: float32 [4, 1024], replicated
- norm_moment1: float32 [4, 1024], replicated
- norm_moment2: float32 [4, 1024], replicated, as said below
- blending_coefficients: float32 [2], replicated, may hold values from -0.5 to 0.5
- knn_moment1: float32 [2], replicated
- knn_moment2: float32 [2], replicated, as said below
Outputs:
- mixed: bfloat16 [12288, 1024], P(('dp', 'tensor'))
- input_grad: float32 [12288, 1024], P(('dp', 'tensor'))
- loss: float32 [], replicated
- attn_grad: float32 [4, 1024, 1024], P(None, 'dp', 'tensor')
- attn_left_new: float32 [4, 1024, 1024], P(None, 'dp', 'tensor')
- attn_right_new: float32 [4, 1024, 1024], P(None, 'tensor', 'dp')
- attn_new: float32 [4, 1024, 1024], P(None, 'dp', 'tensor')
- ffn_grad: float32 [2, 1024, 4096], P(None, 'dp', 'tensor')
- ffn_left_new: float32 [2, 1024, 1024], P(None, 'dp', 'tensor')
- ffn_right_new: float32 [2, 4096, 4096], P(None, 'tensor', 'dp')
- ffn_new: float32 [2, 1024, 4096], P(None, 'dp', 'tensor')
- norm_moment1_new: float32 [4, 1024], replicated
- norm_moment2_new: float32 [4, 1024], replicated
- norm_new: float32 [4, 1024], replicated
- knn_moment1_new: float32 [2], replicated
- knn_moment2_new: float32 [2], replicated
- knn_new: float32 [2], replicated
The draws below stay inside these ranges and needn't reach their ends.
Inputs may be any that keep to these rules, and one draw needn't show every extreme that they name: `seq_lengths`: each row holds, in order, some sequences of length 1536, then sequences of length 512, then zeros, and sums to 1536; some row holds only sequences of length 1536. `attn_left`: symmetric. `attn_right`: symmetric. `ffn_left`: symmetric. `ffn_right`: symmetric. `attn_left_root`: symmetric. `attn_right_root`: symmetric. `ffn_left_root`: symmetric. `ffn_right_root`: symmetric. `norm_moment2`: positive. `knn_moment2`: positive.
All inputs are finite; a program needn't handle non-finite values.
Results may differ from the reference program's by a relative error of at most 0.014.
Values may be sent and summed in bfloat16 or wider, within the bound.
No kernel may reach another device: no remote copies, remote signals or barrier semaphores. Data moves between devices by JAX's collectives and lax.ppermute only.
A program may use at most 256 MiB of HBM per device.

```python
import math
import jax
import jax.numpy as jnp
from jax import lax

D = 1024
HEADS = 16
FF = 4096
ID_SPAN = 8192
NEIGH = 1024
SHORT = 512
STEP = 10
HEAD_DIM = 64
TOK_DP = 1536
LONG = 1536
SLOTS = 3
TOKENS = 12288
N_DP = 8


def knn_pair(key):
    first_key, second_key, third_key = jax.random.split(key, 3)
    target_ids = jax.random.randint(first_key, (TOKENS,), 0, ID_SPAN)
    row_index = jnp.arange(TOKENS)
    target_ids = jnp.where(row_index == 0, ID_SPAN - 1, jnp.where(row_index == 1, 0, target_ids))
    hits = jax.random.randint(second_key, (TOKENS, NEIGH), 0, 4) == 0
    column_index = jnp.arange(NEIGH)[None, :]
    hits = hits | (row_index[:, None] < 2) & (column_index == 0)
    others = jax.random.randint(third_key, (TOKENS, NEIGH), 0, ID_SPAN)
    return (target_ids.astype(jnp.int32), jnp.where(hits, target_ids[:, None], others).astype(jnp.int32))


def draw_targets(key, part):
    shared = knn_pair(key)
    return shared[0].astype(jnp.int32)


def draw_neighbor_ids(key, part):
    shared = knn_pair(key)
    return shared[1]


def draw_seq_lengths(key, part):
    key = jax.random.fold_in(key, 7)
    first_key, second_key = jax.random.split(key)
    most_long = TOK_DP // LONG
    long_count = jax.random.randint(first_key, (N_DP,), 0, most_long + 1)
    chosen = jax.random.randint(second_key, (), 0, N_DP)
    long_count = jnp.where(jnp.arange(N_DP) == chosen, most_long, long_count)
    short_count = (TOK_DP - long_count * LONG) // SHORT
    slot_index = jnp.arange(SLOTS)[None, :]
    lengths = jnp.where(slot_index < long_count[:, None], LONG, jnp.where(slot_index < (long_count + short_count)[:, None], SHORT, 0))
    return lengths.astype(jnp.int32)


def draw_attn_weights(key, part):
    key = jax.random.fold_in(key, 11)
    scales = jnp.array([1.0, 1.0, 1.0, 4.0], jnp.float32)[:, None, None] / math.sqrt(D)
    return jax.random.normal(key, (4, D, D), jnp.float32) * scales


def draw_ffn_weights(key, part):
    key = jax.random.fold_in(key, 13)
    scales = jnp.array([1.0 / math.sqrt(D), 1.0 / math.sqrt(FF)], jnp.float32)[:, None, None]
    return jax.random.normal(key, (2, D, FF), jnp.float32) * scales


def definite(key, stack_count, order, base, low_end, high_end):
    first_key, second_key = jax.random.split(key)
    diagonal = base * jnp.exp(jax.random.uniform(first_key, (stack_count, order), jnp.float32, math.log(low_end), math.log(high_end)))
    noise = jax.random.normal(second_key, (stack_count, order, order), jnp.float32)
    noise = (noise + jnp.swapaxes(noise, 1, 2)) * (0.4 * base / math.sqrt(2.0 * order))
    identity = jnp.eye(order, dtype=jnp.float32)
    return noise * (1.0 - identity) + diagonal[:, :, None] * identity


def attn_square():
    return 0.16 * TOKENS


def ffn_square():
    return 0.04 * TOKENS


def draw_attn_left(key, part):
    key = jax.random.fold_in(key, 17)
    return definite(key, 4, D, D * attn_square(), 1.0, 4.0)


def draw_attn_right(key, part):
    key = jax.random.fold_in(key, 19)
    return definite(key, 4, D, D * attn_square(), 1.0, 4.0)


def draw_ffn_left(key, part):
    key = jax.random.fold_in(key, 23)
    return definite(key, 2, D, FF * ffn_square(), 1.0, 4.0)


def draw_ffn_right(key, part):
    key = jax.random.fold_in(key, 29)
    return definite(key, 2, FF, D * ffn_square(), 1.0, 4.0)


def draw_attn_left_root(key, part):
    key = jax.random.fold_in(key, 31)
    return definite(key, 4, D, (D * attn_square()) ** (-0.25), 1.0, 2.0)


def draw_attn_right_root(key, part):
    key = jax.random.fold_in(key, 37)
    return definite(key, 4, D, (D * attn_square()) ** (-0.25), 1.0, 2.0)


def draw_ffn_left_root(key, part):
    key = jax.random.fold_in(key, 41)
    return definite(key, 2, D, (FF * ffn_square()) ** (-0.25), 1.0, 2.0)


def draw_ffn_right_root(key, part):
    key = jax.random.fold_in(key, 43)
    return definite(key, 2, FF, (D * ffn_square()) ** (-0.25), 1.0, 2.0)


def draw_norm_params(key, part):
    key = jax.random.fold_in(key, 47)
    first_key, second_key = jax.random.split(key)
    gains = jax.random.uniform(first_key, (4, D), jnp.float32, 0.7, 1.3)
    shifts = 0.2 * jax.random.normal(second_key, (4, D), jnp.float32)
    row_index = jnp.arange(4)[:, None]
    return jnp.where(row_index % 2 == 0, gains, shifts)


def signed_sizes(key, shape, size):
    first_key, second_key = jax.random.split(key)
    signs = jnp.where(jax.random.randint(first_key, shape, 0, 2) == 0, -1.0, 1.0)
    return signs * size * jnp.exp(jax.random.uniform(second_key, shape, jnp.float32, math.log(0.5), math.log(2.0)))


def positive_sizes(key, shape, size):
    return size * jnp.exp(jax.random.uniform(key, shape, jnp.float32, 0.0, math.log(4.0)))


def draw_norm_moment1(key, part):
    key = jax.random.fold_in(key, 53)
    return signed_sizes(key, (4, D), 0.111 * 0.5 * math.sqrt(TOKENS))


def draw_norm_moment2(key, part):
    key = jax.random.fold_in(key, 59)
    return positive_sizes(key, (4, D), 0.001 * 0.25 * TOKENS)


def draw_knn_moment1(key, part):
    key = jax.random.fold_in(key, 61)
    return signed_sizes(key, (2,), 0.111 * 0.1 * TOKENS)


def draw_knn_moment2(key, part):
    key = jax.random.fold_in(key, 67)
    return positive_sizes(key, (2,), 0.001 * 0.01 * TOKENS * TOKENS)


def steps_of(stream_key, dims, shards, smallest, high):
    level = 1.0
    for dim, blocks in shards:
        heights = jax.random.uniform(jax.random.fold_in(jax.random.fold_in(stream_key, 6), dim), (blocks,), jnp.float32, smallest / len(shards), high / len(shards))
        level = level * jnp.repeat(jnp.exp(heights), dims[dim] // blocks).reshape((-1,) + (1,) * (len(dims) - 1 - dim))
    return level


def scatter_about(own_key, extent, deviation, reach, shards=(), held_as=jnp.bfloat16):
    result = jax.random.normal(own_key, extent, jnp.float32) * deviation
    if len(shards) > 0:
        result = steps_of(own_key, extent, shards, -0.22, 0.18) * result
    return jnp.clip(result, min=-reach, max=reach).astype(held_as)


def setup_inputs(seed: int = 0) -> dict:
    arg_keys = jax.random.split(jax.random.key(seed), 24)
    tokens_in = scatter_about(arg_keys[0], (TOKENS, D), 1.0, 6.0, ((0, 32),))
    lm_grad = scatter_about(arg_keys[1], (TOKENS, D), 1.0, 6.0, ((0, 32),))
    lm_logprob = jnp.clip(-4.0 + 3.5 * jax.random.uniform(arg_keys[2], (TOKENS,), jnp.float32) ** steps_of(arg_keys[2], (TOKENS,), ((0, 32),), -0.2, 0.2), -4.0, -0.5)
    targets = draw_targets(jax.random.fold_in(arg_keys[23], 71), 0)
    neighbor_ids = draw_neighbor_ids(jax.random.fold_in(arg_keys[23], 71), 0)
    nearby_entry_gaps = jnp.clip(0.5 + 6.0 * jax.random.uniform(arg_keys[5], (TOKENS, NEIGH), jnp.float32) ** steps_of(arg_keys[5], (TOKENS, NEIGH), ((0, 32),), -0.2, 0.2), 0.5, 6.5)
    seq_lengths = draw_seq_lengths(jax.random.fold_in(arg_keys[23], 71), 0)
    attn_weights = draw_attn_weights(jax.random.fold_in(arg_keys[23], 71), 0)
    ffn_weights = draw_ffn_weights(jax.random.fold_in(arg_keys[23], 71), 0)
    attn_left = draw_attn_left(jax.random.fold_in(arg_keys[23], 71), 0)
    attn_right = draw_attn_right(jax.random.fold_in(arg_keys[23], 71), 0)
    ffn_left = draw_ffn_left(jax.random.fold_in(arg_keys[23], 71), 0)
    ffn_right = draw_ffn_right(jax.random.fold_in(arg_keys[23], 71), 0)
    attn_left_root = draw_attn_left_root(jax.random.fold_in(arg_keys[23], 71), 0)
    attn_right_root = draw_attn_right_root(jax.random.fold_in(arg_keys[23], 71), 0)
    ffn_left_root = draw_ffn_left_root(jax.random.fold_in(arg_keys[23], 71), 0)
    ffn_right_root = draw_ffn_right_root(jax.random.fold_in(arg_keys[23], 71), 0)
    norm_params = draw_norm_params(jax.random.fold_in(arg_keys[23], 71), 0)
    norm_moment1 = draw_norm_moment1(jax.random.fold_in(arg_keys[23], 71), 0)
    norm_moment2 = draw_norm_moment2(jax.random.fold_in(arg_keys[23], 71), 0)
    blending_coefficients = jnp.clip(jax.random.uniform(arg_keys[20], (2,), jnp.float32, -0.5, 0.5), -0.5, 0.5)
    knn_moment1 = draw_knn_moment1(jax.random.fold_in(arg_keys[23], 71), 0)
    knn_moment2 = draw_knn_moment2(jax.random.fold_in(arg_keys[23], 71), 0)
    return {"tokens_in": tokens_in, "lm_grad": lm_grad, "lm_logprob": lm_logprob, "targets": targets, "neighbor_ids": neighbor_ids, "nearby_entry_gaps": nearby_entry_gaps, "seq_lengths": seq_lengths, "attn_weights": attn_weights, "ffn_weights": ffn_weights, "attn_left": attn_left, "attn_right": attn_right, "ffn_left": ffn_left, "ffn_right": ffn_right, "attn_left_root": attn_left_root, "attn_right_root": attn_right_root, "ffn_left_root": ffn_left_root, "ffn_right_root": ffn_right_root, "norm_params": norm_params, "norm_moment1": norm_moment1, "norm_moment2": norm_moment2, "blending_coefficients": blending_coefficients, "knn_moment1": knn_moment1, "knn_moment2": knn_moment2}


adam_rate = 0.3
shampoo_rate = 0.5
shampoo_decay = 0.01
norm_eps = 1e-05

@jax.custom_vjp
def low(v):
    return lax.optimization_barrier(v.astype(jnp.bfloat16)).astype(jnp.float32)

@jax.custom_vjp
def low_back(v):
    return v

def low_keep(v):
    return (low(v), None)

def low_pass(kept, grad):
    return (grad,)

def back_keep(v):
    return (v, None)

def back_low(kept, grad):
    return (low(grad),)
low.defvjp(low_keep, low_pass)
low_back.defvjp(back_keep, back_low)

def exact_dot(left_mat, right_mat):
    return jnp.dot(left_mat, right_mat, precision=lax.Precision.HIGHEST)

def layer_norm(values_in, gain, shift):
    centre = lax.optimization_barrier(jnp.mean(values_in, axis=-1, keepdims=True))
    centred = values_in - centre
    spread_sq = lax.optimization_barrier(jnp.mean(centred * centred, axis=-1, keepdims=True))
    return centred * lax.rsqrt(spread_sq + norm_eps) * gain + shift

def gelu_tanh(values_in):
    return jax.nn.gelu(values_in, approximate=True)

def segment_ids(seq_lengths):
    seq_ends = jnp.cumsum(seq_lengths, axis=1)
    places = jnp.arange(TOK_DP, dtype=jnp.int32)
    return lax.optimization_barrier(jnp.sum((places[None, :, None] >= seq_ends[:, None, :]).astype(jnp.int32), axis=2)).astype(jnp.int32)

def attention(query_in, key_in, value_in, segment):
    score_scale = HEAD_DIM ** (-0.5)
    front = LONG - SHORT
    query_all = query_in.reshape(TOK_DP, HEADS, HEAD_DIM)
    key_all = jnp.pad(key_in.reshape(TOK_DP, HEADS, HEAD_DIM), ((front, 0), (0, 0), (0, 0)))
    value_all = jnp.pad(value_in.reshape(TOK_DP, HEADS, HEAD_DIM), ((front, 0), (0, 0), (0, 0)))
    key_segment = jnp.pad(segment, (front, 0), constant_values=-1)

    def one_block(row_start):
        query_rows = lax.dynamic_slice_in_dim(query_all, row_start, SHORT, 0)
        key_rows = lax.dynamic_slice_in_dim(key_all, row_start, LONG, 0)
        value_rows = lax.dynamic_slice_in_dim(value_all, row_start, LONG, 0)
        query_seg = lax.dynamic_slice_in_dim(segment, row_start, SHORT, 0)
        key_seg = lax.dynamic_slice_in_dim(key_segment, row_start, LONG, 0)
        query_pos = row_start + jnp.arange(SHORT, dtype=jnp.int32)
        key_pos = row_start - front + jnp.arange(LONG, dtype=jnp.int32)
        allowed = (key_seg[None, :] == query_seg[:, None]) & (key_pos[None, :] <= query_pos[:, None])
        scores = low_back(jnp.einsum('qhd,khd->hqk', query_rows, key_rows, precision=lax.Precision.HIGHEST) * score_scale)
        scores = jnp.where(allowed[None], scores, -1e+30)
        attn_probs = low(jax.nn.softmax(scores, axis=-1))
        return jnp.einsum('hqk,khd->qhd', attn_probs, value_rows, precision=lax.Precision.HIGHEST)
    row_starts = jnp.arange(TOK_DP // SHORT, dtype=jnp.int32) * SHORT
    heads_out = lax.map(jax.checkpoint(one_block), row_starts)
    return heads_out.reshape(TOK_DP, D)

def shard_block(resid, segment, attn_low, ffn_low, norm_p):
    normed1 = low(layer_norm(resid, norm_p[0], norm_p[1]))
    query_f = low_back(low(exact_dot(normed1, attn_low[0])))
    key_f = low_back(low(exact_dot(normed1, attn_low[1])))
    value_f = low_back(low(exact_dot(normed1, attn_low[2])))
    heads_out = low_back(low(attention(query_f, key_f, value_f, segment)))
    attn_out = low_back(exact_dot(heads_out, attn_low[3].T))
    middle = resid + attn_out
    normed2 = low(layer_norm(middle, norm_p[2], norm_p[3]))
    hidden_pre = low_back(exact_dot(normed2, ffn_low[0]))
    hidden_act = low(gelu_tanh(hidden_pre))
    ffn_out = low_back(exact_dot(hidden_act, ffn_low[1].T))
    return middle + ffn_out

def adamw_step(params_in, grads_in, first_in, second_in):
    first_new = 0.9 * first_in + 0.1 * grads_in
    second_new = 0.999 * second_in + 0.001 * grads_in * grads_in
    first_hat = first_new / (1.0 - 0.9 ** STEP)
    second_hat = second_new / (1.0 - 0.999 ** STEP)
    return (first_new, second_new, params_in - adam_rate * first_hat / (jnp.sqrt(second_hat) + 1e-08))

def shampoo(weights_in, grads_in, left_in, right_in, left_root, right_root):
    left_new = 0.5 * left_in + 0.5 * jnp.einsum('sij,skj->sik', grads_in, grads_in, precision=lax.Precision.HIGHEST)
    right_new = 0.5 * right_in + 0.5 * jnp.einsum('sji,sjk->sik', grads_in, grads_in, precision=lax.Precision.HIGHEST)
    turned = jnp.einsum('sjk,skl->sjl', grads_in, right_root, precision=lax.Precision.HIGHEST)
    update = jnp.einsum('sij,sjl->sil', left_root, turned, precision=lax.Precision.HIGHEST)
    return (left_new, right_new, weights_in - shampoo_rate * (update + shampoo_decay * weights_in))

def reference(tokens_in, lm_grad, lm_logprob, targets, neighbor_ids, nearby_entry_gaps, seq_lengths, attn_weights, ffn_weights, attn_left, attn_right, ffn_left, ffn_right, attn_left_root, attn_right_root, ffn_left_root, ffn_right_root, norm_params, norm_moment1, norm_moment2, blending_coefficients, knn_moment1, knn_moment2):
    segments = segment_ids(seq_lengths)
    target_matches = (neighbor_ids == targets[:, None]).astype(jnp.float32)

    def knn_loss(nearby_entry_chance, log_prob):
        sharpness_divisor = jnp.exp(nearby_entry_chance[0])
        interp = jax.nn.sigmoid(nearby_entry_chance[1])
        nearby_entry_shares = jax.nn.softmax(-nearby_entry_gaps / sharpness_divisor, axis=-1)
        retrieval_probability = lax.optimization_barrier(jnp.sum(nearby_entry_shares * target_matches, axis=-1))
        mixture = interp * retrieval_probability + (1.0 - interp) * jnp.exp(log_prob)
        return jnp.sum(-jnp.log(mixture))
    total_loss, loss_pull = jax.vjp(knn_loss, blending_coefficients, lm_logprob)
    knn_grad, lm_weight = loss_pull(jnp.ones_like(total_loss))
    cotangent = lm_weight[:, None] * lm_grad.astype(jnp.float32)

    def whole_block(resid, attn_w, ffn_w, norm_p):
        attn_low = low(attn_w)
        ffn_low = low(ffn_w)

        def one_shard(inputs):
            part_rows, segment = inputs
            return shard_block(part_rows, segment, attn_low, ffn_low, norm_p)
        outs = lax.map(jax.checkpoint(one_shard), (resid.reshape(N_DP, TOK_DP, D), segments))
        return outs.reshape(TOKENS, D)
    block_out, block_pull = jax.vjp(whole_block, tokens_in.astype(jnp.float32), attn_weights, ffn_weights, norm_params)
    input_grad, attn_grad, ffn_grad, norm_grad = block_pull(cotangent)
    attn_left_new, attn_right_new, attn_new = shampoo(attn_weights, attn_grad, attn_left, attn_right, attn_left_root, attn_right_root)
    ffn_left_new, ffn_right_new, ffn_new = shampoo(ffn_weights, ffn_grad, ffn_left, ffn_right, ffn_left_root, ffn_right_root)
    norm_m1, norm_m2, norm_new = adamw_step(norm_params, norm_grad, norm_moment1, norm_moment2)
    knn_m1, knn_m2, knn_new = adamw_step(blending_coefficients, knn_grad, knn_moment1, knn_moment2)
    return (block_out.astype(jnp.bfloat16), input_grad, total_loss / TOKENS, attn_grad, attn_left_new, attn_right_new, attn_new, ffn_grad, ffn_left_new, ffn_right_new, ffn_new, norm_m1, norm_m2, norm_new, knn_m1, knn_m2, knn_new)
```

```python
import jax
import jax.numpy as jnp
from jax import lax
from jax.experimental import pallas as pl
from jax.experimental.pallas import tpu as pltpu
from jax.sharding import PartitionSpec as P

SHORT = 512
STEP = 10
HEAD_DIM = 64


adam_rate = 0.3
shampoo_rate = 0.5
shampoo_decay = 0.01
norm_eps = 1e-05


def layer_norm(values_in, gain, shift):
    centre = jnp.mean(values_in, axis=-1, keepdims=True)
    centred = values_in - centre
    spread_sq = jnp.mean(centred * centred, axis=-1, keepdims=True)
    return centred * lax.rsqrt(spread_sq + norm_eps) * gain + shift


def gelu_tanh(values_in):
    return jax.nn.gelu(values_in, approximate=True)


def spread_rows(local_low):
    return lax.all_gather(local_low, "tensor", axis=0, tiled=True)


def spread_again(local_low):
    return lax.all_gather(local_low, "tensor", axis=0, tiled=True)


def spread_grads(local_low):
    return lax.all_gather(local_low, "tensor", axis=0, tiled=True)


def branch_total(left_rows, right_mat):
    return lax.psum_scatter(
        jnp.einsum("rc,dc->rd", left_rows, right_mat, preferred_element_type=jnp.float32),
        "tensor",
        scatter_dimension=0,
        tiled=True,
    )


def input_total(left_rows, right_mat):
    return lax.psum_scatter(
        jnp.einsum("rc,dc->rd", left_rows, right_mat, preferred_element_type=jnp.float32),
        "tensor",
        scatter_dimension=0,
        tiled=True,
    )


def first_blocks(seq_lengths, group_rows, block_rows):
    lengths = seq_lengths[0]
    seq_ends = jnp.cumsum(lengths)
    seq_begins = seq_ends - lengths
    block_begins = jnp.arange(group_rows // block_rows, dtype=jnp.int32) * block_rows
    inside = (seq_begins[None, :] <= block_begins[:, None]) & (lengths[None, :] > 0)
    return jnp.max(jnp.where(inside, seq_begins[None, :], 0), axis=1) // block_rows


def block_scores(query_rows, key_rows, query_block, key_block, block_rows, score_scale):
    scores = (
        jnp.einsum("qhd,khd->hqk", query_rows, key_rows, preferred_element_type=jnp.float32)
        * score_scale
    )
    query_pos = query_block * block_rows + jnp.arange(block_rows, dtype=jnp.int32)
    key_pos = key_block * block_rows + jnp.arange(block_rows, dtype=jnp.int32)
    allowed = key_pos[None, :] <= query_pos[:, None]
    return jnp.where(allowed[None], scores, -1e30)


def attend_forward(query_all, key_all, value_all, first_block, block_rows, score_scale):
    group_rows, head_count, head_width = query_all.shape

    def one_block(query_block):
        query_rows = lax.dynamic_slice_in_dim(query_all, query_block * block_rows, block_rows, 0)

        def peak_step(key_block, loop_state):
            running_top, running_mass = loop_state
            key_rows = lax.dynamic_slice_in_dim(key_all, key_block * block_rows, block_rows, 0)
            scores = block_scores(
                query_rows, key_rows, query_block, key_block, block_rows, score_scale
            )
            new_top = jnp.maximum(running_top, jnp.max(scores, axis=2))
            new_mass = running_mass * jnp.exp(running_top - new_top) + jnp.sum(
                jnp.exp(scores - new_top[:, :, None]), axis=2
            )
            return (new_top, new_mass)

        start_state = (
            jnp.full((head_count, block_rows), -1e30, jnp.float32),
            jnp.zeros((head_count, block_rows), jnp.float32),
        )
        final_top, final_mass = lax.fori_loop(
            first_block[query_block], query_block + 1, peak_step, start_state
        )
        log_mass = final_top + jnp.log(final_mass)

        def value_step(key_block, out_acc):
            key_rows = lax.dynamic_slice_in_dim(key_all, key_block * block_rows, block_rows, 0)
            value_rows = lax.dynamic_slice_in_dim(value_all, key_block * block_rows, block_rows, 0)
            scores = block_scores(
                query_rows, key_rows, query_block, key_block, block_rows, score_scale
            )
            attn_probs = jnp.exp(scores - log_mass[:, :, None]).astype(jnp.bfloat16)
            return out_acc + jnp.einsum(
                "hqk,khd->qhd", attn_probs, value_rows, preferred_element_type=jnp.float32
            )

        out_rows = lax.fori_loop(
            first_block[query_block],
            query_block + 1,
            value_step,
            jnp.zeros((block_rows, head_count, head_width), jnp.float32),
        )
        return (out_rows.astype(jnp.bfloat16), log_mass)

    outs, log_masses = lax.map(one_block, jnp.arange(group_rows // block_rows, dtype=jnp.int32))
    return (outs.reshape(group_rows, head_count, head_width), log_masses)


def attend_backward(
    query_all, key_all, value_all, grad_out, log_masses, first_block, block_rows, score_scale
):
    group_rows, head_count, head_width = query_all.shape

    def one_block(query_block, loop_carry):
        grad_keys, grad_values, grad_query = loop_carry
        query_rows = lax.dynamic_slice_in_dim(query_all, query_block * block_rows, block_rows, 0)
        grad_rows = lax.dynamic_slice_in_dim(grad_out, query_block * block_rows, block_rows, 0)
        log_mass = log_masses[query_block]

        def chances(key_block):
            key_rows = lax.dynamic_slice_in_dim(key_all, key_block * block_rows, block_rows, 0)
            value_rows = lax.dynamic_slice_in_dim(value_all, key_block * block_rows, block_rows, 0)
            scores = block_scores(
                query_rows, key_rows, query_block, key_block, block_rows, score_scale
            )
            attn_probs = jnp.exp(scores - log_mass[:, :, None])
            likelihood_cotangent = jnp.einsum(
                "qhd,khd->hqk", grad_rows, value_rows, preferred_element_type=jnp.float32
            )
            return (key_rows, attn_probs, likelihood_cotangent)

        def inner_step(key_block, inner_acc):
            _, attn_probs, likelihood_cotangent = chances(key_block)
            return inner_acc + jnp.sum(attn_probs * likelihood_cotangent, axis=2)

        row_inner = lax.fori_loop(
            first_block[query_block],
            query_block + 1,
            inner_step,
            jnp.zeros((head_count, block_rows), jnp.float32),
        )

        def grad_step(key_block, loop_state):
            query_acc, keys_acc, values_acc = loop_state
            key_rows, attn_probs, likelihood_cotangent = chances(key_block)
            grad_scores = (attn_probs * (likelihood_cotangent - row_inner[:, :, None])).astype(
                jnp.bfloat16
            )
            query_acc = (
                query_acc
                + jnp.einsum(
                    "hqk,khd->qhd", grad_scores, key_rows, preferred_element_type=jnp.float32
                )
                * score_scale
            )
            key_part = (
                jnp.einsum(
                    "hqk,qhd->khd", grad_scores, query_rows, preferred_element_type=jnp.float32
                )
                * score_scale
            )
            value_part = jnp.einsum(
                "hqk,qhd->khd",
                attn_probs.astype(jnp.bfloat16),
                grad_rows,
                preferred_element_type=jnp.float32,
            )
            key_start = key_block * block_rows
            keys_acc = lax.dynamic_update_slice_in_dim(
                keys_acc,
                lax.dynamic_slice_in_dim(keys_acc, key_start, block_rows, 0) + key_part,
                key_start,
                0,
            )
            values_acc = lax.dynamic_update_slice_in_dim(
                values_acc,
                lax.dynamic_slice_in_dim(values_acc, key_start, block_rows, 0) + value_part,
                key_start,
                0,
            )
            return (query_acc, keys_acc, values_acc)

        query_acc, grad_keys, grad_values = lax.fori_loop(
            first_block[query_block],
            query_block + 1,
            grad_step,
            (jnp.zeros((block_rows, head_count, head_width), jnp.float32), grad_keys, grad_values),
        )
        grad_query = lax.dynamic_update_slice_in_dim(
            grad_query, query_acc, query_block * block_rows, 0
        )
        return (grad_keys, grad_values, grad_query)

    zeros_all = jnp.zeros((group_rows, head_count, head_width), jnp.float32)
    return lax.fori_loop(0, group_rows // block_rows, one_block, (zeros_all, zeros_all, zeros_all))


def right_statistics(attn_part_grad, ffn_part_grad, attn_rows, ffn_rows):
    attn_part = jnp.einsum(
        "sri,srj->sij", attn_part_grad, attn_rows, precision=lax.Precision.HIGHEST
    )
    ffn_part = jnp.einsum("sri,srj->sij", ffn_part_grad, ffn_rows, precision=lax.Precision.HIGHEST)
    return (
        lax.psum_scatter(
            attn_part.astype(jnp.bfloat16), "dp", scatter_dimension=2, tiled=True
        ).astype(jnp.float32),
        lax.psum_scatter(
            ffn_part.astype(jnp.bfloat16), "dp", scatter_dimension=2, tiled=True
        ).astype(jnp.float32),
    )


def left_statistics(attn_part_grad, ffn_part_grad, attn_cols, ffn_cols):
    attn_part = jnp.einsum(
        "sri,sqi->srq", attn_part_grad, attn_cols, precision=lax.Precision.HIGHEST
    )
    ffn_part = jnp.einsum("sri,sqi->srq", ffn_part_grad, ffn_cols, precision=lax.Precision.HIGHEST)
    return (
        lax.psum_scatter(
            attn_part.astype(jnp.bfloat16), "tensor", scatter_dimension=2, tiled=True
        ).astype(jnp.float32),
        lax.psum_scatter(
            ffn_part.astype(jnp.bfloat16), "tensor", scatter_dimension=2, tiled=True
        ).astype(jnp.float32),
    )


def adamw_step(params_in, grads_in, first_in, second_in):
    first_new = 0.9 * first_in + 0.1 * grads_in
    second_new = 0.999 * second_in + 0.001 * grads_in * grads_in
    first_hat = first_new / (1.0 - 0.9**STEP)
    second_hat = second_new / (1.0 - 0.999**STEP)
    return (
        first_new,
        second_new,
        params_in - adam_rate * first_hat / (jnp.sqrt(second_hat) + 1e-08),
    )


def local(
    tokens_in,
    lm_grad,
    lm_logprob,
    targets,
    neighbor_ids,
    nearby_entry_gaps,
    seq_lengths,
    attn_weights,
    ffn_weights,
    attn_left,
    attn_right,
    ffn_left,
    ffn_right,
    attn_left_root,
    attn_right_root,
    ffn_left_root,
    ffn_right_root,
    norm_params,
    norm_moment1,
    norm_moment2,
    blending_coefficients,
    knn_moment1,
    knn_moment2,
):
    local_rows = tokens_in.shape[0]
    group_rows = local_rows * lax.axis_size("tensor")
    block_rows = SHORT
    score_scale = HEAD_DIM ** (-0.5)
    attn_full, ffn_full = (
        lax.all_gather(attn_weights.astype(jnp.bfloat16), "dp", axis=1, tiled=True),
        lax.all_gather(ffn_weights.astype(jnp.bfloat16), "dp", axis=1, tiled=True),
    )
    proj_in = jnp.concatenate([attn_full[0], attn_full[1], attn_full[2]], axis=1)
    proj_out = attn_full[3]
    head_cols = proj_out.shape[1]
    head_count = head_cols // HEAD_DIM
    first_block = first_blocks(seq_lengths, group_rows, block_rows)
    resid = tokens_in.astype(jnp.float32)
    normed1, norm1_back = jax.vjp(layer_norm, resid, norm_params[0], norm_params[1])
    normed1_low = normed1.astype(jnp.bfloat16)
    normed1_all = spread_rows(normed1_low)
    qkv_low = jnp.dot(normed1_all, proj_in, preferred_element_type=jnp.float32).astype(jnp.bfloat16)
    query_all = qkv_low[:, :head_cols].reshape(group_rows, head_count, HEAD_DIM)
    key_all = qkv_low[:, head_cols : 2 * head_cols].reshape(group_rows, head_count, HEAD_DIM)
    value_all = qkv_low[:, 2 * head_cols :].reshape(group_rows, head_count, HEAD_DIM)
    heads_out, log_masses = attend_forward(
        query_all, key_all, value_all, first_block, block_rows, score_scale
    )
    heads_flat = heads_out.reshape(group_rows, head_cols)
    attn_out = branch_total(heads_flat, proj_out)
    middle = resid + attn_out
    normed2, norm2_back = jax.vjp(layer_norm, middle, norm_params[2], norm_params[3])
    normed2_low = normed2.astype(jnp.bfloat16)
    w_up = ffn_full[0]
    w_down = ffn_full[1]
    normed2_all = spread_rows(normed2_low)
    hidden_pre = jnp.dot(normed2_all, w_up, preferred_element_type=jnp.float32)
    hidden_act, gelu_back = jax.vjp(gelu_tanh, hidden_pre)
    act_low = hidden_act.astype(jnp.bfloat16)
    ffn_out = branch_total(act_low, w_down)
    mixed = (middle + ffn_out).astype(jnp.bfloat16)
    sharpness_divisor = jnp.exp(blending_coefficients[0])
    interp = jax.nn.sigmoid(blending_coefficients[1])
    nearby_entry_logits = -nearby_entry_gaps / sharpness_divisor
    near_top = jnp.max(nearby_entry_logits, axis=1, keepdims=True)
    near_exp = jnp.exp(nearby_entry_logits - near_top)
    nearby_entry_shares = near_exp / jnp.sum(near_exp, axis=1, keepdims=True)
    target_matches = (neighbor_ids == targets[:, None]).astype(jnp.float32)
    retrieval_probability = jnp.sum(nearby_entry_shares * target_matches, axis=1)
    lm_prob = jnp.exp(lm_logprob)
    mixture = interp * retrieval_probability + (1.0 - interp) * lm_prob
    token_loss = -jnp.log(mixture)
    lm_weight = -(1.0 - interp) * lm_prob / mixture
    temp_terms = (
        jnp.sum(
            nearby_entry_shares
            * (target_matches - retrieval_probability[:, None])
            * nearby_entry_gaps,
            axis=1,
        )
        / sharpness_divisor
    )
    temp_grad = jnp.sum(-(interp / mixture) * temp_terms)
    interp_grad = jnp.sum(-interp * (1.0 - interp) * (retrieval_probability - lm_prob) / mixture)
    knn_grads = jnp.stack([temp_grad, interp_grad])
    cotangent = lm_weight[:, None] * lm_grad.astype(jnp.float32)
    cot_all = spread_grads(cotangent.astype(jnp.bfloat16))
    grad_act = jnp.dot(cot_all, w_down, preferred_element_type=jnp.float32)
    grad_pre_low = gelu_back(grad_act)[0].astype(jnp.bfloat16)
    normed2_used = spread_again(normed2_low)
    grad_up = jnp.einsum(
        "rd,rf->df", normed2_used, grad_pre_low, preferred_element_type=jnp.float32
    )
    grad_down = jnp.einsum("rd,rf->df", cot_all, act_low, preferred_element_type=jnp.float32)
    ffn_local = jnp.stack([grad_up, grad_down])
    grad_normed2 = input_total(grad_pre_low, w_up)
    mid_norm_grad, gain2_grad, shift2_grad = norm2_back(grad_normed2)
    grad_middle = cotangent + mid_norm_grad
    grad_mid_all = spread_grads(grad_middle.astype(jnp.bfloat16))
    grad_heads = jnp.dot(grad_mid_all, proj_out, preferred_element_type=jnp.float32).astype(
        jnp.bfloat16
    )
    grad_out_proj = jnp.einsum(
        "rd,rc->dc", grad_mid_all, heads_flat, preferred_element_type=jnp.float32
    )
    grad_keys, grad_values, grad_query = attend_backward(
        query_all,
        key_all,
        value_all,
        grad_heads.reshape(group_rows, head_count, HEAD_DIM),
        log_masses,
        first_block,
        block_rows,
        score_scale,
    )
    grad_qkv = jnp.concatenate(
        [
            grad_query.reshape(group_rows, head_cols),
            grad_keys.reshape(group_rows, head_cols),
            grad_values.reshape(group_rows, head_cols),
        ],
        axis=1,
    ).astype(jnp.bfloat16)
    normed1_used = spread_again(normed1_low)
    grad_proj_in = jnp.einsum(
        "rd,rc->dc", normed1_used, grad_qkv, preferred_element_type=jnp.float32
    )
    grad_normed1 = input_total(grad_qkv, proj_in)
    res_norm_grad, gain1_grad, bias_first_cotangent = norm1_back(grad_normed1)
    input_grad = grad_middle + res_norm_grad
    norm_grads = jnp.stack([gain1_grad, bias_first_cotangent, gain2_grad, shift2_grad])
    norm_total, knn_total, loss_total = lax.psum(
        (norm_grads, knn_grads, jnp.sum(token_loss)), ("dp", "tensor")
    )
    token_count = group_rows * lax.axis_size("dp")
    attn_local = jnp.stack(
        [
            grad_proj_in[:, :head_cols],
            grad_proj_in[:, head_cols : 2 * head_cols],
            grad_proj_in[:, 2 * head_cols :],
            grad_out_proj,
        ]
    )
    attn_grad, ffn_grad = (
        lax.psum_scatter(attn_local, "dp", scatter_dimension=1, tiled=True),
        lax.psum_scatter(ffn_local, "dp", scatter_dimension=1, tiled=True),
    )
    attn_rows, ffn_rows = (
        lax.all_gather(attn_grad.astype(jnp.bfloat16), "tensor", axis=2, tiled=True).astype(
            attn_grad.dtype
        ),
        lax.all_gather(ffn_grad.astype(jnp.bfloat16), "tensor", axis=2, tiled=True).astype(
            ffn_grad.dtype
        ),
    )
    attn_right_sum, ffn_right_sum = right_statistics(attn_grad, ffn_grad, attn_rows, ffn_rows)
    attn_turned = jnp.einsum(
        "sri,sij->srj", attn_rows, attn_right_root, precision=lax.Precision.HIGHEST
    )
    ffn_turned = jnp.einsum(
        "sri,sij->srj", ffn_rows, ffn_right_root, precision=lax.Precision.HIGHEST
    )
    attn_cols, ffn_cols, attn_turned_cols, ffn_turned_cols = (
        lax.all_gather(attn_grad.astype(jnp.bfloat16), "dp", axis=1, tiled=True).astype(
            attn_grad.dtype
        ),
        lax.all_gather(ffn_grad.astype(jnp.bfloat16), "dp", axis=1, tiled=True).astype(
            ffn_grad.dtype
        ),
        lax.all_gather(attn_turned.astype(jnp.bfloat16), "dp", axis=1, tiled=True).astype(
            attn_turned.dtype
        ),
        lax.all_gather(ffn_turned.astype(jnp.bfloat16), "dp", axis=1, tiled=True).astype(
            ffn_turned.dtype
        ),
    )
    attn_left_sum, ffn_left_sum = left_statistics(attn_grad, ffn_grad, attn_cols, ffn_cols)
    attn_update = jnp.einsum(
        "srq,sqi->sri", attn_left_root, attn_turned_cols, precision=lax.Precision.HIGHEST
    )
    ffn_update = jnp.einsum(
        "srq,sqi->sri", ffn_left_root, ffn_turned_cols, precision=lax.Precision.HIGHEST
    )
    attn_left_new = 0.5 * attn_left + 0.5 * attn_left_sum
    attn_right_new = 0.5 * attn_right + 0.5 * attn_right_sum
    ffn_left_new = 0.5 * ffn_left + 0.5 * ffn_left_sum
    ffn_right_new = 0.5 * ffn_right + 0.5 * ffn_right_sum
    attn_new = attn_weights - shampoo_rate * (attn_update + shampoo_decay * attn_weights)
    ffn_new = ffn_weights - shampoo_rate * (ffn_update + shampoo_decay * ffn_weights)
    norm_m1, norm_m2, norm_new = adamw_step(norm_params, norm_total, norm_moment1, norm_moment2)
    knn_m1, knn_m2, knn_new = adamw_step(blending_coefficients, knn_total, knn_moment1, knn_moment2)
    return (
        mixed,
        input_grad,
        loss_total / token_count,
        attn_grad,
        attn_left_new,
        attn_right_new,
        attn_new,
        ffn_grad,
        ffn_left_new,
        ffn_right_new,
        ffn_new,
        norm_m1,
        norm_m2,
        norm_new,
        knn_m1,
        knn_m2,
        knn_new,
    )


LINE_BIT, HALF_BIT, CORE_BIT, X_BIT, Y_BIT = 1, 2, 4, 8, 16


def flip(values_in, mask):
    return lax.ppermute(
        values_in, ("dp", "tensor"), [(index, index ^ mask) for index in range(32)]
    )


def swap_core_half(values_in):
    pairs = []
    for index in range(32):
        core, half = (index >> 2) & 1, (index >> 1) & 1
        pairs.append((index, (index & 25) | (half << 2) | (core << 1)))
    return lax.ppermute(values_in, ("dp", "tensor"), pairs)


def pick(values_in, index, axis):
    return lax.dynamic_index_in_dim(values_in, index, axis, keepdims=False)


def ordered_pair(own, other, bit, axis):
    return jnp.where(
        bit == 0, jnp.stack([own, other], axis=axis), jnp.stack([other, own], axis=axis)
    )


def gather_group(own):
    near = flip(own, LINE_BIT)
    far = flip(own, CORE_BIT)
    both = flip(near, CORE_BIT)
    return jnp.concatenate([own, near, far, both], axis=0)


def reduce_group(partial_of, rows):
    sent = partial_of(2 * rows, 4 * rows).astype(jnp.bfloat16)
    received = flip(sent, CORE_BIT)
    near = partial_of(rows, 2 * rows) + received[rows:].astype(jnp.float32)
    from_near = flip(near.astype(jnp.bfloat16), LINE_BIT)
    own = partial_of(0, rows) + received[:rows].astype(jnp.float32)
    return own + from_near.astype(jnp.float32)


def gather_weight(local_low, place, first, second):
    stack_count, own_rows, width = local_low.shape
    halves = local_low.reshape(stack_count, own_rows, 2, width // 2)
    mine = pick(halves, place["core"], 2)
    theirs = flip(pick(halves, 1 - place["core"], 2), CORE_BIT)
    both_cores = ordered_pair(mine, theirs, place["core"], 1).reshape(
        stack_count, 2 * own_rows, width // 2
    )
    block = ordered_pair(both_cores, flip(both_cores, HALF_BIT), place["half"], 2).reshape(
        stack_count, 2 * own_rows, width
    )
    first_block = flip(block, first)
    second_block = flip(block, second)
    third_block = flip(first_block, second)
    whole = jnp.zeros((stack_count, 8 * own_rows, width), local_low.dtype)
    for part, mask in (
        (block, 0),
        (first_block, first),
        (second_block, second),
        (third_block, first ^ second),
    ):
        start = (place["chip"] ^ (mask // X_BIT)) * (2 * own_rows)
        whole = lax.dynamic_update_slice_in_dim(whole, part, start, 1)
    return whole


def scatter_grad(partial, place, first):
    stack_count, rows, width = partial.shape
    parts = partial.reshape(stack_count, 2, 2, rows // 4, width)
    at = {X_BIT: (2, place["x"]), Y_BIT: (1, place["y"])}
    second = X_BIT + Y_BIT - first
    axis, bit = at[first]
    kept = pick(parts, bit, axis)
    received = flip(pick(parts, 1 - bit, axis).astype(jnp.bfloat16), first)
    kept = kept + received.astype(jnp.float32)
    _, bit = at[second]
    received = flip(pick(kept, 1 - bit, 1).astype(jnp.bfloat16), second)
    kept = pick(kept, bit, 1) + received.astype(jnp.float32)
    halves = kept.reshape(stack_count, 2, rows // 8, width)
    received = flip(pick(halves, 1 - place["half"], 1).astype(jnp.bfloat16), HALF_BIT)
    return (pick(halves, place["half"], 1) + received.astype(jnp.float32)).astype(jnp.bfloat16)


def gather_grad(own, place, first):
    stack_count, own_rows, width = own.shape
    second = X_BIT + Y_BIT - first
    own = own.reshape(stack_count, 1, own_rows, 2, 1, width // 2)
    other_half = flip(own, HALF_BIT)
    near = flip(own, LINE_BIT)
    near_half = flip(other_half, LINE_BIT)
    line = jnp.zeros((stack_count, 2, own_rows, 2, 2, width // 2), own.dtype)
    half, line_bit = place["half"], place["line"]
    for part, row, col in (
        (own, half, line_bit),
        (other_half, 1 - half, line_bit),
        (near, half, 1 - line_bit),
        (near_half, 1 - half, 1 - line_bit),
    ):
        line = lax.dynamic_update_slice(line, part, (0, row, 0, 0, col, 0))
    line = line.reshape(stack_count, 1, 1, 2 * own_rows, 4, width // 2)
    first_block = flip(line, first)
    second_block = flip(line, second)
    third_block = flip(first_block, second)
    whole = jnp.zeros((stack_count, 2, 4, 2 * own_rows, 4, width // 2), own.dtype)
    for part, mask in (
        (line, 0),
        (first_block, first),
        (second_block, second),
        (third_block, first ^ second),
    ):
        chip = place["chip"] ^ (mask // X_BIT)
        whole = lax.dynamic_update_slice(whole, part, (0, place["core"], chip, 0, 0, 0))
        whole = lax.dynamic_update_slice(
            whole, flip(part, CORE_BIT), (0, 1 - place["core"], chip, 0, 0, 0)
        )
    return whole.reshape(stack_count, 2, 8 * own_rows, 4, width // 2)


def sum_everywhere(values_in):
    for mask in (CORE_BIT, LINE_BIT, HALF_BIT, X_BIT, Y_BIT):
        values_in = values_in + flip(values_in, mask)
    return values_in


def dot32(spec, left_mat, right_mat):
    return jnp.einsum(spec, left_mat, right_mat, preferred_element_type=jnp.float32)


def shampoo_part(
    whole, weights_in, left_in, right_in, left_root, right_low, place, tensor_index, dp_index
):
    stack_count, _, rows, blocks, width = whole.shape
    own_rows = weights_in.shape[1]
    left_low = left_root.astype(jnp.bfloat16)
    flat = whole.reshape(stack_count, 2, rows, blocks * width)
    turned = dot32("srq,scqk->scrk", left_low, flat).astype(jnp.bfloat16)
    update = dot32("scrk,sckj->srj", turned, right_low)
    dp_rows = lax.dynamic_slice_in_dim(flat, dp_index * own_rows, own_rows, 2)
    line_rows = lax.dynamic_slice_in_dim(flat, tensor_index * 2 * own_rows, 2 * own_rows, 2)
    left_sum = dot32("scrk,scqk->srq", dp_rows, line_rows)
    tensor_cols = pick(whole, tensor_index, 3)
    dp_cols = pick(pick(whole, place["chip"], 3), place["core"], 1)
    right_sum = dot32("scrk,srj->sckj", tensor_cols, dp_cols).reshape(right_in.shape)
    grad = lax.dynamic_slice_in_dim(tensor_cols, dp_index * own_rows, own_rows, 2)
    grad = jnp.swapaxes(grad, 1, 2).reshape(weights_in.shape).astype(jnp.float32)
    return (
        grad,
        0.5 * left_in + 0.5 * left_sum,
        0.5 * right_in + 0.5 * right_sum,
        weights_in - shampoo_rate * (update + shampoo_decay * weights_in),
    )


def right_root_low(right_root, blocks):
    stack_count, rows, width = right_root.shape
    low = right_root.astype(jnp.bfloat16).reshape(stack_count, blocks, 2, rows // (2 * blocks), width)
    return jnp.swapaxes(low, 1, 2).reshape(stack_count, 2, rows // 2, width)


def masked_heads(values_in, lanes, head, scale):
    keep = (lanes >= head * HEAD_DIM) & (lanes < (head + 1) * HEAD_DIM)
    return jnp.where(keep, values_in * scale, jnp.zeros_like(values_in))


def forward_kernel(info_ref, qkv_ref, out_ref):
    pieces = 4
    rows = qkv_ref.shape[1] // pieces
    me = info_ref[0]
    starts = [pl.multiple_of((me ^ piece) * rows, rows) for piece in range(pieces)]
    lanes = lax.broadcasted_iota(jnp.int32, (rows, 128), 1)
    row_of = lax.broadcasted_iota(jnp.int32, (rows, rows), 0)
    col_of = lax.broadcasted_iota(jnp.int32, (rows, rows), 1)
    row_line = lax.broadcasted_iota(jnp.int32, (rows, 1), 0)
    for query in range(pieces):
        query_rows = qkv_ref[0, pl.ds(starts[query], rows), :]
        place = row_line + query * rows
        begin = info_ref[1] * jnp.ones_like(place)
        for block in range(1, qkv_ref.shape[1] // SHORT):
            begin = jnp.where(place >= block * SHORT, info_ref[1 + block], begin)
        outs = []
        for head in range(2):
            query_head = masked_heads(query_rows, lanes, head, HEAD_DIM**-0.5)
            scores = []
            for key in range(query + 1):
                key_rows = qkv_ref[1, pl.ds(starts[key], rows), :]
                score = lax.dot_general(
                    query_head, key_rows, (((1,), (1,)), ((), ())), preferred_element_type=jnp.float32
                )
                allowed = col_of + key * rows >= begin
                if key == query:
                    allowed = allowed & (col_of <= row_of)
                scores.append(jnp.where(allowed, score, -1e30))
            top = scores[0].max(axis=1, keepdims=True)
            for score in scores[1:]:
                top = jnp.maximum(top, score.max(axis=1, keepdims=True))
            mass = jnp.zeros_like(top)
            total = jnp.zeros((rows, 128), jnp.float32)
            for key in range(query + 1):
                value_rows = qkv_ref[2, pl.ds(starts[key], rows), :]
                chance = jnp.exp(scores[key] - top)
                mass = mass + chance.sum(axis=1, keepdims=True)
                total = total + jnp.dot(
                    chance.astype(jnp.bfloat16), value_rows, preferred_element_type=jnp.float32
                )
            outs.append(total / mass)
        out = jnp.where(lanes < HEAD_DIM, outs[0], outs[1])
        out_ref[pl.ds(starts[query], rows), :] = out.astype(jnp.bfloat16)


def backward_kernel(info_ref, qkv_ref, grad_ref, out_ref, key_acc, value_acc, key_turned):
    pieces = 4
    rows = qkv_ref.shape[1] // pieces
    me = info_ref[0]
    starts = [pl.multiple_of((me ^ piece) * rows, rows) for piece in range(pieces)]
    lanes = lax.broadcasted_iota(jnp.int32, (rows, 128), 1)
    key_of = lax.broadcasted_iota(jnp.int32, (rows, rows), 0)
    row_of = lax.broadcasted_iota(jnp.int32, (rows, rows), 1)
    row_line = lax.broadcasted_iota(jnp.int32, (1, rows), 1)
    key_acc[...] = jnp.zeros_like(key_acc)
    value_acc[...] = jnp.zeros_like(value_acc)
    for key in range(pieces):
        key_rows = qkv_ref[1, pl.ds(starts[key], rows), :]
        key_turned[key] = key_rows.astype(jnp.float32).T.astype(jnp.bfloat16)
    for query in range(pieces):
        query_rows = qkv_ref[0, pl.ds(starts[query], rows), :]
        grad_rows = grad_ref[pl.ds(starts[query], rows), :]
        place = row_line + query * rows
        begin = info_ref[1] * jnp.ones_like(place)
        for block in range(1, qkv_ref.shape[1] // SHORT):
            begin = jnp.where(place >= block * SHORT, info_ref[1 + block], begin)
        query_grad = jnp.zeros((128, rows), jnp.float32)
        for head in range(2):
            query_head = masked_heads(query_rows, lanes, head, HEAD_DIM**-0.5)
            grad_head = masked_heads(grad_rows, lanes, head, 1.0)
            scores, slopes = [], []
            for key in range(query + 1):
                key_rows = qkv_ref[1, pl.ds(starts[key], rows), :]
                score = lax.dot_general(
                    key_rows, query_head, (((1,), (1,)), ((), ())), preferred_element_type=jnp.float32
                )
                allowed = key_of + key * rows >= begin
                if key == query:
                    allowed = allowed & (key_of <= row_of)
                scores.append(jnp.where(allowed, score, -1e30))
            top = scores[0].max(axis=0, keepdims=True)
            for score in scores[1:]:
                top = jnp.maximum(top, score.max(axis=0, keepdims=True))
            mass = jnp.zeros_like(top)
            inner = jnp.zeros_like(top)
            chances = []
            for key in range(query + 1):
                value_rows = qkv_ref[2, pl.ds(starts[key], rows), :]
                slope = lax.dot_general(
                    value_rows, grad_head, (((1,), (1,)), ((), ())), preferred_element_type=jnp.float32
                )
                chance = jnp.exp(scores[key] - top)
                mass = mass + chance.sum(axis=0, keepdims=True)
                inner = inner + (chance * slope).sum(axis=0, keepdims=True)
                chances.append(chance)
                slopes.append(slope)
            share = 1.0 / mass
            inner = inner * share
            half = slice(head * HEAD_DIM, (head + 1) * HEAD_DIM)
            parts = []
            for key in range(query + 1):
                probs = chances[key] * share
                grad_scores = (probs * (slopes[key] - inner)).astype(jnp.bfloat16)
                value_acc[key] += jnp.dot(
                    probs.astype(jnp.bfloat16), grad_head, preferred_element_type=jnp.float32
                )
                key_acc[key] += jnp.dot(
                    grad_scores, query_head, preferred_element_type=jnp.float32
                )
                parts.append(
                    jnp.dot(
                        key_turned[key, half, :], grad_scores, preferred_element_type=jnp.float32
                    )
                )
            total = parts[0]
            for part in parts[1:]:
                total = total + part
            if head == 0:
                query_grad = total
            else:
                query_grad = jnp.concatenate([query_grad, total], axis=0)
        out_ref[0, pl.ds(starts[query], rows), :] = (
            query_grad.T * (HEAD_DIM**-0.5)
        ).astype(jnp.bfloat16)
    for key in range(pieces):
        out_ref[1, pl.ds(starts[key], rows), :] = key_acc[key].astype(jnp.bfloat16)
        out_ref[2, pl.ds(starts[key], rows), :] = value_acc[key].astype(jnp.bfloat16)


def attend(info, qkv):
    _, rows, width = qkv.shape
    return pl.pallas_call(
        forward_kernel,
        grid_spec=pltpu.PrefetchScalarGridSpec(
            num_scalar_prefetch=1,
            grid=(width // 128,),
            in_specs=[pl.BlockSpec((3, rows, 128), lambda pair, info_ref: (0, 0, pair))],
            out_specs=pl.BlockSpec((rows, 128), lambda pair, info_ref: (0, pair)),
        ),
        out_shape=jax.ShapeDtypeStruct((rows, width), jnp.bfloat16),
        compiler_params=pltpu.CompilerParams(vmem_limit_bytes=48 * 1024 * 1024),
        cost_estimate=pl.CostEstimate(
            flops=rows * rows * width * 2, bytes_accessed=8 * rows * width, transcendentals=0
        ),
    )(info, qkv)


def attend_back(info, qkv, grad_heads):
    _, rows, width = qkv.shape
    return pl.pallas_call(
        backward_kernel,
        grid_spec=pltpu.PrefetchScalarGridSpec(
            num_scalar_prefetch=1,
            grid=(width // 128,),
            in_specs=[
                pl.BlockSpec((3, rows, 128), lambda pair, info_ref: (0, 0, pair)),
                pl.BlockSpec((rows, 128), lambda pair, info_ref: (0, pair)),
            ],
            out_specs=pl.BlockSpec((3, rows, 128), lambda pair, info_ref: (0, 0, pair)),
            scratch_shapes=[
                pltpu.VMEM((4, rows // 4, 128), jnp.float32),
                pltpu.VMEM((4, rows // 4, 128), jnp.float32),
                pltpu.VMEM((4, 128, rows // 4), jnp.bfloat16),
            ],
        ),
        out_shape=jax.ShapeDtypeStruct(qkv.shape, jnp.bfloat16),
        compiler_params=pltpu.CompilerParams(vmem_limit_bytes=48 * 1024 * 1024),
        cost_estimate=pl.CostEstimate(
            flops=rows * rows * width * 5, bytes_accessed=14 * rows * width, transcendentals=0
        ),
    )(info, qkv, grad_heads)


def regrouped(
    tokens_in,
    lm_grad,
    lm_logprob,
    targets,
    neighbor_ids,
    nearby_entry_gaps,
    seq_lengths,
    attn_weights,
    ffn_weights,
    attn_left,
    attn_right,
    ffn_left,
    ffn_right,
    attn_left_root,
    attn_right_root,
    ffn_left_root,
    ffn_right_root,
    norm_params,
    norm_moment1,
    norm_moment2,
    blending_coefficients,
    knn_moment1,
    knn_moment2,
):
    low = jnp.bfloat16
    rows = tokens_in.shape[0]
    group_rows = 4 * rows
    dp_index, tensor_index = lax.axis_index("dp"), lax.axis_index("tensor")
    place = {
        "line": tensor_index & 1,
        "half": tensor_index >> 1,
        "core": dp_index & 1,
        "x": (dp_index >> 1) & 1,
        "y": dp_index >> 2,
        "chip": dp_index >> 1,
    }
    me = place["core"] * 2 + place["line"]

    moved = swap_core_half(tokens_in)
    wa, wf = attn_weights.astype(low), ffn_weights.astype(low)
    w_first = gather_weight(wa[:2], place, X_BIT, Y_BIT)
    w_second = gather_weight(wa[2:], place, Y_BIT, X_BIT)
    w_up = gather_weight(wf[:1], place, X_BIT, Y_BIT)[0]
    w_down = gather_weight(wf[1:], place, Y_BIT, X_BIT)[0]
    proj_in = jnp.concatenate([w_first, w_second[:1]], axis=0)
    proj_out = w_second[1]

    lengths = swap_core_half(seq_lengths.astype(jnp.float32)).astype(jnp.int32)
    block_begins = first_blocks(lengths, group_rows, SHORT) * SHORT
    info = jnp.concatenate([me[None].astype(jnp.int32), block_begins.astype(jnp.int32)])

    resid = moved.astype(jnp.float32)
    normed1, norm1_back = jax.vjp(layer_norm, resid, norm_params[0], norm_params[1])
    normed1_all = gather_group(normed1.astype(low))
    qkv = dot32("rd,sdc->src", normed1_all, proj_in).astype(low)
    heads_flat = attend(info, qkv)
    attn_out = reduce_group(
        lambda a, b: dot32("rc,dc->rd", heads_flat[a:b], proj_out), rows
    )
    middle = resid + attn_out
    normed2, norm2_back = jax.vjp(layer_norm, middle, norm_params[2], norm_params[3])
    normed2_all = gather_group(normed2.astype(low))

    sharpness_divisor = jnp.exp(blending_coefficients[0])
    interp = jax.nn.sigmoid(blending_coefficients[1])
    nearby_entry_logits = -nearby_entry_gaps / sharpness_divisor
    near_top = jnp.max(nearby_entry_logits, axis=1, keepdims=True)
    near_exp = jnp.exp(nearby_entry_logits - near_top)
    nearby_entry_shares = near_exp / jnp.sum(near_exp, axis=1, keepdims=True)
    target_matches = (neighbor_ids == targets[:, None]).astype(jnp.float32)
    retrieval_probability = jnp.sum(nearby_entry_shares * target_matches, axis=1)
    lm_prob = jnp.exp(lm_logprob)
    mixture = interp * retrieval_probability + (1.0 - interp) * lm_prob
    token_loss = -jnp.log(mixture)
    lm_weight = -(1.0 - interp) * lm_prob / mixture
    temp_terms = (
        jnp.sum(
            nearby_entry_shares
            * (target_matches - retrieval_probability[:, None])
            * nearby_entry_gaps,
            axis=1,
        )
        / sharpness_divisor
    )
    temp_grad = jnp.sum(-(interp / mixture) * temp_terms)
    interp_grad = jnp.sum(-interp * (1.0 - interp) * (retrieval_probability - lm_prob) / mixture)
    cotangent = swap_core_half(lm_weight)[:, None] * swap_core_half(lm_grad).astype(jnp.float32)
    cot_all = gather_group(cotangent.astype(low))

    hidden_pre = dot32("rd,df->rf", normed2_all, w_up)
    hidden_act, gelu_back = jax.vjp(gelu_tanh, hidden_pre)
    act_low = hidden_act.astype(low)
    grad_act = dot32("rd,df->rf", cot_all, w_down)
    grad_pre_low = gelu_back(grad_act)[0].astype(low)
    grad_normed2 = reduce_group(
        lambda a, b: dot32("rf,df->rd", grad_pre_low[a:b], w_up), rows
    )
    grad_up = dot32("rd,rf->df", normed2_all, grad_pre_low)
    grad_down = dot32("rd,rf->df", cot_all, act_low)
    mid_norm_grad, gain2_grad, shift2_grad = norm2_back(grad_normed2)
    grad_middle = cotangent + mid_norm_grad
    grad_mid_all = gather_group(grad_middle.astype(low))
    grad_heads = dot32("rd,dc->rc", grad_mid_all, proj_out).astype(low)
    grad_qkv = attend_back(info, qkv, grad_heads)
    grad_out_proj = dot32("rd,rc->dc", grad_mid_all, heads_flat)
    grad_proj_in = dot32("rd,src->sdc", normed1_all, grad_qkv)
    grad_normed1 = reduce_group(
        lambda a, b: dot32("src,sdc->rd", grad_qkv[:, a:b], proj_in), rows
    )
    ffn_out = reduce_group(lambda a, b: dot32("rf,df->rd", act_low[a:b], w_down), rows)
    mixed = swap_core_half((middle + ffn_out).astype(low))

    up_own = scatter_grad(grad_up[None], place, X_BIT)
    down_own = scatter_grad(grad_down[None], place, Y_BIT)
    first_own = scatter_grad(grad_proj_in[:2], place, X_BIT)
    second_own = scatter_grad(
        jnp.concatenate([grad_proj_in[2:], grad_out_proj[None]], axis=0), place, Y_BIT
    )
    up_whole = gather_grad(up_own, place, X_BIT)
    down_whole = gather_grad(down_own, place, Y_BIT)
    first_whole = gather_grad(first_own, place, X_BIT)
    second_whole = gather_grad(second_own, place, Y_BIT)

    res_norm_grad, gain1_grad, shift1_grad = norm1_back(grad_normed1)
    input_grad = swap_core_half((grad_middle + res_norm_grad).astype(low)).astype(jnp.float32)

    width = norm_params.shape[1]
    scalars = jnp.zeros((1, width), jnp.float32)
    scalars = scalars.at[0, 0].set(temp_grad).at[0, 1].set(interp_grad)
    scalars = scalars.at[0, 2].set(jnp.sum(token_loss))
    early = sum_everywhere(
        jnp.concatenate([gain2_grad[None], shift2_grad[None], scalars], axis=0)
    )
    late = sum_everywhere(jnp.stack([gain1_grad, shift1_grad]))
    norm_total = jnp.concatenate([late, early[:2]], axis=0)
    knn_total = early[2, :2]
    loss = early[2, 2] / (group_rows * 8)

    blocks = 4
    attn_right_low = right_root_low(attn_right_root, blocks)
    ffn_right_low = right_root_low(ffn_right_root, blocks)
    ffn_parts = [
        shampoo_part(
            whole,
            ffn_weights[at : at + 1],
            ffn_left[at : at + 1],
            ffn_right[at : at + 1],
            ffn_left_root[at : at + 1],
            ffn_right_low[at : at + 1],
            place,
            tensor_index,
            dp_index,
        )
        for at, whole in enumerate((up_whole, down_whole))
    ]
    attn_parts = [
        shampoo_part(
            whole,
            attn_weights[at : at + 2],
            attn_left[at : at + 2],
            attn_right[at : at + 2],
            attn_left_root[at : at + 2],
            attn_right_low[at : at + 2],
            place,
            tensor_index,
            dp_index,
        )
        for at, whole in ((0, first_whole), (2, second_whole))
    ]
    ffn_grad, ffn_left_new, ffn_right_new, ffn_new = (
        jnp.concatenate(parts, axis=0) for parts in zip(*ffn_parts)
    )
    attn_grad, attn_left_new, attn_right_new, attn_new = (
        jnp.concatenate(parts, axis=0) for parts in zip(*attn_parts)
    )
    norm_m1, norm_m2, norm_new = adamw_step(norm_params, norm_total, norm_moment1, norm_moment2)
    knn_m1, knn_m2, knn_new = adamw_step(blending_coefficients, knn_total, knn_moment1, knn_moment2)
    return (
        mixed,
        input_grad,
        loss,
        attn_grad,
        attn_left_new,
        attn_right_new,
        attn_new,
        ffn_grad,
        ffn_left_new,
        ffn_right_new,
        ffn_new,
        norm_m1,
        norm_m2,
        norm_new,
        knn_m1,
        knn_m2,
        knn_new,
    )


def solution(mesh):
    sized = (mesh.shape["dp"], mesh.shape["tensor"]) == (8, 4)
    placed = (
        P(("dp", "tensor"), None),
        P(("dp", "tensor"), None),
        P(("dp", "tensor")),
        P(("dp", "tensor")),
        P(("dp", "tensor"), None),
        P(("dp", "tensor"), None),
        P("dp", None),
        P(None, "dp", "tensor"),
        P(None, "dp", "tensor"),
        P(None, "dp", "tensor"),
        P(None, "tensor", "dp"),
        P(None, "dp", "tensor"),
        P(None, "tensor", "dp"),
        P(None, "dp", None),
        P(None, None, "tensor"),
        P(None, "dp", None),
        P(None, None, "tensor"),
        P(),
        P(),
        P(),
        P(),
        P(),
        P(),
    )
    return jax.shard_map(
        regrouped if sized else local,
        mesh=mesh,
        in_specs=placed,
        out_specs=(
            P(("dp", "tensor"), None),
            P(("dp", "tensor"), None),
            P(),
            P(None, "dp", "tensor"),
            P(None, "dp", "tensor"),
            P(None, "tensor", "dp"),
            P(None, "dp", "tensor"),
            P(None, "dp", "tensor"),
            P(None, "dp", "tensor"),
            P(None, "tensor", "dp"),
            P(None, "dp", "tensor"),
            P(),
            P(),
            P(),
            P(),
            P(),
            P(),
        ),
        check_vma=False,
    )
```

```python
import jax
import jax.numpy as jnp
from jax import lax
from jax.experimental import pallas as pl
from jax.experimental.pallas import tpu as pltpu
from jax.sharding import PartitionSpec as P

SHORT = 512
STEP = 10
HEAD_DIM = 64


adam_rate = 0.3
shampoo_rate = 0.5
shampoo_decay = 0.01
norm_eps = 1e-05


def layer_norm(values_in, gain, shift):
    centre = jnp.mean(values_in, axis=-1, keepdims=True)
    centred = values_in - centre
    spread_sq = jnp.mean(centred * centred, axis=-1, keepdims=True)
    return centred * lax.rsqrt(spread_sq + norm_eps) * gain + shift


def gelu_tanh(values_in):
    return jax.nn.gelu(values_in, approximate=True)


def spread_rows(local_low):
    return lax.all_gather(local_low, "tensor", axis=0, tiled=True)


def spread_again(local_low):
    return lax.all_gather(local_low, "tensor", axis=0, tiled=True)


def spread_grads(local_low):
    return lax.all_gather(local_low, "tensor", axis=0, tiled=True)


def branch_total(left_rows, right_mat):
    return lax.psum_scatter(
        jnp.einsum("rc,dc->rd", left_rows, right_mat, preferred_element_type=jnp.float32),
        "tensor",
        scatter_dimension=0,
        tiled=True,
    )


def input_total(left_rows, right_mat):
    return lax.psum_scatter(
        jnp.einsum("rc,dc->rd", left_rows, right_mat, preferred_element_type=jnp.float32),
        "tensor",
        scatter_dimension=0,
        tiled=True,
    )


def first_blocks(seq_lengths, group_rows, block_rows):
    lengths = seq_lengths[0]
    seq_ends = jnp.cumsum(lengths)
    seq_begins = seq_ends - lengths
    block_begins = jnp.arange(group_rows // block_rows, dtype=jnp.int32) * block_rows
    inside = (seq_begins[None, :] <= block_begins[:, None]) & (lengths[None, :] > 0)
    return jnp.max(jnp.where(inside, seq_begins[None, :], 0), axis=1) // block_rows


def block_scores(query_rows, key_rows, query_block, key_block, block_rows, score_scale):
    scores = (
        jnp.einsum("qhd,khd->hqk", query_rows, key_rows, preferred_element_type=jnp.float32)
        * score_scale
    )
    query_pos = query_block * block_rows + jnp.arange(block_rows, dtype=jnp.int32)
    key_pos = key_block * block_rows + jnp.arange(block_rows, dtype=jnp.int32)
    allowed = key_pos[None, :] <= query_pos[:, None]
    return jnp.where(allowed[None], scores, -1e30)


def attend_forward(query_all, key_all, value_all, first_block, block_rows, score_scale):
    group_rows, head_count, head_width = query_all.shape

    def one_block(query_block):
        query_rows = lax.dynamic_slice_in_dim(query_all, query_block * block_rows, block_rows, 0)

        def peak_step(key_block, loop_state):
            running_top, running_mass = loop_state
            key_rows = lax.dynamic_slice_in_dim(key_all, key_block * block_rows, block_rows, 0)
            scores = block_scores(
                query_rows, key_rows, query_block, key_block, block_rows, score_scale
            )
            new_top = jnp.maximum(running_top, jnp.max(scores, axis=2))
            new_mass = running_mass * jnp.exp(running_top - new_top) + jnp.sum(
                jnp.exp(scores - new_top[:, :, None]), axis=2
            )
            return (new_top, new_mass)

        start_state = (
            jnp.full((head_count, block_rows), -1e30, jnp.float32),
            jnp.zeros((head_count, block_rows), jnp.float32),
        )
        final_top, final_mass = lax.fori_loop(
            first_block[query_block], query_block + 1, peak_step, start_state
        )
        log_mass = final_top + jnp.log(final_mass)

        def value_step(key_block, out_acc):
            key_rows = lax.dynamic_slice_in_dim(key_all, key_block * block_rows, block_rows, 0)
            value_rows = lax.dynamic_slice_in_dim(value_all, key_block * block_rows, block_rows, 0)
            scores = block_scores(
                query_rows, key_rows, query_block, key_block, block_rows, score_scale
            )
            attn_probs = jnp.exp(scores - log_mass[:, :, None]).astype(jnp.bfloat16)
            return out_acc + jnp.einsum(
                "hqk,khd->qhd", attn_probs, value_rows, preferred_element_type=jnp.float32
            )

        out_rows = lax.fori_loop(
            first_block[query_block],
            query_block + 1,
            value_step,
            jnp.zeros((block_rows, head_count, head_width), jnp.float32),
        )
        return (out_rows.astype(jnp.bfloat16), log_mass)

    outs, log_masses = lax.map(one_block, jnp.arange(group_rows // block_rows, dtype=jnp.int32))
    return (outs.reshape(group_rows, head_count, head_width), log_masses)


def attend_backward(
    query_all, key_all, value_all, grad_out, log_masses, first_block, block_rows, score_scale
):
    group_rows, head_count, head_width = query_all.shape

    def one_block(query_block, loop_carry):
        grad_keys, grad_values, grad_query = loop_carry
        query_rows = lax.dynamic_slice_in_dim(query_all, query_block * block_rows, block_rows, 0)
        grad_rows = lax.dynamic_slice_in_dim(grad_out, query_block * block_rows, block_rows, 0)
        log_mass = log_masses[query_block]

        def chances(key_block):
            key_rows = lax.dynamic_slice_in_dim(key_all, key_block * block_rows, block_rows, 0)
            value_rows = lax.dynamic_slice_in_dim(value_all, key_block * block_rows, block_rows, 0)
            scores = block_scores(
                query_rows, key_rows, query_block, key_block, block_rows, score_scale
            )
            attn_probs = jnp.exp(scores - log_mass[:, :, None])
            likelihood_cotangent = jnp.einsum(
                "qhd,khd->hqk", grad_rows, value_rows, preferred_element_type=jnp.float32
            )
            return (key_rows, attn_probs, likelihood_cotangent)

        def inner_step(key_block, inner_acc):
            _, attn_probs, likelihood_cotangent = chances(key_block)
            return inner_acc + jnp.sum(attn_probs * likelihood_cotangent, axis=2)

        row_inner = lax.fori_loop(
            first_block[query_block],
            query_block + 1,
            inner_step,
            jnp.zeros((head_count, block_rows), jnp.float32),
        )

        def grad_step(key_block, loop_state):
            query_acc, keys_acc, values_acc = loop_state
            key_rows, attn_probs, likelihood_cotangent = chances(key_block)
            grad_scores = (attn_probs * (likelihood_cotangent - row_inner[:, :, None])).astype(
                jnp.bfloat16
            )
            query_acc = (
                query_acc
                + jnp.einsum(
                    "hqk,khd->qhd", grad_scores, key_rows, preferred_element_type=jnp.float32
                )
                * score_scale
            )
            key_part = (
                jnp.einsum(
                    "hqk,qhd->khd", grad_scores, query_rows, preferred_element_type=jnp.float32
                )
                * score_scale
            )
            value_part = jnp.einsum(
                "hqk,qhd->khd",
                attn_probs.astype(jnp.bfloat16),
                grad_rows,
                preferred_element_type=jnp.float32,
            )
            key_start = key_block * block_rows
            keys_acc = lax.dynamic_update_slice_in_dim(
                keys_acc,
                lax.dynamic_slice_in_dim(keys_acc, key_start, block_rows, 0) + key_part,
                key_start,
                0,
            )
            values_acc = lax.dynamic_update_slice_in_dim(
                values_acc,
                lax.dynamic_slice_in_dim(values_acc, key_start, block_rows, 0) + value_part,
                key_start,
                0,
            )
            return (query_acc, keys_acc, values_acc)

        query_acc, grad_keys, grad_values = lax.fori_loop(
            first_block[query_block],
            query_block + 1,
            grad_step,
            (jnp.zeros((block_rows, head_count, head_width), jnp.float32), grad_keys, grad_values),
        )
        grad_query = lax.dynamic_update_slice_in_dim(
            grad_query, query_acc, query_block * block_rows, 0
        )
        return (grad_keys, grad_values, grad_query)

    zeros_all = jnp.zeros((group_rows, head_count, head_width), jnp.float32)
    return lax.fori_loop(0, group_rows // block_rows, one_block, (zeros_all, zeros_all, zeros_all))


def right_statistics(attn_part_grad, ffn_part_grad, attn_rows, ffn_rows):
    attn_part = jnp.einsum(
        "sri,srj->sij", attn_part_grad, attn_rows, precision=lax.Precision.HIGHEST
    )
    ffn_part = jnp.einsum("sri,srj->sij", ffn_part_grad, ffn_rows, precision=lax.Precision.HIGHEST)
    return (
        lax.psum_scatter(
            attn_part.astype(jnp.bfloat16), "dp", scatter_dimension=2, tiled=True
        ).astype(jnp.float32),
        lax.psum_scatter(
            ffn_part.astype(jnp.bfloat16), "dp", scatter_dimension=2, tiled=True
        ).astype(jnp.float32),
    )


def left_statistics(attn_part_grad, ffn_part_grad, attn_cols, ffn_cols):
    attn_part = jnp.einsum(
        "sri,sqi->srq", attn_part_grad, attn_cols, precision=lax.Precision.HIGHEST
    )
    ffn_part = jnp.einsum("sri,sqi->srq", ffn_part_grad, ffn_cols, precision=lax.Precision.HIGHEST)
    return (
        lax.psum_scatter(
            attn_part.astype(jnp.bfloat16), "tensor", scatter_dimension=2, tiled=True
        ).astype(jnp.float32),
        lax.psum_scatter(
            ffn_part.astype(jnp.bfloat16), "tensor", scatter_dimension=2, tiled=True
        ).astype(jnp.float32),
    )


def adamw_step(params_in, grads_in, first_in, second_in):
    first_new = 0.9 * first_in + 0.1 * grads_in
    second_new = 0.999 * second_in + 0.001 * grads_in * grads_in
    first_hat = first_new / (1.0 - 0.9**STEP)
    second_hat = second_new / (1.0 - 0.999**STEP)
    return (
        first_new,
        second_new,
        params_in - adam_rate * first_hat / (jnp.sqrt(second_hat) + 1e-08),
    )


def local(
    tokens_in,
    lm_grad,
    lm_logprob,
    targets,
    neighbor_ids,
    nearby_entry_gaps,
    seq_lengths,
    attn_weights,
    ffn_weights,
    attn_left,
    attn_right,
    ffn_left,
    ffn_right,
    attn_left_root,
    attn_right_root,
    ffn_left_root,
    ffn_right_root,
    norm_params,
    norm_moment1,
    norm_moment2,
    blending_coefficients,
    knn_moment1,
    knn_moment2,
):
    local_rows = tokens_in.shape[0]
    group_rows = local_rows * lax.axis_size("tensor")
    block_rows = SHORT
    score_scale = HEAD_DIM ** (-0.5)
    attn_full, ffn_full = (
        lax.all_gather(attn_weights.astype(jnp.bfloat16), "dp", axis=1, tiled=True),
        lax.all_gather(ffn_weights.astype(jnp.bfloat16), "dp", axis=1, tiled=True),
    )
    proj_in = jnp.concatenate([attn_full[0], attn_full[1], attn_full[2]], axis=1)
    proj_out = attn_full[3]
    head_cols = proj_out.shape[1]
    head_count = head_cols // HEAD_DIM
    first_block = first_blocks(seq_lengths, group_rows, block_rows)
    resid = tokens_in.astype(jnp.float32)
    normed1, norm1_back = jax.vjp(layer_norm, resid, norm_params[0], norm_params[1])
    normed1_low = normed1.astype(jnp.bfloat16)
    normed1_all = spread_rows(normed1_low)
    qkv_low = jnp.dot(normed1_all, proj_in, preferred_element_type=jnp.float32).astype(jnp.bfloat16)
    query_all = qkv_low[:, :head_cols].reshape(group_rows, head_count, HEAD_DIM)
    key_all = qkv_low[:, head_cols : 2 * head_cols].reshape(group_rows, head_count, HEAD_DIM)
    value_all = qkv_low[:, 2 * head_cols :].reshape(group_rows, head_count, HEAD_DIM)
    heads_out, log_masses = attend_forward(
        query_all, key_all, value_all, first_block, block_rows, score_scale
    )
    heads_flat = heads_out.reshape(group_rows, head_cols)
    attn_out = branch_total(heads_flat, proj_out)
    middle = resid + attn_out
    normed2, norm2_back = jax.vjp(layer_norm, middle, norm_params[2], norm_params[3])
    normed2_low = normed2.astype(jnp.bfloat16)
    w_up = ffn_full[0]
    w_down = ffn_full[1]
    normed2_all = spread_rows(normed2_low)
    hidden_pre = jnp.dot(normed2_all, w_up, preferred_element_type=jnp.float32)
    hidden_act, gelu_back = jax.vjp(gelu_tanh, hidden_pre)
    act_low = hidden_act.astype(jnp.bfloat16)
    ffn_out = branch_total(act_low, w_down)
    mixed = (middle + ffn_out).astype(jnp.bfloat16)
    sharpness_divisor = jnp.exp(blending_coefficients[0])
    interp = jax.nn.sigmoid(blending_coefficients[1])
    nearby_entry_logits = -nearby_entry_gaps / sharpness_divisor
    near_top = jnp.max(nearby_entry_logits, axis=1, keepdims=True)
    near_exp = jnp.exp(nearby_entry_logits - near_top)
    nearby_entry_shares = near_exp / jnp.sum(near_exp, axis=1, keepdims=True)
    target_matches = (neighbor_ids == targets[:, None]).astype(jnp.float32)
    retrieval_probability = jnp.sum(nearby_entry_shares * target_matches, axis=1)
    lm_prob = jnp.exp(lm_logprob)
    mixture = interp * retrieval_probability + (1.0 - interp) * lm_prob
    token_loss = -jnp.log(mixture)
    lm_weight = -(1.0 - interp) * lm_prob / mixture
    temp_terms = (
        jnp.sum(
            nearby_entry_shares
            * (target_matches - retrieval_probability[:, None])
            * nearby_entry_gaps,
            axis=1,
        )
        / sharpness_divisor
    )
    temp_grad = jnp.sum(-(interp / mixture) * temp_terms)
    interp_grad = jnp.sum(-interp * (1.0 - interp) * (retrieval_probability - lm_prob) / mixture)
    knn_grads = jnp.stack([temp_grad, interp_grad])
    cotangent = lm_weight[:, None] * lm_grad.astype(jnp.float32)
    cot_all = spread_grads(cotangent.astype(jnp.bfloat16))
    grad_act = jnp.dot(cot_all, w_down, preferred_element_type=jnp.float32)
    grad_pre_low = gelu_back(grad_act)[0].astype(jnp.bfloat16)
    normed2_used = spread_again(normed2_low)
    grad_up = jnp.einsum(
        "rd,rf->df", normed2_used, grad_pre_low, preferred_element_type=jnp.float32
    )
    grad_down = jnp.einsum("rd,rf->df", cot_all, act_low, preferred_element_type=jnp.float32)
    ffn_local = jnp.stack([grad_up, grad_down])
    grad_normed2 = input_total(grad_pre_low, w_up)
    mid_norm_grad, gain2_grad, shift2_grad = norm2_back(grad_normed2)
    grad_middle = cotangent + mid_norm_grad
    grad_mid_all = spread_grads(grad_middle.astype(jnp.bfloat16))
    grad_heads = jnp.dot(grad_mid_all, proj_out, preferred_element_type=jnp.float32).astype(
        jnp.bfloat16
    )
    grad_out_proj = jnp.einsum(
        "rd,rc->dc", grad_mid_all, heads_flat, preferred_element_type=jnp.float32
    )
    grad_keys, grad_values, grad_query = attend_backward(
        query_all,
        key_all,
        value_all,
        grad_heads.reshape(group_rows, head_count, HEAD_DIM),
        log_masses,
        first_block,
        block_rows,
        score_scale,
    )
    grad_qkv = jnp.concatenate(
        [
            grad_query.reshape(group_rows, head_cols),
            grad_keys.reshape(group_rows, head_cols),
            grad_values.reshape(group_rows, head_cols),
        ],
        axis=1,
    ).astype(jnp.bfloat16)
    normed1_used = spread_again(normed1_low)
    grad_proj_in = jnp.einsum(
        "rd,rc->dc", normed1_used, grad_qkv, preferred_element_type=jnp.float32
    )
    grad_normed1 = input_total(grad_qkv, proj_in)
    res_norm_grad, gain1_grad, bias_first_cotangent = norm1_back(grad_normed1)
    input_grad = grad_middle + res_norm_grad
    norm_grads = jnp.stack([gain1_grad, bias_first_cotangent, gain2_grad, shift2_grad])
    norm_total, knn_total, loss_total = lax.psum(
        (norm_grads, knn_grads, jnp.sum(token_loss)), ("dp", "tensor")
    )
    token_count = group_rows * lax.axis_size("dp")
    attn_local = jnp.stack(
        [
            grad_proj_in[:, :head_cols],
            grad_proj_in[:, head_cols : 2 * head_cols],
            grad_proj_in[:, 2 * head_cols :],
            grad_out_proj,
        ]
    )
    attn_grad, ffn_grad = (
        lax.psum_scatter(attn_local, "dp", scatter_dimension=1, tiled=True),
        lax.psum_scatter(ffn_local, "dp", scatter_dimension=1, tiled=True),
    )
    attn_rows, ffn_rows = (
        lax.all_gather(attn_grad.astype(jnp.bfloat16), "tensor", axis=2, tiled=True).astype(
            attn_grad.dtype
        ),
        lax.all_gather(ffn_grad.astype(jnp.bfloat16), "tensor", axis=2, tiled=True).astype(
            ffn_grad.dtype
        ),
    )
    attn_right_sum, ffn_right_sum = right_statistics(attn_grad, ffn_grad, attn_rows, ffn_rows)
    attn_turned = jnp.einsum(
        "sri,sij->srj", attn_rows, attn_right_root, precision=lax.Precision.HIGHEST
    )
    ffn_turned = jnp.einsum(
        "sri,sij->srj", ffn_rows, ffn_right_root, precision=lax.Precision.HIGHEST
    )
    attn_cols, ffn_cols, attn_turned_cols, ffn_turned_cols = (
        lax.all_gather(attn_grad.astype(jnp.bfloat16), "dp", axis=1, tiled=True).astype(
            attn_grad.dtype
        ),
        lax.all_gather(ffn_grad.astype(jnp.bfloat16), "dp", axis=1, tiled=True).astype(
            ffn_grad.dtype
        ),
        lax.all_gather(attn_turned.astype(jnp.bfloat16), "dp", axis=1, tiled=True).astype(
            attn_turned.dtype
        ),
        lax.all_gather(ffn_turned.astype(jnp.bfloat16), "dp", axis=1, tiled=True).astype(
            ffn_turned.dtype
        ),
    )
    attn_left_sum, ffn_left_sum = left_statistics(attn_grad, ffn_grad, attn_cols, ffn_cols)
    attn_update = jnp.einsum(
        "srq,sqi->sri", attn_left_root, attn_turned_cols, precision=lax.Precision.HIGHEST
    )
    ffn_update = jnp.einsum(
        "srq,sqi->sri", ffn_left_root, ffn_turned_cols, precision=lax.Precision.HIGHEST
    )
    attn_left_new = 0.5 * attn_left + 0.5 * attn_left_sum
    attn_right_new = 0.5 * attn_right + 0.5 * attn_right_sum
    ffn_left_new = 0.5 * ffn_left + 0.5 * ffn_left_sum
    ffn_right_new = 0.5 * ffn_right + 0.5 * ffn_right_sum
    attn_new = attn_weights - shampoo_rate * (attn_update + shampoo_decay * attn_weights)
    ffn_new = ffn_weights - shampoo_rate * (ffn_update + shampoo_decay * ffn_weights)
    norm_m1, norm_m2, norm_new = adamw_step(norm_params, norm_total, norm_moment1, norm_moment2)
    knn_m1, knn_m2, knn_new = adamw_step(blending_coefficients, knn_total, knn_moment1, knn_moment2)
    return (
        mixed,
        input_grad,
        loss_total / token_count,
        attn_grad,
        attn_left_new,
        attn_right_new,
        attn_new,
        ffn_grad,
        ffn_left_new,
        ffn_right_new,
        ffn_new,
        norm_m1,
        norm_m2,
        norm_new,
        knn_m1,
        knn_m2,
        knn_new,
    )


LINE_BIT, HALF_BIT, CORE_BIT, X_BIT, Y_BIT = 1, 2, 4, 8, 16


def send_by(values_in, target):
    return lax.ppermute(values_in, ("dp", "tensor"), [(index, target(index)) for index in range(32)])


def flip(values_in, mask):
    return send_by(values_in, lambda index: index ^ mask)


def moves(index):
    return ((index >> 2) ^ (index >> 1)) & 1 == 1


def swapped(index):
    return index ^ (CORE_BIT | HALF_BIT) if moves(index) else index


def swap_core_half(values_in):
    return send_by(values_in, swapped)


def swap_or_near(values_in):
    return send_by(
        values_in, lambda index: swapped(index) if moves(index) else index ^ LINE_BIT
    )


def near_of_moved(values_in):
    pairs = [(index, index ^ LINE_BIT) for index in range(32) if moves(index)]
    return lax.ppermute(values_in, ("dp", "tensor"), pairs)


def cross_one(values_in):
    return send_by(values_in, lambda index: index ^ (Y_BIT if index & CORE_BIT else X_BIT))


def cross_two(values_in):
    return send_by(values_in, lambda index: index ^ (X_BIT if index & CORE_BIT else Y_BIT))


def pick(values_in, index, axis):
    return lax.dynamic_index_in_dim(values_in, index, axis, keepdims=False)


def ordered_pair(own, other, bit, axis):
    return jnp.where(
        bit == 0, jnp.stack([own, other], axis=axis), jnp.stack([other, own], axis=axis)
    )


def together(*values_in):
    return lax.optimization_barrier(values_in)


def by_chip(values_in, chip):
    width = values_in.shape[-1] // 4
    return jnp.concatenate(
        [
            lax.dynamic_slice_in_dim(values_in, (chip ^ block) * width, width, values_in.ndim - 1)
            for block in range(4)
        ],
        axis=-1,
    )


def add_far(pair):
    return jnp.concatenate([pair, flip(pair, CORE_BIT)], axis=0)


def weight_core(local_low, place):
    width = local_low.shape[2] // 2
    mine = lax.dynamic_slice_in_dim(local_low, place["core"] * width, width, 2)
    theirs = lax.dynamic_slice_in_dim(local_low, (1 - place["core"]) * width, width, 2)
    both = ordered_pair(mine, flip(theirs, CORE_BIT), place["core"], 1)
    return both.reshape(local_low.shape[0], 2 * local_low.shape[1], width)


def weight_halves(own, other, place):
    return jnp.where(
        place["half"] == 0,
        jnp.concatenate([own, other], axis=2),
        jnp.concatenate([other, own], axis=2),
    )


def by_rel(core, own, first, pair, axis):
    middle = jnp.where(
        core == 0,
        jnp.concatenate([first, pair[0]], axis=axis),
        jnp.concatenate([pair[0], first], axis=axis),
    )
    return jnp.concatenate([own, middle, pair[1]], axis=axis)


def scatter_parts(core, partials):
    parts = [partial.reshape(2, 2, -1, partial.shape[1]) for partial in partials]
    kept = [jnp.where(core == 0, part[:, 0], part[0]) for part in parts]
    sent = [jnp.where(core == 0, part[:, 1], part[1]) for part in parts]
    return jnp.stack(kept), jnp.stack(sent)


def add_low(left_part, right_part):
    return (left_part.astype(jnp.float32) + right_part.astype(jnp.float32)).astype(jnp.bfloat16)


def dot32(spec, left_mat, right_mat):
    return jnp.einsum(spec, left_mat, right_mat, preferred_element_type=jnp.float32)


def update_kernel(
    info_ref, left_ref, line_ref, first_ref, pair_ref, root_ref, own_ref, sent_ref, update_acc, gram_acc
):
    step = pl.program_id(1)
    steps = pl.num_programs(1)
    chip, core, tensor = info_ref[0], info_ref[1], info_ref[2]
    block = left_ref.shape[2] // 4
    own_rows = block // 2
    cols = update_acc.shape[1]

    @pl.when(step == 0)
    def _():
        update_acc[...] = jnp.zeros_like(update_acc)
        gram_acc[...] = jnp.zeros_like(gram_acc)

    pieces = (
        lambda: line_ref[0, 0],
        lambda: first_ref[0, 0],
        lambda: pair_ref[0, 0, 0],
        lambda: pair_ref[1, 0, 0],
    )
    rels = (0, 1 + core, 2 - core, 3)
    turned = None
    for rel, piece in zip(rels, pieces):
        start = pl.multiple_of((chip ^ rel) * block, block)
        part = jnp.dot(
            left_ref[0, :, pl.ds(start, block)], piece(), preferred_element_type=jnp.float32
        )
        turned = part if turned is None else turned + part

        @pl.when((chip ^ tensor) == rel)
        def _(piece=piece):
            gram_acc[...] += lax.dot_general(
                pieces[0](), piece(), (((1,), (1,)), ((), ())), preferred_element_type=jnp.float32
            )

    root = root_ref[...].reshape(-1, cols).astype(jnp.bfloat16)
    update_acc[...] += jnp.dot(
        turned.astype(jnp.bfloat16), root, preferred_element_type=jnp.float32
    )

    @pl.when(step == steps - 1)
    def _():
        own_ref[0, :, :cols] = update_acc[:own_rows]
        sent_ref[0, :, :cols] = update_acc[own_rows:].astype(jnp.bfloat16)
        gram_own = gram_acc[pl.ds(pl.multiple_of(core * own_rows, own_rows), own_rows), :]
        gram_sent = gram_acc[pl.ds(pl.multiple_of((1 - core) * own_rows, own_rows), own_rows), :]
        own_ref[0, :, cols:] = gram_own
        sent_ref[0, :, cols:] = gram_sent.astype(jnp.bfloat16)


def updates(info, left_low, pieces, root, split, at):
    line, first, pair = pieces
    _, lead, rows, width = line.shape
    count = 1 if split else lead
    cols = root.shape[2]
    root_rows = root.shape[1] // 8
    root = root.reshape(root.shape[0], 2, 2, 2, root_rows, cols)
    if split:
        steps = 4
        root_spec = pl.BlockSpec(
            (1, 1, 1, 1, root_rows, cols),
            lambda m, k, info_ref: (at, k & 1, info_ref[3] ^ (k >> 1), info_ref[1], 0, 0),
        )
    else:
        steps = 2
        root_spec = pl.BlockSpec(
            (1, 2, 1, 1, root_rows, cols),
            lambda m, k, info_ref: (m, 0, info_ref[3] ^ k, info_ref[1], 0, 0),
        )

    def place_of(m, k):
        return (k >> 1, k & 1) if split else (k, m)

    out_shape = (count, rows // 2, cols + rows)
    out_spec = pl.BlockSpec((1, rows // 2, cols + rows), lambda m, k, info_ref: (m, 0, 0))
    piece_spec = pl.BlockSpec(
        (1, 1, rows, width), lambda m, k, info_ref: place_of(m, k) + (0, 0)
    )
    return pl.pallas_call(
        update_kernel,
        grid_spec=pltpu.PrefetchScalarGridSpec(
            num_scalar_prefetch=1,
            grid=(count, steps),
            in_specs=[
                pl.BlockSpec((1, rows, 4 * rows), lambda m, k, info_ref: (m, 0, 0)),
                piece_spec,
                piece_spec,
                pl.BlockSpec(
                    (2, 1, 1, rows, width), lambda m, k, info_ref: (0,) + place_of(m, k) + (0, 0)
                ),
                root_spec,
            ],
            out_specs=[out_spec, out_spec],
            scratch_shapes=[
                pltpu.VMEM((rows, cols), jnp.float32),
                pltpu.VMEM((rows, rows), jnp.float32),
            ],
        ),
        out_shape=(
            jax.ShapeDtypeStruct(out_shape, jnp.float32),
            jax.ShapeDtypeStruct(out_shape, jnp.bfloat16),
        ),
        compiler_params=pltpu.CompilerParams(vmem_limit_bytes=48 * 1024 * 1024),
        cost_estimate=pl.CostEstimate(flops=1_000_000, bytes_accessed=100_000, transcendentals=0),
    )(info, left_low, line, first, pair, root)


def column_block(pieces, line_rel, half, split, core):
    line, first, pair = pieces

    def cut(piece):
        piece = piece[0] if line_rel is None else pick(piece, line_rel, 0)
        if split:
            return pick(piece, half, 0)[None]
        width = piece.shape[2] // 2
        return lax.dynamic_slice_in_dim(piece, half * width, width, 2)

    return by_rel(core, cut(line), cut(first), (cut(pair[0]), cut(pair[1])), 1)


def shampoo_part(info, pieces, left_low, weights_in, left_in, right_in, root, place, split, at):
    core = place["core"]
    own, sent = updates(info, left_low, pieces, root, split, at)
    received = flip(sent, CORE_BIT)
    total = own + received.astype(jnp.float32)
    rows, cols = weights_in.shape[1:]
    tensor_cols = column_block(pieces, None, place["half"], split, core)
    other_cols = flip(tensor_cols, CORE_BIT)
    chip_cols = column_block(pieces, place["line"] ^ place["x"], place["y"], split, core)
    both = jnp.where(
        core == 0,
        jnp.concatenate([tensor_cols, other_cols], axis=2),
        jnp.concatenate([other_cols, tensor_cols], axis=2),
    )
    right_sum = dot32("srk,srj->skj", both, chip_cols)
    grad = lax.dynamic_slice_in_dim(both, core * rows, rows, 1).astype(jnp.float32)
    return (
        grad,
        0.5 * left_in + 0.5 * total[:, :, cols:],
        0.5 * right_in + 0.5 * right_sum,
        weights_in - shampoo_rate * (total[:, :, :cols] + shampoo_decay * weights_in),
    )


def knn_kernel(
    info_ref, blend_ref, gaps_ref, ids_ref, targets_ref, logprob_ref, lm_ref, cot_ref, sums_ref
):
    step = pl.program_id(0)
    chip = info_ref[0]
    log_temperature = blend_ref[0:1, 0:1]
    sharpness_divisor = jnp.exp(log_temperature)
    interp = 1.0 / (1.0 + jnp.exp(-blend_ref[0:1, 1:2]))
    gaps = gaps_ref[...]
    logits = -gaps / sharpness_divisor
    near_exp = jnp.exp(logits - jnp.max(logits, axis=1, keepdims=True))
    mass = jnp.sum(near_exp, axis=1, keepdims=True)
    hits = ids_ref[...] == targets_ref[...]
    hit_exp = jnp.where(hits, near_exp, 0.0)
    retrieval = jnp.sum(hit_exp, axis=1, keepdims=True) / mass
    hit_gaps = jnp.sum(hit_exp * gaps, axis=1, keepdims=True) / mass
    all_gaps = jnp.sum(near_exp * gaps, axis=1, keepdims=True) / mass
    temp_terms = (hit_gaps - retrieval * all_gaps) / sharpness_divisor
    lm_prob = jnp.exp(logprob_ref[...])
    mixture = interp * retrieval + (1.0 - interp) * lm_prob
    lm_weight = -(1.0 - interp) * lm_prob / mixture
    temp_grad = jnp.sum(-(interp / mixture) * temp_terms, axis=0, keepdims=True)
    interp_grad = jnp.sum(
        -interp * (1.0 - interp) * (retrieval - lm_prob) / mixture, axis=0, keepdims=True
    )
    loss = jnp.sum(-jnp.log(mixture), axis=0, keepdims=True)
    lane = lax.broadcasted_iota(jnp.int32, sums_ref.shape, 1)
    sums = jnp.where(lane == 0, temp_grad, jnp.where(lane == 1, interp_grad, 0.0))
    sums = jnp.where(lane == 2, loss, sums)

    @pl.when(step == 0)
    def _():
        sums_ref[...] = jnp.zeros_like(sums_ref)

    sums_ref[...] += sums
    block = lm_ref.shape[1] // 4
    for rel in range(4):
        start = pl.multiple_of((chip ^ rel) * block, block)
        part = lm_weight * lm_ref[:, pl.ds(start, block)].astype(jnp.float32)
        cot_ref[:, rel * block : (rel + 1) * block] = part.astype(cot_ref.dtype)


def neighbours(where, blend, gaps, ids, targets, logprob, lm_grad):
    rows, width = gaps.shape
    step_rows = rows // 3
    wide = pl.BlockSpec((step_rows, width), lambda r, info_ref: (r, 0))
    thin = pl.BlockSpec((step_rows, 1), lambda r, info_ref: (r, 0))
    cot, sums = pl.pallas_call(
        knn_kernel,
        grid_spec=pltpu.PrefetchScalarGridSpec(
            num_scalar_prefetch=1,
            grid=(3,),
            in_specs=[
                pl.BlockSpec((1, 2), lambda r, info_ref: (0, 0)),
                wide,
                wide,
                thin,
                thin,
                wide,
            ],
            out_specs=[wide, pl.BlockSpec((8, width), lambda r, info_ref: (0, 0))],
        ),
        out_shape=(
            jax.ShapeDtypeStruct((rows, width), jnp.bfloat16),
            jax.ShapeDtypeStruct((8, width), jnp.float32),
        ),
        compiler_params=pltpu.CompilerParams(vmem_limit_bytes=32 * 1024 * 1024),
        cost_estimate=pl.CostEstimate(flops=1_000_000, bytes_accessed=100_000, transcendentals=0),
    )(where, blend[None], gaps, ids, targets[:, None], logprob[:, None], lm_grad)
    return cot, sums[:1]


def normalize_kernel(info_ref, pair_ref, far_ref, params_ref, out_ref, own_ref):
    step = pl.program_id(0)
    chip = info_ref[0]
    block = out_ref.shape[1] // 4

    def work(rows_ref):
        values_in = rows_ref[...].astype(jnp.float32)
        centre = jnp.mean(values_in, axis=-1, keepdims=True)
        spread_sq = jnp.mean((values_in - centre) ** 2, axis=-1, keepdims=True)
        scale = lax.rsqrt(spread_sq + norm_eps)
        for rel in range(4):
            start = pl.multiple_of((chip ^ rel) * block, block)
            own = slice(rel * block, (rel + 1) * block)
            part = rows_ref[:, pl.ds(start, block)].astype(jnp.float32)
            normed = (part - centre) * scale * params_ref[0:1, own] + params_ref[1:2, own]
            out_ref[:, own] = normed.astype(out_ref.dtype)

    @pl.when(step < 2)
    def _():
        work(pair_ref)

    @pl.when(step >= 2)
    def _():
        work(far_ref)

    @pl.when(step == 0)
    def _():
        for rel in range(4):
            start = pl.multiple_of((chip ^ rel) * block, block)
            own_ref[:, rel * block : (rel + 1) * block] = pair_ref[:, pl.ds(start, block)]


def normalize(where, pair, far, params):
    rows, width = pair.shape
    step_rows = rows // 2
    pair_spec = pl.BlockSpec((step_rows, width), lambda r, info_ref: (jnp.minimum(r, 1), 0))
    far_spec = pl.BlockSpec((step_rows, width), lambda r, info_ref: (jnp.maximum(r - 2, 0), 0))
    return pl.pallas_call(
        normalize_kernel,
        grid_spec=pltpu.PrefetchScalarGridSpec(
            num_scalar_prefetch=1,
            grid=(4,),
            in_specs=[
                pair_spec,
                far_spec,
                pl.BlockSpec(params.shape, lambda r, info_ref: (0, 0)),
            ],
            out_specs=[
                pl.BlockSpec((step_rows, width), lambda r, info_ref: (r, 0)),
                pl.BlockSpec((step_rows, width), lambda r, info_ref: (0, 0)),
            ],
        ),
        out_shape=(
            jax.ShapeDtypeStruct((2 * rows, width), pair.dtype),
            jax.ShapeDtypeStruct((step_rows, width), pair.dtype),
        ),
        compiler_params=pltpu.CompilerParams(vmem_limit_bytes=32 * 1024 * 1024),
        cost_estimate=pl.CostEstimate(flops=1_000_000, bytes_accessed=100_000, transcendentals=0),
    )(where, pair, far, params)


def ffn_kernel(normed_a, normed_b, cot_a, cot_b, up_ref, down_ref, act_ref, grad_ref):
    def work(normed_ref, cot_ref):
        pre = jnp.dot(normed_ref[...], up_ref[...], preferred_element_type=jnp.float32)
        grad_act = jnp.dot(cot_ref[...], down_ref[...], preferred_element_type=jnp.float32)
        scale = 0.7978845608028654
        square = pre * pre
        turn = jnp.tanh(pre * (scale + (scale * 0.044715) * square))
        gate = 0.5 + 0.5 * turn
        act_ref[...] = (pre * gate).astype(jnp.bfloat16)
        slope = gate + 0.5 * pre * (1.0 - turn * turn) * (scale + (3.0 * scale * 0.044715) * square)
        grad_ref[...] = (grad_act * slope).astype(jnp.bfloat16)

    @pl.when(pl.program_id(1) < 2)
    def _():
        work(normed_a, cot_a)

    @pl.when(pl.program_id(1) >= 2)
    def _():
        work(normed_b, cot_b)


def ffn_middle(normed, cot, w_up, w_down):
    rows, width = normed[0].shape
    hidden = w_up.shape[1]
    step_rows, step_cols = rows // 2, hidden // 2
    pair_spec = pl.BlockSpec((step_rows, width), lambda f, r: (jnp.minimum(r, 1), 0))
    far_spec = pl.BlockSpec((step_rows, width), lambda f, r: (jnp.maximum(r - 2, 0), 0))
    col_spec = pl.BlockSpec((width, step_cols), lambda f, r: (0, f))
    out_spec = pl.BlockSpec((step_rows, step_cols), lambda f, r: (r, f))
    shape = jax.ShapeDtypeStruct((2 * rows, hidden), jnp.bfloat16)
    return pl.pallas_call(
        ffn_kernel,
        grid=(2, 4),
        in_specs=[pair_spec, far_spec, pair_spec, far_spec, col_spec, col_spec],
        out_specs=[out_spec, out_spec],
        out_shape=(shape, shape),
        compiler_params=pltpu.CompilerParams(vmem_limit_bytes=48 * 1024 * 1024),
        cost_estimate=pl.CostEstimate(flops=1_000_000, bytes_accessed=100_000, transcendentals=0),
    )(*normed, *cot, w_up, w_down)


def masked_heads(values_in, lanes, head, scale):
    keep = (lanes >= head * HEAD_DIM) & (lanes < (head + 1) * HEAD_DIM)
    return jnp.where(keep, values_in * scale, jnp.zeros_like(values_in))


def forward_kernel(info_ref, qkv_ref, out_ref):
    pieces = 4
    rows = qkv_ref.shape[1] // pieces
    me = info_ref[0]
    starts = [pl.multiple_of((me ^ piece) * rows, rows) for piece in range(pieces)]
    lanes = lax.broadcasted_iota(jnp.int32, (rows, 128), 1)
    row_of = lax.broadcasted_iota(jnp.int32, (rows, rows), 0)
    col_of = lax.broadcasted_iota(jnp.int32, (rows, rows), 1)
    row_line = lax.broadcasted_iota(jnp.int32, (rows, 1), 0)
    for query in range(pieces):
        query_rows = qkv_ref[0, pl.ds(starts[query], rows), :]
        place = row_line + query * rows
        begin = info_ref[1] * jnp.ones_like(place)
        for block in range(1, qkv_ref.shape[1] // SHORT):
            begin = jnp.where(place >= block * SHORT, info_ref[1 + block], begin)
        outs = []
        for head in range(2):
            query_head = masked_heads(query_rows, lanes, head, HEAD_DIM**-0.5)
            scores = []
            for key in range(query + 1):
                key_rows = qkv_ref[1, pl.ds(starts[key], rows), :]
                score = lax.dot_general(
                    query_head, key_rows, (((1,), (1,)), ((), ())), preferred_element_type=jnp.float32
                )
                allowed = col_of + key * rows >= begin
                if key == query:
                    allowed = allowed & (col_of <= row_of)
                scores.append(jnp.where(allowed, score, -1e30))
            top = scores[0].max(axis=1, keepdims=True)
            for score in scores[1:]:
                top = jnp.maximum(top, score.max(axis=1, keepdims=True))
            mass = jnp.zeros_like(top)
            total = jnp.zeros((rows, 128), jnp.float32)
            for key in range(query + 1):
                value_rows = qkv_ref[2, pl.ds(starts[key], rows), :]
                chance = jnp.exp(scores[key] - top)
                mass = mass + chance.sum(axis=1, keepdims=True)
                total = total + jnp.dot(
                    chance.astype(jnp.bfloat16), value_rows, preferred_element_type=jnp.float32
                )
            outs.append(total / mass)
        out = jnp.where(lanes < HEAD_DIM, outs[0], outs[1])
        out_ref[pl.ds(starts[query], rows), :] = out.astype(jnp.bfloat16)


def backward_kernel(info_ref, qkv_ref, grad_ref, out_ref, key_acc, value_acc, key_turned):
    pieces = 4
    rows = qkv_ref.shape[1] // pieces
    me = info_ref[0]
    starts = [pl.multiple_of((me ^ piece) * rows, rows) for piece in range(pieces)]
    lanes = lax.broadcasted_iota(jnp.int32, (rows, 128), 1)
    key_of = lax.broadcasted_iota(jnp.int32, (rows, rows), 0)
    row_of = lax.broadcasted_iota(jnp.int32, (rows, rows), 1)
    row_line = lax.broadcasted_iota(jnp.int32, (1, rows), 1)
    key_acc[...] = jnp.zeros_like(key_acc)
    value_acc[...] = jnp.zeros_like(value_acc)
    for key in range(pieces):
        key_rows = qkv_ref[1, pl.ds(starts[key], rows), :]
        key_turned[key] = key_rows.astype(jnp.float32).T.astype(jnp.bfloat16)
    for query in range(pieces):
        query_rows = qkv_ref[0, pl.ds(starts[query], rows), :]
        grad_rows = grad_ref[pl.ds(starts[query], rows), :]
        place = row_line + query * rows
        begin = info_ref[1] * jnp.ones_like(place)
        for block in range(1, qkv_ref.shape[1] // SHORT):
            begin = jnp.where(place >= block * SHORT, info_ref[1 + block], begin)
        query_grad = jnp.zeros((128, rows), jnp.float32)
        for head in range(2):
            query_head = masked_heads(query_rows, lanes, head, HEAD_DIM**-0.5)
            grad_head = masked_heads(grad_rows, lanes, head, 1.0)
            scores, slopes = [], []
            for key in range(query + 1):
                key_rows = qkv_ref[1, pl.ds(starts[key], rows), :]
                score = lax.dot_general(
                    key_rows, query_head, (((1,), (1,)), ((), ())), preferred_element_type=jnp.float32
                )
                allowed = key_of + key * rows >= begin
                if key == query:
                    allowed = allowed & (key_of <= row_of)
                scores.append(jnp.where(allowed, score, -1e30))
            top = scores[0].max(axis=0, keepdims=True)
            for score in scores[1:]:
                top = jnp.maximum(top, score.max(axis=0, keepdims=True))
            mass = jnp.zeros_like(top)
            inner = jnp.zeros_like(top)
            chances = []
            for key in range(query + 1):
                value_rows = qkv_ref[2, pl.ds(starts[key], rows), :]
                slope = lax.dot_general(
                    value_rows, grad_head, (((1,), (1,)), ((), ())), preferred_element_type=jnp.float32
                )
                chance = jnp.exp(scores[key] - top)
                mass = mass + chance.sum(axis=0, keepdims=True)
                inner = inner + (chance * slope).sum(axis=0, keepdims=True)
                chances.append(chance)
                slopes.append(slope)
            share = 1.0 / mass
            inner = inner * share
            half = slice(head * HEAD_DIM, (head + 1) * HEAD_DIM)
            parts = []
            for key in range(query + 1):
                probs = chances[key] * share
                grad_scores = (probs * (slopes[key] - inner)).astype(jnp.bfloat16)
                value_acc[key] += jnp.dot(
                    probs.astype(jnp.bfloat16), grad_head, preferred_element_type=jnp.float32
                )
                key_acc[key] += jnp.dot(
                    grad_scores, query_head, preferred_element_type=jnp.float32
                )
                parts.append(
                    jnp.dot(
                        key_turned[key, half, :], grad_scores, preferred_element_type=jnp.float32
                    )
                )
            total = parts[0]
            for part in parts[1:]:
                total = total + part
            if head == 0:
                query_grad = total
            else:
                query_grad = jnp.concatenate([query_grad, total], axis=0)
        out_ref[0, pl.ds(starts[query], rows), :] = (
            query_grad.T * (HEAD_DIM**-0.5)
        ).astype(jnp.bfloat16)
    for key in range(pieces):
        out_ref[1, pl.ds(starts[key], rows), :] = key_acc[key].astype(jnp.bfloat16)
        out_ref[2, pl.ds(starts[key], rows), :] = value_acc[key].astype(jnp.bfloat16)


def attend(info, qkv):
    _, rows, width = qkv.shape
    return pl.pallas_call(
        forward_kernel,
        grid_spec=pltpu.PrefetchScalarGridSpec(
            num_scalar_prefetch=1,
            grid=(width // 128,),
            in_specs=[pl.BlockSpec((3, rows, 128), lambda pair, info_ref: (0, 0, pair))],
            out_specs=pl.BlockSpec((rows, 128), lambda pair, info_ref: (0, pair)),
        ),
        out_shape=jax.ShapeDtypeStruct((rows, width), jnp.bfloat16),
        compiler_params=pltpu.CompilerParams(vmem_limit_bytes=48 * 1024 * 1024),
        cost_estimate=pl.CostEstimate(
            flops=1_000_000, bytes_accessed=100_000, transcendentals=0
        ),
    )(info, qkv)


def attend_back(info, qkv, grad_heads, pair, earlier):
    _, rows, width = qkv.shape
    extra = [] if earlier is None else [pl.BlockSpec(memory_space=pl.ANY)]

    def kernel(info_ref, qkv_ref, grad_ref, *others):
        backward_kernel(info_ref, qkv_ref, grad_ref, *others[len(extra) :])

    return pl.pallas_call(
        kernel,
        grid_spec=pltpu.PrefetchScalarGridSpec(
            num_scalar_prefetch=1,
            grid=(1,),
            in_specs=[
                pl.BlockSpec((3, rows, 128), lambda step, info_ref: (0, 0, pair)),
                pl.BlockSpec((rows, 128), lambda step, info_ref: (0, pair)),
            ]
            + extra,
            out_specs=pl.BlockSpec((3, rows, 128), lambda step, info_ref: (0, 0, pair)),
            scratch_shapes=[
                pltpu.VMEM((4, rows // 4, 128), jnp.float32),
                pltpu.VMEM((4, rows // 4, 128), jnp.float32),
                pltpu.VMEM((4, 128, rows // 4), jnp.bfloat16),
            ],
        ),
        out_shape=jax.ShapeDtypeStruct(qkv.shape, jnp.bfloat16),
        input_output_aliases={} if earlier is None else {3: 0},
        compiler_params=pltpu.CompilerParams(vmem_limit_bytes=48 * 1024 * 1024),
        cost_estimate=pl.CostEstimate(
            flops=1_000_000, bytes_accessed=100_000, transcendentals=0
        ),
    )(info, qkv, grad_heads, *([] if earlier is None else [earlier]))


def regrouped(
    tokens_in,
    lm_grad,
    lm_logprob,
    targets,
    neighbor_ids,
    nearby_entry_gaps,
    seq_lengths,
    attn_weights,
    ffn_weights,
    attn_left,
    attn_right,
    ffn_left,
    ffn_right,
    attn_left_root,
    attn_right_root,
    ffn_left_root,
    ffn_right_root,
    norm_params,
    norm_moment1,
    norm_moment2,
    blending_coefficients,
    knn_moment1,
    knn_moment2,
):
    low = jnp.bfloat16
    rows = tokens_in.shape[0]
    group_rows = 4 * rows
    dp_index, tensor_index = lax.axis_index("dp"), lax.axis_index("tensor")
    place = {
        "line": tensor_index & 1,
        "half": tensor_index >> 1,
        "core": dp_index & 1,
        "x": (dp_index >> 1) & 1,
        "y": dp_index >> 2,
        "chip": dp_index >> 1,
    }
    me = place["core"] * 2 + place["line"]
    chip, core = place["chip"], place["core"]
    staying = core == place["half"]

    where = jnp.stack([chip, core, tensor_index, place["line"]]).astype(jnp.int32)
    tokens_one = swap_or_near(tokens_in)
    wa = weight_core(attn_weights.astype(low), place)
    wa, ffn_weights_in, nearby_entry_gaps, lengths_in = together(
        wa, ffn_weights, nearby_entry_gaps, seq_lengths
    )
    wa_other = flip(wa, HALF_BIT)
    wf = weight_core(ffn_weights_in.astype(low), place)
    other_lengths = flip(lengths_in.astype(jnp.float32), CORE_BIT).astype(jnp.int32)
    lengths = jnp.where(staying, seq_lengths, other_lengths)
    params = by_chip(norm_params, chip)
    block_begins = first_blocks(lengths, group_rows, SHORT) * SHORT
    info = jnp.concatenate([me[None].astype(jnp.int32), block_begins.astype(jnp.int32)])
    cot_low, knn_sums = neighbours(
        where,
        blending_coefficients,
        nearby_entry_gaps,
        neighbor_ids,
        targets,
        lm_logprob,
        lm_grad,
    )
    tokens_one, wf, params, info, wa_other, cot_low = together(
        tokens_one, wf, params, info, wa_other, cot_low
    )
    tokens_two = near_of_moved(tokens_one)
    wa = weight_halves(wa, wa_other, place)
    wa_first = cross_one(wa)
    wf_other = flip(wf, HALF_BIT)
    tokens_one, tokens_two, wa_first, cot_low = together(tokens_one, tokens_two, wa_first, cot_low)
    pair1 = jnp.concatenate(
        [
            jnp.where(staying, tokens_in, tokens_one),
            jnp.where(staying, tokens_one, tokens_two),
        ],
        axis=0,
    )
    far1 = flip(pair1, CORE_BIT)
    wa_pair = cross_two(jnp.stack([wa, wa_first]))
    cot_one = swap_or_near(cot_low)
    far1, pair1 = together(far1, pair1)
    normed1_all, own_low = normalize(where, pair1, far1, params)
    resid = own_low.astype(jnp.float32)
    _, norm1_back = jax.vjp(layer_norm, resid, params[0], params[1])
    normed1_all, wa_pair = together(normed1_all, wa_pair)
    wa_all = by_rel(core, wa, wa_first, wa_pair, 1)
    proj_in, proj_out = wa_all[:3], wa_all[3]

    qkv = dot32("rd,sdc->src", normed1_all, proj_in).astype(low)
    heads_flat = attend(info, qkv)
    heads_flat, wf_other, wf, cot_one = together(heads_flat, wf_other, wf, cot_one)

    def out_rows(a, b):
        return dot32("rc,dc->rd", heads_flat[a:b], proj_out)

    sent4 = out_rows(2 * rows, 4 * rows).astype(low)
    sent4, wf, heads_flat = together(sent4, weight_halves(wf, wf_other, place), heads_flat)
    received4 = flip(sent4, CORE_BIT)
    wf_first = cross_one(wf)
    near4 = (out_rows(rows, 2 * rows) + received4[rows:].astype(jnp.float32)).astype(low)
    near4, cot_one, heads_flat = together(near4, cot_one, heads_flat)
    from_near4 = flip(near4, LINE_BIT)
    cot_two = near_of_moved(cot_one)
    attn_out = out_rows(0, rows) + received4[:rows].astype(jnp.float32)
    attn_out, from_near4, wf_first, cot_two = together(attn_out, from_near4, wf_first, cot_two)
    middle = resid + attn_out + from_near4.astype(jnp.float32)
    normed2, norm2_back = jax.vjp(layer_norm, middle, params[2], params[3])
    normed2_low = normed2.astype(low)
    normed2_low, cot_two = together(normed2_low, cot_two)
    near2 = flip(normed2_low, LINE_BIT)
    wf_pair = cross_two(jnp.stack([wf, wf_first]))
    cot_moved = jnp.where(staying, cot_low, cot_one)
    pair_cot = jnp.concatenate([cot_moved, jnp.where(staying, cot_one, cot_two)], axis=0)
    far_cot = flip(pair_cot, CORE_BIT)
    cotangent = cot_moved.astype(jnp.float32)
    near2, far_cot, cotangent, normed2_low, wf_pair = together(
        near2, far_cot, cotangent, normed2_low, wf_pair
    )
    pair2 = jnp.concatenate([normed2_low, near2], axis=0)
    far2 = flip(pair2, CORE_BIT)
    wf_all = by_rel(core, wf, wf_first, wf_pair, 1)
    w_up, w_down = wf_all[0], wf_all[1]

    far2, w_up, w_down = together(far2, w_up, w_down)
    act_low, grad_pre_low = ffn_middle((pair2, far2), (pair_cot, far_cot), w_up, w_down)

    def back_rows(a, b):
        return dot32("rf,df->rd", grad_pre_low[a:b], w_up)

    sent2 = back_rows(2 * rows, 4 * rows).astype(low)
    sent2, pair2, far2, pair_cot, far_cot, act_low = together(
        sent2, pair2, far2, pair_cot, far_cot, act_low
    )
    normed2_all = jnp.concatenate([pair2, far2], axis=0)
    cot_all = jnp.concatenate([pair_cot, far_cot], axis=0)
    received2 = flip(sent2, CORE_BIT)
    cut = ffn_weights.shape[2] // 2
    up_halves = [
        dot32("rd,rf->df", normed2_all, grad_pre_low[:, :cut]),
        dot32("rd,rf->df", normed2_all, grad_pre_low[:, cut:]),
    ]
    up_kept, up_sent = scatter_parts(core, [part.astype(low) for part in up_halves])
    near2 = back_rows(rows, 2 * rows) + received2[rows:].astype(jnp.float32)
    near2, up_kept, up_sent, act_low = together(near2.astype(low), up_kept, up_sent, act_low)
    from_near2 = flip(near2, LINE_BIT)
    up_got = cross_one(up_sent)
    own2 = back_rows(0, rows) + received2[:rows].astype(jnp.float32)
    down_halves = [
        dot32("rd,rf->df", cot_all, act_low[:, :cut]),
        dot32("rd,rf->df", cot_all, act_low[:, cut:]),
    ]
    down_kept, down_sent = scatter_parts(core, [part.astype(low) for part in down_halves])
    down_got = cross_one(down_sent)
    own2, from_near2, up_kept, up_got, down_kept = together(
        own2, from_near2, up_kept, up_got, down_kept
    )
    grad_normed2 = own2 + from_near2.astype(jnp.float32)
    mid_norm_grad, gain2_grad, shift2_grad = norm2_back(grad_normed2)
    grad_middle = cotangent + mid_norm_grad
    up_kept = add_low(up_kept, up_got)
    mid_low, up_kept, act_low = together(grad_middle.astype(low), up_kept, act_low)
    near_mid = flip(mid_low, LINE_BIT)
    up_got = cross_two(up_kept[:, 1])
    ffn_sent = dot32("rf,df->rd", act_low[2 * rows :], w_down).astype(low)
    down_got, ffn_sent, act_low = together(down_got, ffn_sent, act_low)
    down_kept = add_low(down_kept, down_got)
    down_got = cross_two(down_kept[:, 1])
    ffn_received = flip(ffn_sent, CORE_BIT)
    ffn_near = dot32("rf,df->rd", act_low[rows : 2 * rows], w_down) + ffn_received[rows:].astype(
        jnp.float32
    )
    ffn_out = dot32("rf,df->rd", act_low[:rows], w_down) + ffn_received[:rows].astype(jnp.float32)
    near_mid, up_got, ffn_near, ffn_out, mid_low = together(
        near_mid, up_got, ffn_near.astype(low), ffn_out, mid_low
    )
    pair_mid = jnp.concatenate([mid_low, near_mid], axis=0)
    far_mid = flip(pair_mid, CORE_BIT)
    up_part = add_low(up_kept[:, 0], up_got)
    up_other = flip(up_part, HALF_BIT)

    grad_heads = jnp.concatenate(
        [dot32("rd,dc->rc", part, proj_out).astype(low) for part in (pair_mid, far_mid)], axis=0
    )
    grad_heads, down_got, ffn_near = together(grad_heads, down_got, ffn_near)
    grad_heads, down_part = together(grad_heads, add_low(down_kept[:, 0], down_got))
    down_other = flip(down_part, HALF_BIT)
    ffn_from_near = flip(ffn_near, LINE_BIT)
    grad_half = attend_back(info, qkv, grad_heads, 0, None)
    grad_half, pair_mid, far_mid = together(grad_half, pair_mid, far_mid)
    grad_out_proj = dot32("rd,rc->dc", pair_mid, heads_flat[: 2 * rows]) + dot32(
        "rd,rc->dc", far_mid, heads_flat[2 * rows :]
    )
    grad_out_proj = grad_out_proj.astype(low)
    grad_qkv = attend_back(info, qkv, grad_heads, 1, grad_half)
    grad_qkv, up_other, grad_out_proj = together(grad_qkv, up_other, grad_out_proj)
    grad_qkv, up_own = together(grad_qkv, add_low(up_part, up_other))
    up_near = flip(up_own, LINE_BIT)
    grad_parts = [
        dot32("rd,rc->dc", normed1_all, grad_qkv[part]).astype(low) for part in range(3)
    ] + [grad_out_proj]
    attn_kept, attn_sent = scatter_parts(core, grad_parts)
    attn_kept, attn_sent, grad_qkv, up_near = together(attn_kept, attn_sent, grad_qkv, up_near)
    attn_got = cross_one(attn_sent)

    def back_in(a, b):
        return dot32("src,sdc->rd", grad_qkv[:, a:b], proj_in)

    sent1 = back_in(2 * rows, 4 * rows).astype(low)
    attn_got, attn_kept, sent1, up_own, up_near, down_other = together(
        attn_got, attn_kept, sent1, up_own, up_near, down_other
    )

    attn_kept = add_low(attn_kept, attn_got)
    down_own = add_low(down_part, down_other)
    up_line = jnp.stack([up_own, up_near])
    attn_kept, down_own, up_line, sent1, grad_qkv = together(
        attn_kept, down_own, up_line, sent1, grad_qkv
    )
    attn_got = cross_two(attn_kept[:, 1])
    down_first = cross_one(down_own)
    up_first = cross_one(up_line)
    received1 = flip(sent1, CORE_BIT)
    near3 = back_in(rows, 2 * rows)
    attn_got, attn_kept, received1, near3, grad_qkv = together(
        attn_got, attn_kept, received1, near3, grad_qkv
    )

    attn_part = add_low(attn_kept[:, 0], attn_got)
    near3 = near3 + received1[rows:].astype(jnp.float32)
    attn_part, near3, grad_qkv = together(attn_part, near3.astype(low), grad_qkv)
    attn_other = flip(attn_part, HALF_BIT)
    from_near3 = flip(near3, LINE_BIT)
    own3 = back_in(0, rows) + received1[:rows].astype(jnp.float32)
    up_first, up_line, down_first, down_own, own3, ffn_out = together(
        up_first, up_line, down_first, down_own, own3, ffn_out
    )
    down_two = jnp.stack([down_own, down_first])
    down_pair = cross_two(down_two)
    up_pair = cross_two(jnp.stack([up_line, up_first]))
    ffn_out = ffn_out + ffn_from_near.astype(jnp.float32)
    mixed = by_chip((middle + ffn_out).astype(low), chip)
    attn_other, attn_part, from_near3, mixed, own3 = together(
        attn_other, attn_part, from_near3, mixed, own3
    )

    attn_own = add_low(attn_part, attn_other)
    attn_own, own3, from_near3 = together(attn_own, own3, from_near3)
    attn_near = flip(attn_own, LINE_BIT)
    grad_normed1 = own3 + from_near3.astype(jnp.float32)
    res_norm_grad, gain1_grad, shift1_grad = norm1_back(grad_normed1)
    input_grad = by_chip((grad_middle + res_norm_grad).astype(low), chip)
    norm_grads = by_chip(jnp.stack([gain1_grad, shift1_grad, gain2_grad, shift2_grad]), chip)
    small = jnp.concatenate([norm_grads, knn_sums], axis=0)

    attn_left_low = attn_left_root.astype(low)
    ffn_left_low = ffn_left_root.astype(low)
    attn_left_low = jnp.concatenate([attn_left_low, flip(attn_left_low, CORE_BIT)], axis=1)
    ffn_left_low = jnp.concatenate([ffn_left_low, flip(ffn_left_low, CORE_BIT)], axis=1)

    def ffn_part(at, pieces):
        return shampoo_part(
            where,
            pieces,
            ffn_left_low[at : at + 1],
            ffn_weights[at : at + 1],
            ffn_left[at : at + 1],
            ffn_right[at : at + 1],
            ffn_right_root,
            place,
            True,
            at,
        )

    attn_near, attn_own, small, mixed, input_grad, up_pair, down_pair = together(
        attn_near, attn_own, small, mixed, input_grad, up_pair, down_pair
    )

    attn_line = jnp.stack([attn_own, attn_near])
    down_four = jnp.concatenate([down_two, down_pair], axis=0)
    attn_line, up_pair, small, mixed, down_four = together(
        attn_line, up_pair, small, mixed, down_four
    )
    attn_first = cross_one(attn_line)
    down_far = flip(down_four, LINE_BIT)
    mixed = swap_core_half(mixed)
    small = small + flip(small, CORE_BIT)
    up_new = ffn_part(0, (up_line, up_first, up_pair))
    attn_first, attn_line, small, input_grad = together(attn_first, attn_line, small, input_grad)

    attn_two = jnp.stack([attn_line, attn_first])
    attn_two, input_grad, small, down_far = together(attn_two, input_grad, small, down_far)
    attn_pair = cross_two(attn_two)
    input_grad = swap_core_half(input_grad)
    down_all = jnp.stack([down_four, down_far], axis=1)
    down_new = ffn_part(1, (down_all[0], down_all[1], down_all[2:]))
    ffn_new_all = tuple(jnp.concatenate(parts, axis=0) for parts in zip(up_new, down_new))
    attn_pair, ffn_new_all, mixed, small = together(attn_pair, ffn_new_all, mixed, small)
    ffn_grad, ffn_left_new, ffn_right_new, ffn_new = ffn_new_all
    for mask in (X_BIT, Y_BIT, LINE_BIT, HALF_BIT):
        small = small + flip(small, mask)
    summed = small
    attn_grad, attn_left_new, attn_right_new, attn_new = shampoo_part(
        where,
        (attn_line, attn_first, attn_pair),
        attn_left_low,
        attn_weights,
        attn_left,
        attn_right,
        attn_right_root,
        place,
        False,
        0,
    )
    input_grad = input_grad.astype(jnp.float32)
    norm_total = summed[:4]
    knn_total = summed[4, :2]
    loss = summed[4, 2] / (group_rows * 8)
    norm_m1, norm_m2, norm_new = adamw_step(norm_params, norm_total, norm_moment1, norm_moment2)
    knn_m1, knn_m2, knn_new = adamw_step(blending_coefficients, knn_total, knn_moment1, knn_moment2)
    return (
        mixed,
        input_grad,
        loss,
        attn_grad,
        attn_left_new,
        attn_right_new,
        attn_new,
        ffn_grad,
        ffn_left_new,
        ffn_right_new,
        ffn_new,
        norm_m1,
        norm_m2,
        norm_new,
        knn_m1,
        knn_m2,
        knn_new,
    )


def solution(mesh):
    sized = (mesh.shape["dp"], mesh.shape["tensor"]) == (8, 4)
    placed = (
        P(("dp", "tensor"), None),
        P(("dp", "tensor"), None),
        P(("dp", "tensor")),
        P(("dp", "tensor")),
        P(("dp", "tensor"), None),
        P(("dp", "tensor"), None),
        P("dp", None),
        P(None, "dp", "tensor"),
        P(None, "dp", "tensor"),
        P(None, "dp", "tensor"),
        P(None, "tensor", "dp"),
        P(None, "dp", "tensor"),
        P(None, "tensor", "dp"),
        P(None, "dp", None),
        P(None, None, "tensor"),
        P(None, "dp", None),
        P(None, None, "tensor"),
        P(),
        P(),
        P(),
        P(),
        P(),
        P(),
    )
    return jax.shard_map(
        regrouped if sized else local,
        mesh=mesh,
        in_specs=placed,
        out_specs=(
            P(("dp", "tensor"), None),
            P(("dp", "tensor"), None),
            P(),
            P(None, "dp", "tensor"),
            P(None, "dp", "tensor"),
            P(None, "tensor", "dp"),
            P(None, "dp", "tensor"),
            P(None, "dp", "tensor"),
            P(None, "dp", "tensor"),
            P(None, "tensor", "dp"),
            P(None, "dp", "tensor"),
            P(),
            P(),
            P(),
            P(),
            P(),
            P(),
        ),
        check_vma=False,
    )
```

```python
import jax
import jax.numpy as jnp
from jax import lax
from jax.experimental import pallas as pl
from jax.experimental.pallas import tpu as pltpu
from jax.sharding import PartitionSpec as P

SHORT = 512
STEP = 10
HEAD_DIM = 64


adam_rate = 0.3
shampoo_rate = 0.5
shampoo_decay = 0.01
norm_eps = 1e-05


def layer_norm(values_in, gain, shift):
    centre = jnp.mean(values_in, axis=-1, keepdims=True)
    centred = values_in - centre
    spread_sq = jnp.mean(centred * centred, axis=-1, keepdims=True)
    return centred * lax.rsqrt(spread_sq + norm_eps) * gain + shift


def gelu_tanh(values_in):
    return jax.nn.gelu(values_in, approximate=True)


def spread_rows(local_low):
    return lax.all_gather(local_low, "tensor", axis=0, tiled=True)


def spread_again(local_low):
    return lax.all_gather(local_low, "tensor", axis=0, tiled=True)


def spread_grads(local_low):
    return lax.all_gather(local_low, "tensor", axis=0, tiled=True)


def branch_total(left_rows, right_mat):
    return lax.psum_scatter(
        jnp.einsum("rc,dc->rd", left_rows, right_mat, preferred_element_type=jnp.float32),
        "tensor",
        scatter_dimension=0,
        tiled=True,
    )


def input_total(left_rows, right_mat):
    return lax.psum_scatter(
        jnp.einsum("rc,dc->rd", left_rows, right_mat, preferred_element_type=jnp.float32),
        "tensor",
        scatter_dimension=0,
        tiled=True,
    )


def first_blocks(seq_lengths, group_rows, block_rows):
    lengths = seq_lengths[0]
    seq_ends = jnp.cumsum(lengths)
    seq_begins = seq_ends - lengths
    block_begins = jnp.arange(group_rows // block_rows, dtype=jnp.int32) * block_rows
    inside = (seq_begins[None, :] <= block_begins[:, None]) & (lengths[None, :] > 0)
    return jnp.max(jnp.where(inside, seq_begins[None, :], 0), axis=1) // block_rows


def block_scores(query_rows, key_rows, query_block, key_block, block_rows, score_scale):
    scores = (
        jnp.einsum("qhd,khd->hqk", query_rows, key_rows, preferred_element_type=jnp.float32)
        * score_scale
    )
    query_pos = query_block * block_rows + jnp.arange(block_rows, dtype=jnp.int32)
    key_pos = key_block * block_rows + jnp.arange(block_rows, dtype=jnp.int32)
    allowed = key_pos[None, :] <= query_pos[:, None]
    return jnp.where(allowed[None], scores, -1e30)


def attend_forward(query_all, key_all, value_all, first_block, block_rows, score_scale):
    group_rows, head_count, head_width = query_all.shape

    def one_block(query_block):
        query_rows = lax.dynamic_slice_in_dim(query_all, query_block * block_rows, block_rows, 0)

        def peak_step(key_block, loop_state):
            running_top, running_mass = loop_state
            key_rows = lax.dynamic_slice_in_dim(key_all, key_block * block_rows, block_rows, 0)
            scores = block_scores(
                query_rows, key_rows, query_block, key_block, block_rows, score_scale
            )
            new_top = jnp.maximum(running_top, jnp.max(scores, axis=2))
            new_mass = running_mass * jnp.exp(running_top - new_top) + jnp.sum(
                jnp.exp(scores - new_top[:, :, None]), axis=2
            )
            return (new_top, new_mass)

        start_state = (
            jnp.full((head_count, block_rows), -1e30, jnp.float32),
            jnp.zeros((head_count, block_rows), jnp.float32),
        )
        final_top, final_mass = lax.fori_loop(
            first_block[query_block], query_block + 1, peak_step, start_state
        )
        log_mass = final_top + jnp.log(final_mass)

        def value_step(key_block, out_acc):
            key_rows = lax.dynamic_slice_in_dim(key_all, key_block * block_rows, block_rows, 0)
            value_rows = lax.dynamic_slice_in_dim(value_all, key_block * block_rows, block_rows, 0)
            scores = block_scores(
                query_rows, key_rows, query_block, key_block, block_rows, score_scale
            )
            attn_probs = jnp.exp(scores - log_mass[:, :, None]).astype(jnp.bfloat16)
            return out_acc + jnp.einsum(
                "hqk,khd->qhd", attn_probs, value_rows, preferred_element_type=jnp.float32
            )

        out_rows = lax.fori_loop(
            first_block[query_block],
            query_block + 1,
            value_step,
            jnp.zeros((block_rows, head_count, head_width), jnp.float32),
        )
        return (out_rows.astype(jnp.bfloat16), log_mass)

    outs, log_masses = lax.map(one_block, jnp.arange(group_rows // block_rows, dtype=jnp.int32))
    return (outs.reshape(group_rows, head_count, head_width), log_masses)


def attend_backward(
    query_all, key_all, value_all, grad_out, log_masses, first_block, block_rows, score_scale
):
    group_rows, head_count, head_width = query_all.shape

    def one_block(query_block, loop_carry):
        grad_keys, grad_values, grad_query = loop_carry
        query_rows = lax.dynamic_slice_in_dim(query_all, query_block * block_rows, block_rows, 0)
        grad_rows = lax.dynamic_slice_in_dim(grad_out, query_block * block_rows, block_rows, 0)
        log_mass = log_masses[query_block]

        def chances(key_block):
            key_rows = lax.dynamic_slice_in_dim(key_all, key_block * block_rows, block_rows, 0)
            value_rows = lax.dynamic_slice_in_dim(value_all, key_block * block_rows, block_rows, 0)
            scores = block_scores(
                query_rows, key_rows, query_block, key_block, block_rows, score_scale
            )
            attn_probs = jnp.exp(scores - log_mass[:, :, None])
            likelihood_cotangent = jnp.einsum(
                "qhd,khd->hqk", grad_rows, value_rows, preferred_element_type=jnp.float32
            )
            return (key_rows, attn_probs, likelihood_cotangent)

        def inner_step(key_block, inner_acc):
            _, attn_probs, likelihood_cotangent = chances(key_block)
            return inner_acc + jnp.sum(attn_probs * likelihood_cotangent, axis=2)

        row_inner = lax.fori_loop(
            first_block[query_block],
            query_block + 1,
            inner_step,
            jnp.zeros((head_count, block_rows), jnp.float32),
        )

        def grad_step(key_block, loop_state):
            query_acc, keys_acc, values_acc = loop_state
            key_rows, attn_probs, likelihood_cotangent = chances(key_block)
            grad_scores = (attn_probs * (likelihood_cotangent - row_inner[:, :, None])).astype(
                jnp.bfloat16
            )
            query_acc = (
                query_acc
                + jnp.einsum(
                    "hqk,khd->qhd", grad_scores, key_rows, preferred_element_type=jnp.float32
                )
                * score_scale
            )
            key_part = (
                jnp.einsum(
                    "hqk,qhd->khd", grad_scores, query_rows, preferred_element_type=jnp.float32
                )
                * score_scale
            )
            value_part = jnp.einsum(
                "hqk,qhd->khd",
                attn_probs.astype(jnp.bfloat16),
                grad_rows,
                preferred_element_type=jnp.float32,
            )
            key_start = key_block * block_rows
            keys_acc = lax.dynamic_update_slice_in_dim(
                keys_acc,
                lax.dynamic_slice_in_dim(keys_acc, key_start, block_rows, 0) + key_part,
                key_start,
                0,
            )
            values_acc = lax.dynamic_update_slice_in_dim(
                values_acc,
                lax.dynamic_slice_in_dim(values_acc, key_start, block_rows, 0) + value_part,
                key_start,
                0,
            )
            return (query_acc, keys_acc, values_acc)

        query_acc, grad_keys, grad_values = lax.fori_loop(
            first_block[query_block],
            query_block + 1,
            grad_step,
            (jnp.zeros((block_rows, head_count, head_width), jnp.float32), grad_keys, grad_values),
        )
        grad_query = lax.dynamic_update_slice_in_dim(
            grad_query, query_acc, query_block * block_rows, 0
        )
        return (grad_keys, grad_values, grad_query)

    zeros_all = jnp.zeros((group_rows, head_count, head_width), jnp.float32)
    return lax.fori_loop(0, group_rows // block_rows, one_block, (zeros_all, zeros_all, zeros_all))


def right_statistics(attn_part_grad, ffn_part_grad, attn_rows, ffn_rows):
    attn_part = jnp.einsum(
        "sri,srj->sij", attn_part_grad, attn_rows, precision=lax.Precision.HIGHEST
    )
    ffn_part = jnp.einsum("sri,srj->sij", ffn_part_grad, ffn_rows, precision=lax.Precision.HIGHEST)
    return (
        lax.psum_scatter(
            attn_part.astype(jnp.bfloat16), "dp", scatter_dimension=2, tiled=True
        ).astype(jnp.float32),
        lax.psum_scatter(
            ffn_part.astype(jnp.bfloat16), "dp", scatter_dimension=2, tiled=True
        ).astype(jnp.float32),
    )


def left_statistics(attn_part_grad, ffn_part_grad, attn_cols, ffn_cols):
    attn_part = jnp.einsum(
        "sri,sqi->srq", attn_part_grad, attn_cols, precision=lax.Precision.HIGHEST
    )
    ffn_part = jnp.einsum("sri,sqi->srq", ffn_part_grad, ffn_cols, precision=lax.Precision.HIGHEST)
    return (
        lax.psum_scatter(
            attn_part.astype(jnp.bfloat16), "tensor", scatter_dimension=2, tiled=True
        ).astype(jnp.float32),
        lax.psum_scatter(
            ffn_part.astype(jnp.bfloat16), "tensor", scatter_dimension=2, tiled=True
        ).astype(jnp.float32),
    )


def adamw_step(params_in, grads_in, first_in, second_in):
    first_new = 0.9 * first_in + 0.1 * grads_in
    second_new = 0.999 * second_in + 0.001 * grads_in * grads_in
    first_hat = first_new / (1.0 - 0.9**STEP)
    second_hat = second_new / (1.0 - 0.999**STEP)
    return (
        first_new,
        second_new,
        params_in - adam_rate * first_hat / (jnp.sqrt(second_hat) + 1e-08),
    )


def local(
    tokens_in,
    lm_grad,
    lm_logprob,
    targets,
    neighbor_ids,
    nearby_entry_gaps,
    seq_lengths,
    attn_weights,
    ffn_weights,
    attn_left,
    attn_right,
    ffn_left,
    ffn_right,
    attn_left_root,
    attn_right_root,
    ffn_left_root,
    ffn_right_root,
    norm_params,
    norm_moment1,
    norm_moment2,
    blending_coefficients,
    knn_moment1,
    knn_moment2,
):
    local_rows = tokens_in.shape[0]
    group_rows = local_rows * lax.axis_size("tensor")
    block_rows = SHORT
    score_scale = HEAD_DIM ** (-0.5)
    attn_full, ffn_full = (
        lax.all_gather(attn_weights.astype(jnp.bfloat16), "dp", axis=1, tiled=True),
        lax.all_gather(ffn_weights.astype(jnp.bfloat16), "dp", axis=1, tiled=True),
    )
    proj_in = jnp.concatenate([attn_full[0], attn_full[1], attn_full[2]], axis=1)
    proj_out = attn_full[3]
    head_cols = proj_out.shape[1]
    head_count = head_cols // HEAD_DIM
    first_block = first_blocks(seq_lengths, group_rows, block_rows)
    resid = tokens_in.astype(jnp.float32)
    normed1, norm1_back = jax.vjp(layer_norm, resid, norm_params[0], norm_params[1])
    normed1_low = normed1.astype(jnp.bfloat16)
    normed1_all = spread_rows(normed1_low)
    qkv_low = jnp.dot(normed1_all, proj_in, preferred_element_type=jnp.float32).astype(jnp.bfloat16)
    query_all = qkv_low[:, :head_cols].reshape(group_rows, head_count, HEAD_DIM)
    key_all = qkv_low[:, head_cols : 2 * head_cols].reshape(group_rows, head_count, HEAD_DIM)
    value_all = qkv_low[:, 2 * head_cols :].reshape(group_rows, head_count, HEAD_DIM)
    heads_out, log_masses = attend_forward(
        query_all, key_all, value_all, first_block, block_rows, score_scale
    )
    heads_flat = heads_out.reshape(group_rows, head_cols)
    attn_out = branch_total(heads_flat, proj_out)
    middle = resid + attn_out
    normed2, norm2_back = jax.vjp(layer_norm, middle, norm_params[2], norm_params[3])
    normed2_low = normed2.astype(jnp.bfloat16)
    w_up = ffn_full[0]
    w_down = ffn_full[1]
    normed2_all = spread_rows(normed2_low)
    hidden_pre = jnp.dot(normed2_all, w_up, preferred_element_type=jnp.float32)
    hidden_act, gelu_back = jax.vjp(gelu_tanh, hidden_pre)
    act_low = hidden_act.astype(jnp.bfloat16)
    ffn_out = branch_total(act_low, w_down)
    mixed = (middle + ffn_out).astype(jnp.bfloat16)
    sharpness_divisor = jnp.exp(blending_coefficients[0])
    interp = jax.nn.sigmoid(blending_coefficients[1])
    nearby_entry_logits = -nearby_entry_gaps / sharpness_divisor
    near_top = jnp.max(nearby_entry_logits, axis=1, keepdims=True)
    near_exp = jnp.exp(nearby_entry_logits - near_top)
    nearby_entry_shares = near_exp / jnp.sum(near_exp, axis=1, keepdims=True)
    target_matches = (neighbor_ids == targets[:, None]).astype(jnp.float32)
    retrieval_probability = jnp.sum(nearby_entry_shares * target_matches, axis=1)
    lm_prob = jnp.exp(lm_logprob)
    mixture = interp * retrieval_probability + (1.0 - interp) * lm_prob
    token_loss = -jnp.log(mixture)
    lm_weight = -(1.0 - interp) * lm_prob / mixture
    temp_terms = (
        jnp.sum(
            nearby_entry_shares
            * (target_matches - retrieval_probability[:, None])
            * nearby_entry_gaps,
            axis=1,
        )
        / sharpness_divisor
    )
    temp_grad = jnp.sum(-(interp / mixture) * temp_terms)
    interp_grad = jnp.sum(-interp * (1.0 - interp) * (retrieval_probability - lm_prob) / mixture)
    knn_grads = jnp.stack([temp_grad, interp_grad])
    cotangent = lm_weight[:, None] * lm_grad.astype(jnp.float32)
    cot_all = spread_grads(cotangent.astype(jnp.bfloat16))
    grad_act = jnp.dot(cot_all, w_down, preferred_element_type=jnp.float32)
    grad_pre_low = gelu_back(grad_act)[0].astype(jnp.bfloat16)
    normed2_used = spread_again(normed2_low)
    grad_up = jnp.einsum(
        "rd,rf->df", normed2_used, grad_pre_low, preferred_element_type=jnp.float32
    )
    grad_down = jnp.einsum("rd,rf->df", cot_all, act_low, preferred_element_type=jnp.float32)
    ffn_local = jnp.stack([grad_up, grad_down])
    grad_normed2 = input_total(grad_pre_low, w_up)
    mid_norm_grad, gain2_grad, shift2_grad = norm2_back(grad_normed2)
    grad_middle = cotangent + mid_norm_grad
    grad_mid_all = spread_grads(grad_middle.astype(jnp.bfloat16))
    grad_heads = jnp.dot(grad_mid_all, proj_out, preferred_element_type=jnp.float32).astype(
        jnp.bfloat16
    )
    grad_out_proj = jnp.einsum(
        "rd,rc->dc", grad_mid_all, heads_flat, preferred_element_type=jnp.float32
    )
    grad_keys, grad_values, grad_query = attend_backward(
        query_all,
        key_all,
        value_all,
        grad_heads.reshape(group_rows, head_count, HEAD_DIM),
        log_masses,
        first_block,
        block_rows,
        score_scale,
    )
    grad_qkv = jnp.concatenate(
        [
            grad_query.reshape(group_rows, head_cols),
            grad_keys.reshape(group_rows, head_cols),
            grad_values.reshape(group_rows, head_cols),
        ],
        axis=1,
    ).astype(jnp.bfloat16)
    normed1_used = spread_again(normed1_low)
    grad_proj_in = jnp.einsum(
        "rd,rc->dc", normed1_used, grad_qkv, preferred_element_type=jnp.float32
    )
    grad_normed1 = input_total(grad_qkv, proj_in)
    res_norm_grad, gain1_grad, bias_first_cotangent = norm1_back(grad_normed1)
    input_grad = grad_middle + res_norm_grad
    norm_grads = jnp.stack([gain1_grad, bias_first_cotangent, gain2_grad, shift2_grad])
    norm_total, knn_total, loss_total = lax.psum(
        (norm_grads, knn_grads, jnp.sum(token_loss)), ("dp", "tensor")
    )
    token_count = group_rows * lax.axis_size("dp")
    attn_local = jnp.stack(
        [
            grad_proj_in[:, :head_cols],
            grad_proj_in[:, head_cols : 2 * head_cols],
            grad_proj_in[:, 2 * head_cols :],
            grad_out_proj,
        ]
    )
    attn_grad, ffn_grad = (
        lax.psum_scatter(attn_local, "dp", scatter_dimension=1, tiled=True),
        lax.psum_scatter(ffn_local, "dp", scatter_dimension=1, tiled=True),
    )
    attn_rows, ffn_rows = (
        lax.all_gather(attn_grad.astype(jnp.bfloat16), "tensor", axis=2, tiled=True).astype(
            attn_grad.dtype
        ),
        lax.all_gather(ffn_grad.astype(jnp.bfloat16), "tensor", axis=2, tiled=True).astype(
            ffn_grad.dtype
        ),
    )
    attn_right_sum, ffn_right_sum = right_statistics(attn_grad, ffn_grad, attn_rows, ffn_rows)
    attn_turned = jnp.einsum(
        "sri,sij->srj", attn_rows, attn_right_root, precision=lax.Precision.HIGHEST
    )
    ffn_turned = jnp.einsum(
        "sri,sij->srj", ffn_rows, ffn_right_root, precision=lax.Precision.HIGHEST
    )
    attn_cols, ffn_cols, attn_turned_cols, ffn_turned_cols = (
        lax.all_gather(attn_grad.astype(jnp.bfloat16), "dp", axis=1, tiled=True).astype(
            attn_grad.dtype
        ),
        lax.all_gather(ffn_grad.astype(jnp.bfloat16), "dp", axis=1, tiled=True).astype(
            ffn_grad.dtype
        ),
        lax.all_gather(attn_turned.astype(jnp.bfloat16), "dp", axis=1, tiled=True).astype(
            attn_turned.dtype
        ),
        lax.all_gather(ffn_turned.astype(jnp.bfloat16), "dp", axis=1, tiled=True).astype(
            ffn_turned.dtype
        ),
    )
    attn_left_sum, ffn_left_sum = left_statistics(attn_grad, ffn_grad, attn_cols, ffn_cols)
    attn_update = jnp.einsum(
        "srq,sqi->sri", attn_left_root, attn_turned_cols, precision=lax.Precision.HIGHEST
    )
    ffn_update = jnp.einsum(
        "srq,sqi->sri", ffn_left_root, ffn_turned_cols, precision=lax.Precision.HIGHEST
    )
    attn_left_new = 0.5 * attn_left + 0.5 * attn_left_sum
    attn_right_new = 0.5 * attn_right + 0.5 * attn_right_sum
    ffn_left_new = 0.5 * ffn_left + 0.5 * ffn_left_sum
    ffn_right_new = 0.5 * ffn_right + 0.5 * ffn_right_sum
    attn_new = attn_weights - shampoo_rate * (attn_update + shampoo_decay * attn_weights)
    ffn_new = ffn_weights - shampoo_rate * (ffn_update + shampoo_decay * ffn_weights)
    norm_m1, norm_m2, norm_new = adamw_step(norm_params, norm_total, norm_moment1, norm_moment2)
    knn_m1, knn_m2, knn_new = adamw_step(blending_coefficients, knn_total, knn_moment1, knn_moment2)
    return (
        mixed,
        input_grad,
        loss_total / token_count,
        attn_grad,
        attn_left_new,
        attn_right_new,
        attn_new,
        ffn_grad,
        ffn_left_new,
        ffn_right_new,
        ffn_new,
        norm_m1,
        norm_m2,
        norm_new,
        knn_m1,
        knn_m2,
        knn_new,
    )


LINE_BIT, HALF_BIT, CORE_BIT, X_BIT, Y_BIT = 1, 2, 4, 8, 16


def send_by(values_in, target):
    return lax.ppermute(values_in, ("dp", "tensor"), [(index, target(index)) for index in range(32)])


def flip(values_in, mask):
    return send_by(values_in, lambda index: index ^ mask)


def moves(index):
    return ((index >> 2) ^ (index >> 1)) & 1 == 1


def swapped(index):
    return index ^ (CORE_BIT | HALF_BIT) if moves(index) else index


def swap_core_half(values_in):
    return send_by(values_in, swapped)


def swap_or_near(values_in):
    return send_by(
        values_in, lambda index: swapped(index) if moves(index) else index ^ LINE_BIT
    )


def near_of_moved(values_in):
    pairs = [(index, index ^ LINE_BIT) for index in range(32) if moves(index)]
    return lax.ppermute(values_in, ("dp", "tensor"), pairs)


def cross_one(values_in):
    return send_by(values_in, lambda index: index ^ (Y_BIT if index & CORE_BIT else X_BIT))


def cross_two(values_in):
    return send_by(values_in, lambda index: index ^ (X_BIT if index & CORE_BIT else Y_BIT))


def pick(values_in, index, axis):
    return lax.dynamic_index_in_dim(values_in, index, axis, keepdims=False)


def ordered_pair(own, other, bit, axis):
    return jnp.where(
        bit == 0, jnp.stack([own, other], axis=axis), jnp.stack([other, own], axis=axis)
    )


def together(*values_in):
    return lax.optimization_barrier(values_in)


def by_chip(values_in, chip):
    width = values_in.shape[-1] // 4
    return jnp.concatenate(
        [
            lax.dynamic_slice_in_dim(values_in, (chip ^ block) * width, width, values_in.ndim - 1)
            for block in range(4)
        ],
        axis=-1,
    )


def add_far(pair):
    return jnp.concatenate([pair, flip(pair, CORE_BIT)], axis=0)


def weight_core(local_low, place):
    width = local_low.shape[2] // 2
    mine = lax.dynamic_slice_in_dim(local_low, place["core"] * width, width, 2)
    theirs = lax.dynamic_slice_in_dim(local_low, (1 - place["core"]) * width, width, 2)
    both = ordered_pair(mine, flip(theirs, CORE_BIT), place["core"], 1)
    return both.reshape(local_low.shape[0], 2 * local_low.shape[1], width)


def weight_halves(own, other, place):
    return jnp.where(
        place["half"] == 0,
        jnp.concatenate([own, other], axis=2),
        jnp.concatenate([other, own], axis=2),
    )


def by_core(core, own, other, axis):
    return jnp.where(
        core == 0,
        jnp.concatenate([own, other], axis=axis),
        jnp.concatenate([other, own], axis=axis),
    )


def by_rel(core, own, first, pair, axis):
    middle = jnp.where(
        core == 0,
        jnp.concatenate([first, pair[0]], axis=axis),
        jnp.concatenate([pair[0], first], axis=axis),
    )
    return jnp.concatenate([own, middle, pair[1]], axis=axis)


def scatter_parts(core, partials):
    parts = [partial.reshape(2, 2, -1, partial.shape[1]) for partial in partials]
    kept = [jnp.where(core == 0, part[:, 0], part[0]) for part in parts]
    sent = [jnp.where(core == 0, part[:, 1], part[1]) for part in parts]
    return jnp.stack(kept), jnp.stack(sent)


def add_low(left_part, right_part):
    return (left_part.astype(jnp.float32) + right_part.astype(jnp.float32)).astype(jnp.bfloat16)


def dot32(spec, left_mat, right_mat):
    return jnp.einsum(spec, left_mat, right_mat, preferred_element_type=jnp.float32)


def update_kernel(
    info_ref, left_ref, line_ref, first_ref, pair_ref, root_ref, own_ref, sent_ref, update_acc, gram_acc
):
    step = pl.program_id(1)
    steps = pl.num_programs(1)
    chip, core, tensor = info_ref[0], info_ref[1], info_ref[2]
    block = left_ref.shape[2] // 4
    own_rows = block // 2
    cols = update_acc.shape[1]

    @pl.when(step == 0)
    def _():
        update_acc[...] = jnp.zeros_like(update_acc)
        gram_acc[...] = jnp.zeros_like(gram_acc)

    pieces = (
        lambda: line_ref[0, 0],
        lambda: first_ref[0, 0],
        lambda: pair_ref[0, 0, 0],
        lambda: pair_ref[1, 0, 0],
    )
    rels = (0, 1 + core, 2 - core, 3)
    turned = None
    for rel, piece in zip(rels, pieces):
        start = pl.multiple_of((chip ^ rel) * block, block)
        part = jnp.dot(
            left_ref[0, :, pl.ds(start, block)], piece(), preferred_element_type=jnp.float32
        )
        turned = part if turned is None else turned + part

        @pl.when((chip ^ tensor) == rel)
        def _(piece=piece):
            gram_acc[...] += lax.dot_general(
                pieces[0](), piece(), (((1,), (1,)), ((), ())), preferred_element_type=jnp.float32
            )

    root = root_ref[...].reshape(-1, cols).astype(jnp.bfloat16)
    update_acc[...] += jnp.dot(
        turned.astype(jnp.bfloat16), root, preferred_element_type=jnp.float32
    )

    @pl.when(step == steps - 1)
    def _():
        own_ref[0, :, :cols] = update_acc[:own_rows]
        sent_ref[0, :, :cols] = update_acc[own_rows:].astype(jnp.bfloat16)
        gram_own = gram_acc[pl.ds(pl.multiple_of(core * own_rows, own_rows), own_rows), :]
        gram_sent = gram_acc[pl.ds(pl.multiple_of((1 - core) * own_rows, own_rows), own_rows), :]
        own_ref[0, :, cols:] = gram_own
        sent_ref[0, :, cols:] = gram_sent.astype(jnp.bfloat16)


def updates(info, left_low, pieces, root, split):
    line, first, pair = pieces
    _, lead, rows, width = line.shape
    count = lead // 2 if split else lead
    cols = root.shape[2]
    root_rows = root.shape[1] // 8
    root = root.reshape(root.shape[0], 2, 2, 2, root_rows, cols)
    if split:
        steps = 4
        root_spec = pl.BlockSpec(
            (1, 1, 1, 1, root_rows, cols),
            lambda m, k, info_ref: (m, k & 1, info_ref[3] ^ (k >> 1), info_ref[1], 0, 0),
        )
    else:
        steps = 2
        root_spec = pl.BlockSpec(
            (1, 2, 1, 1, root_rows, cols),
            lambda m, k, info_ref: (m, 0, info_ref[3] ^ k, info_ref[1], 0, 0),
        )

    def place_of(m, k):
        return (k >> 1, 2 * m + (k & 1)) if split else (k, m)

    out_shape = (count, rows // 2, cols + rows)
    out_spec = pl.BlockSpec((1, rows // 2, cols + rows), lambda m, k, info_ref: (m, 0, 0))
    piece_spec = pl.BlockSpec(
        (1, 1, rows, width), lambda m, k, info_ref: place_of(m, k) + (0, 0)
    )
    return pl.pallas_call(
        update_kernel,
        grid_spec=pltpu.PrefetchScalarGridSpec(
            num_scalar_prefetch=1,
            grid=(count, steps),
            in_specs=[
                pl.BlockSpec((1, rows, 4 * rows), lambda m, k, info_ref: (m, 0, 0)),
                piece_spec,
                piece_spec,
                pl.BlockSpec(
                    (2, 1, 1, rows, width), lambda m, k, info_ref: (0,) + place_of(m, k) + (0, 0)
                ),
                root_spec,
            ],
            out_specs=[out_spec, out_spec],
            scratch_shapes=[
                pltpu.VMEM((rows, cols), jnp.float32),
                pltpu.VMEM((rows, rows), jnp.float32),
            ],
        ),
        out_shape=(
            jax.ShapeDtypeStruct(out_shape, jnp.float32),
            jax.ShapeDtypeStruct(out_shape, jnp.bfloat16),
        ),
        compiler_params=pltpu.CompilerParams(vmem_limit_bytes=48 * 1024 * 1024),
        cost_estimate=pl.CostEstimate(flops=1_000_000, bytes_accessed=100_000, transcendentals=0),
    )(info, left_low, line, first, pair, root)


def column_block(pieces, line_rel, half, split, core):
    line, first, pair = pieces

    def cut(piece):
        piece = piece[0] if line_rel is None else pick(piece, line_rel, 0)
        if split:
            return pick(piece.reshape(-1, 2, *piece.shape[1:]), half, 1)
        width = piece.shape[2] // 2
        return lax.dynamic_slice_in_dim(piece, half * width, width, 2)

    return by_rel(core, cut(line), cut(first), (cut(pair[0]), cut(pair[1])), 1)


def right_kernel(
    info_ref,
    line_t,
    first_t,
    pair_t,
    line_c,
    first_c,
    pair_c,
    other_ref,
    right_in_ref,
    right_ref,
    grad_ref,
):
    core = info_ref[1]
    half = other_ref.shape[2]
    chip_rows = other_ref.shape[1] // 4
    own_rows = chip_rows // 2
    own = (line_t[0, 0], first_t[0, 0], pair_t[0, 0, 0], pair_t[1, 0, 0])
    cols = (line_c[0, 0], first_c[0, 0], pair_c[0, 0, 0], pair_c[1, 0, 0])
    rels = (0, 1 + core, 2 - core, 3)
    sums = [None, None]
    for rel, own_piece, col_piece in zip(rels, own, cols):
        other_piece = other_ref[0, pl.ds(pl.multiple_of(rel * chip_rows, chip_rows), chip_rows), :]
        for at, piece in enumerate((own_piece, other_piece)):
            part = lax.dot_general(
                piece, col_piece, (((0,), (0,)), ((), ())), preferred_element_type=jnp.float32
            )
            sums[at] = part if sums[at] is None else sums[at] + part
    row = pl.ds(pl.multiple_of(core * own_rows, own_rows), own_rows)
    grads = (line_t[0, 0, row, :], other_ref[0, row, :])
    for at in range(2):
        block = core if at == 0 else 1 - core
        rows = pl.ds(pl.multiple_of(block * half, half), half)
        right_ref[0, rows, :] = 0.5 * right_in_ref[0, rows, :] + 0.5 * sums[at]
        grad_ref[0, :, rows] = grads[at].astype(jnp.float32)


def right_statistics_new(info, pieces, other_cols, right_in, own_rows, split):
    line, first, pair = pieces
    _, lead, rows, width = line.shape
    count = right_in.shape[0]
    half = other_cols.shape[2]
    cols = right_in.shape[2]
    if split:

        def own(m, info_ref):
            return (0, 2 * m + info_ref[4], 0, 0)

        def col(m, info_ref):
            return (info_ref[5], 2 * m + info_ref[6], 0, 0)

    else:

        def own(m, info_ref):
            return (0, m, 0, info_ref[4])

        def col(m, info_ref):
            return (info_ref[5], m, 0, info_ref[6])

    def specs(place_of):
        one = pl.BlockSpec((1, 1, rows, half), place_of)
        two = pl.BlockSpec((2, 1, 1, rows, half), lambda m, info_ref: (0,) + place_of(m, info_ref))
        return [one, one, two]

    return pl.pallas_call(
        right_kernel,
        grid_spec=pltpu.PrefetchScalarGridSpec(
            num_scalar_prefetch=1,
            grid=(count,),
            in_specs=specs(own)
            + specs(col)
            + [
                pl.BlockSpec((1, 4 * rows, half), lambda m, info_ref: (m, 0, 0)),
                pl.BlockSpec((1, 2 * half, cols), lambda m, info_ref: (m, 0, 0)),
            ],
            out_specs=[
                pl.BlockSpec((1, 2 * half, cols), lambda m, info_ref: (m, 0, 0)),
                pl.BlockSpec((1, own_rows, 2 * half), lambda m, info_ref: (m, 0, 0)),
            ],
        ),
        out_shape=(
            jax.ShapeDtypeStruct(right_in.shape, jnp.float32),
            jax.ShapeDtypeStruct((count, own_rows, 2 * half), jnp.float32),
        ),
        compiler_params=pltpu.CompilerParams(vmem_limit_bytes=48 * 1024 * 1024),
        cost_estimate=pl.CostEstimate(flops=1_000_000, bytes_accessed=100_000, transcendentals=0),
    )(info, line, first, pair, line, first, pair, other_cols, right_in)


def shampoo_left(own, received, left_in, weights_in):
    total = own + received.astype(jnp.float32)
    cols = weights_in.shape[2]
    return (
        0.5 * left_in + 0.5 * total[:, :, cols:],
        weights_in - shampoo_rate * (total[:, :, :cols] + shampoo_decay * weights_in),
    )


def halve_kernel(info_ref, weights_ref, mine_ref, theirs_ref):
    core = info_ref[1]
    width = mine_ref.shape[2]
    mine = pl.ds(pl.multiple_of(core * width, width), width)
    theirs = pl.ds(pl.multiple_of((1 - core) * width, width), width)
    mine_ref[...] = weights_ref[:, :, mine].astype(mine_ref.dtype)
    theirs_ref[...] = weights_ref[:, :, theirs].astype(theirs_ref.dtype)


def halve(where, weights):
    count, rows, width = weights.shape
    shape = jax.ShapeDtypeStruct((count, rows, width // 2), jnp.bfloat16)
    return pl.pallas_call(
        halve_kernel,
        grid_spec=pltpu.PrefetchScalarGridSpec(
            num_scalar_prefetch=1,
            grid=(1,),
            in_specs=[pl.BlockSpec(weights.shape, lambda step, info_ref: (0, 0, 0))],
            out_specs=[pl.BlockSpec(shape.shape, lambda step, info_ref: (0, 0, 0))] * 2,
        ),
        out_shape=(shape, shape),
        compiler_params=pltpu.CompilerParams(vmem_limit_bytes=32 * 1024 * 1024),
        cost_estimate=pl.CostEstimate(flops=1_000_000, bytes_accessed=100_000, transcendentals=0),
    )(where, weights)


def unite_kernel(info_ref, mine_ref, other_ref, out_ref):
    core = info_ref[1]
    rows = mine_ref.shape[1]
    out_ref[:, pl.ds(pl.multiple_of(core * rows, rows), rows), :] = mine_ref[...]
    out_ref[:, pl.ds(pl.multiple_of((1 - core) * rows, rows), rows), :] = other_ref[...]


def unite(where, mine, other):
    count, rows, width = mine.shape
    spec = pl.BlockSpec(mine.shape, lambda step, info_ref: (0, 0, 0))
    out = (count, 2 * rows, width)
    return pl.pallas_call(
        unite_kernel,
        grid_spec=pltpu.PrefetchScalarGridSpec(
            num_scalar_prefetch=1,
            grid=(1,),
            in_specs=[spec, spec],
            out_specs=pl.BlockSpec(out, lambda step, info_ref: (0, 0, 0)),
        ),
        out_shape=jax.ShapeDtypeStruct(out, mine.dtype),
        compiler_params=pltpu.CompilerParams(vmem_limit_bytes=32 * 1024 * 1024),
        cost_estimate=pl.CostEstimate(flops=1_000_000, bytes_accessed=100_000, transcendentals=0),
    )(where, mine, other)


def knn_kernel(
    info_ref, blend_ref, gaps_ref, ids_ref, targets_ref, logprob_ref, lm_ref, cot_ref, sums_ref
):
    step = pl.program_id(0)
    chip = info_ref[0]
    log_temperature = blend_ref[0:1, 0:1]
    sharpness_divisor = jnp.exp(log_temperature)
    interp = 1.0 / (1.0 + jnp.exp(-blend_ref[0:1, 1:2]))
    gaps = gaps_ref[...]
    logits = -gaps / sharpness_divisor
    near_exp = jnp.exp(logits - jnp.max(logits, axis=1, keepdims=True))
    mass = jnp.sum(near_exp, axis=1, keepdims=True)
    hits = ids_ref[...] == targets_ref[...]
    hit_exp = jnp.where(hits, near_exp, 0.0)
    retrieval = jnp.sum(hit_exp, axis=1, keepdims=True) / mass
    hit_gaps = jnp.sum(hit_exp * gaps, axis=1, keepdims=True) / mass
    all_gaps = jnp.sum(near_exp * gaps, axis=1, keepdims=True) / mass
    temp_terms = (hit_gaps - retrieval * all_gaps) / sharpness_divisor
    lm_prob = jnp.exp(logprob_ref[...])
    mixture = interp * retrieval + (1.0 - interp) * lm_prob
    lm_weight = -(1.0 - interp) * lm_prob / mixture
    temp_grad = jnp.sum(-(interp / mixture) * temp_terms, axis=0, keepdims=True)
    interp_grad = jnp.sum(
        -interp * (1.0 - interp) * (retrieval - lm_prob) / mixture, axis=0, keepdims=True
    )
    loss = jnp.sum(-jnp.log(mixture), axis=0, keepdims=True)
    lane = lax.broadcasted_iota(jnp.int32, sums_ref.shape, 1)
    sums = jnp.where(lane == 0, temp_grad, jnp.where(lane == 1, interp_grad, 0.0))
    sums = jnp.where(lane == 2, loss, sums)

    @pl.when(step == 0)
    def _():
        sums_ref[...] = jnp.zeros_like(sums_ref)

    sums_ref[...] += sums
    block = lm_ref.shape[1] // 4
    for rel in range(4):
        start = pl.multiple_of((chip ^ rel) * block, block)
        part = lm_weight * lm_ref[:, pl.ds(start, block)].astype(jnp.float32)
        cot_ref[:, rel * block : (rel + 1) * block] = part.astype(cot_ref.dtype)


def neighbours(where, blend, gaps, ids, targets, logprob, lm_grad):
    rows, width = gaps.shape
    step_rows = rows // 3
    wide = pl.BlockSpec((step_rows, width), lambda r, info_ref: (r, 0))
    thin = pl.BlockSpec((step_rows, 1), lambda r, info_ref: (r, 0))
    cot, sums = pl.pallas_call(
        knn_kernel,
        grid_spec=pltpu.PrefetchScalarGridSpec(
            num_scalar_prefetch=1,
            grid=(3,),
            in_specs=[
                pl.BlockSpec((1, 2), lambda r, info_ref: (0, 0)),
                wide,
                wide,
                thin,
                thin,
                wide,
            ],
            out_specs=[wide, pl.BlockSpec((8, width), lambda r, info_ref: (0, 0))],
        ),
        out_shape=(
            jax.ShapeDtypeStruct((rows, width), jnp.bfloat16),
            jax.ShapeDtypeStruct((8, width), jnp.float32),
        ),
        compiler_params=pltpu.CompilerParams(vmem_limit_bytes=32 * 1024 * 1024),
        cost_estimate=pl.CostEstimate(flops=1_000_000, bytes_accessed=100_000, transcendentals=0),
    )(where, blend[None], gaps, ids, targets[:, None], logprob[:, None], lm_grad)
    return cot, sums[:1]


def normalize_kernel(info_ref, pair_ref, far_ref, params_ref, out_ref, own_ref):
    step = pl.program_id(0)
    chip = info_ref[0]
    block = out_ref.shape[1] // 4

    def work(rows_ref):
        values_in = rows_ref[...].astype(jnp.float32)
        centre = jnp.mean(values_in, axis=-1, keepdims=True)
        spread_sq = jnp.mean((values_in - centre) ** 2, axis=-1, keepdims=True)
        scale = lax.rsqrt(spread_sq + norm_eps)
        for rel in range(4):
            start = pl.multiple_of((chip ^ rel) * block, block)
            own = slice(rel * block, (rel + 1) * block)
            part = rows_ref[:, pl.ds(start, block)].astype(jnp.float32)
            normed = (part - centre) * scale * params_ref[0:1, own] + params_ref[1:2, own]
            out_ref[:, own] = normed.astype(out_ref.dtype)

    @pl.when(step < 2)
    def _():
        work(pair_ref)

    @pl.when(step >= 2)
    def _():
        work(far_ref)

    @pl.when(step == 0)
    def _():
        for rel in range(4):
            start = pl.multiple_of((chip ^ rel) * block, block)
            own_ref[:, rel * block : (rel + 1) * block] = pair_ref[:, pl.ds(start, block)]


def normalize(where, pair, far, params):
    rows, width = pair.shape
    step_rows = rows // 2
    pair_spec = pl.BlockSpec((step_rows, width), lambda r, info_ref: (jnp.minimum(r, 1), 0))
    far_spec = pl.BlockSpec((step_rows, width), lambda r, info_ref: (jnp.maximum(r - 2, 0), 0))
    return pl.pallas_call(
        normalize_kernel,
        grid_spec=pltpu.PrefetchScalarGridSpec(
            num_scalar_prefetch=1,
            grid=(4,),
            in_specs=[
                pair_spec,
                far_spec,
                pl.BlockSpec(params.shape, lambda r, info_ref: (0, 0)),
            ],
            out_specs=[
                pl.BlockSpec((step_rows, width), lambda r, info_ref: (r, 0)),
                pl.BlockSpec((step_rows, width), lambda r, info_ref: (0, 0)),
            ],
        ),
        out_shape=(
            jax.ShapeDtypeStruct((2 * rows, width), pair.dtype),
            jax.ShapeDtypeStruct((step_rows, width), pair.dtype),
        ),
        compiler_params=pltpu.CompilerParams(vmem_limit_bytes=32 * 1024 * 1024),
        cost_estimate=pl.CostEstimate(flops=1_000_000, bytes_accessed=100_000, transcendentals=0),
    )(where, pair, far, params)


def norm_back_kernel(
    info_ref, own_ref, near_ref, rows_ref, later_ref, gain_ref, out_ref, sums_ref
):
    chip = info_ref[0]
    grads = own_ref[...] + near_ref[...].astype(jnp.float32)
    values_in = rows_ref[...].astype(jnp.float32)
    centred = values_in - jnp.mean(values_in, axis=-1, keepdims=True)
    spread_sq = jnp.mean(centred * centred, axis=-1, keepdims=True)
    scale = lax.rsqrt(spread_sq + norm_eps)
    normed = centred * scale
    sums_ref[0:1, :] = jnp.sum(grads * normed, axis=0, keepdims=True)
    sums_ref[1:2, :] = jnp.sum(grads, axis=0, keepdims=True)
    sloped = grads * gain_ref[0:1, :]
    along = jnp.mean(sloped * normed, axis=-1, keepdims=True)
    back = (sloped - jnp.mean(sloped, axis=-1, keepdims=True) - normed * along) * scale
    result = (later_ref[...] + back).astype(out_ref.dtype)
    block = out_ref.shape[1] // 4
    for rel in range(4):
        start = pl.multiple_of((chip ^ rel) * block, block)
        out_ref[:, pl.ds(start, block)] = result[:, rel * block : (rel + 1) * block]


def norm_back(where, own, near, rows_low, later, gain):
    rows, width = own.shape

    def whole(shape):
        return pl.BlockSpec(shape, lambda step, info_ref: (0, 0))

    return pl.pallas_call(
        norm_back_kernel,
        grid_spec=pltpu.PrefetchScalarGridSpec(
            num_scalar_prefetch=1,
            grid=(1,),
            in_specs=[whole(own.shape)] * 4 + [whole((1, width))],
            out_specs=[whole(own.shape), whole((2, width))],
        ),
        out_shape=(
            jax.ShapeDtypeStruct((rows, width), jnp.bfloat16),
            jax.ShapeDtypeStruct((2, width), jnp.float32),
        ),
        compiler_params=pltpu.CompilerParams(vmem_limit_bytes=40 * 1024 * 1024),
        cost_estimate=pl.CostEstimate(flops=1_000_000, bytes_accessed=100_000, transcendentals=0),
    )(where, own, near, rows_low, later, gain)


def ffn_kernel(normed_a, normed_b, cot_a, cot_b, up_ref, down_ref, act_ref, grad_ref):
    def work(normed_ref, cot_ref):
        pre = jnp.dot(normed_ref[...], up_ref[...], preferred_element_type=jnp.float32)
        grad_act = jnp.dot(cot_ref[...], down_ref[...], preferred_element_type=jnp.float32)
        scale = 0.7978845608028654
        square = pre * pre
        turn = jnp.tanh(pre * (scale + (scale * 0.044715) * square))
        gate = 0.5 + 0.5 * turn
        act_ref[...] = (pre * gate).astype(jnp.bfloat16)
        slope = gate + 0.5 * pre * (1.0 - turn * turn) * (scale + (3.0 * scale * 0.044715) * square)
        grad_ref[...] = (grad_act * slope).astype(jnp.bfloat16)

    @pl.when(pl.program_id(1) < 2)
    def _():
        work(normed_a, cot_a)

    @pl.when(pl.program_id(1) >= 2)
    def _():
        work(normed_b, cot_b)


def ffn_middle(normed, cot, w_up, w_down):
    rows, width = normed[0].shape
    hidden = w_up.shape[1]
    step_rows, step_cols = rows // 2, hidden // 2
    pair_spec = pl.BlockSpec((step_rows, width), lambda f, r: (jnp.minimum(r, 1), 0))
    far_spec = pl.BlockSpec((step_rows, width), lambda f, r: (jnp.maximum(r - 2, 0), 0))
    col_spec = pl.BlockSpec((width, step_cols), lambda f, r: (0, f))
    out_spec = pl.BlockSpec((step_rows, step_cols), lambda f, r: (r, f))
    shape = jax.ShapeDtypeStruct((2 * rows, hidden), jnp.bfloat16)
    return pl.pallas_call(
        ffn_kernel,
        grid=(2, 4),
        in_specs=[pair_spec, far_spec, pair_spec, far_spec, col_spec, col_spec],
        out_specs=[out_spec, out_spec],
        out_shape=(shape, shape),
        compiler_params=pltpu.CompilerParams(vmem_limit_bytes=48 * 1024 * 1024),
        cost_estimate=pl.CostEstimate(flops=1_000_000, bytes_accessed=100_000, transcendentals=0),
    )(*normed, *cot, w_up, w_down)


def masked_heads(values_in, lanes, head, scale):
    keep = (lanes >= head * HEAD_DIM) & (lanes < (head + 1) * HEAD_DIM)
    return jnp.where(keep, values_in * scale, jnp.zeros_like(values_in))


def in_order(info_ref, source, held, rows):
    for piece in range(4):
        start = pl.multiple_of((info_ref[0] ^ piece) * rows, rows)
        held[piece * rows : (piece + 1) * rows, :] = source(pl.ds(start, rows))


def out_of_order(info_ref, held, store, rows):
    for piece in range(4):
        start = pl.multiple_of((info_ref[0] ^ piece) * rows, rows)
        store(pl.ds(start, rows), held[piece * rows : (piece + 1) * rows, :])


def block_bias(info_ref, query, key):
    return jnp.where(info_ref[1 + query] <= key * SHORT, 0.0, -1e30).astype(jnp.float32)


def forward_kernel(info_ref, qkv_ref, out_ref, query_held, key_held, value_held, out_held):
    rows = qkv_ref.shape[1] // 4
    for part, held in enumerate((query_held, key_held, value_held)):
        in_order(info_ref, lambda at, part=part: qkv_ref[part, at, :], held, rows)
    lanes = lax.broadcasted_iota(jnp.int32, (SHORT, 128), 1)
    earlier = lax.broadcasted_iota(jnp.int32, (SHORT, SHORT), 1) <= lax.broadcasted_iota(
        jnp.int32, (SHORT, SHORT), 0
    )
    for query in range(qkv_ref.shape[1] // SHORT):
        query_rows = query_held[query * SHORT : (query + 1) * SHORT, :]
        outs = []
        for head in range(2):
            query_head = masked_heads(query_rows, lanes, head, HEAD_DIM**-0.5)
            scores, biases = [], []
            for key in range(query + 1):
                score = lax.dot_general(
                    query_head,
                    key_held[key * SHORT : (key + 1) * SHORT, :],
                    (((1,), (1,)), ((), ())),
                    preferred_element_type=jnp.float32,
                )
                scores.append(jnp.where(earlier, score, -1e30) if key == query else score)
                biases.append(block_bias(info_ref, query, key))
            top = scores[query].max(axis=1, keepdims=True)
            for score, bias in zip(scores[:query], biases):
                top = jnp.maximum(top, score.max(axis=1, keepdims=True) + bias)
            mass = jnp.zeros_like(top)
            total = jnp.zeros((SHORT, 128), jnp.float32)
            for key in range(query + 1):
                chance = jnp.exp(scores[key] - (top - biases[key]))
                mass = mass + chance.sum(axis=1, keepdims=True)
                total = total + jnp.dot(
                    chance.astype(jnp.bfloat16),
                    value_held[key * SHORT : (key + 1) * SHORT, :],
                    preferred_element_type=jnp.float32,
                )
            outs.append(total / mass)
        out = jnp.where(lanes < HEAD_DIM, outs[0], outs[1])
        out_held[query * SHORT : (query + 1) * SHORT, :] = out.astype(jnp.bfloat16)

    def store(at, values_in):
        out_ref[at, :] = values_in

    out_of_order(info_ref, out_held, store, rows)


def backward_kernel(
    info_ref,
    qkv_ref,
    grad_ref,
    out_ref,
    query_held,
    key_held,
    value_held,
    grad_held,
    key_turned,
    query_grad,
    key_grad,
    value_grad,
):
    rows = qkv_ref.shape[1] // 4
    for part, held in enumerate((query_held, key_held, value_held)):
        in_order(info_ref, lambda at, part=part: qkv_ref[part, at, :], held, rows)
    in_order(info_ref, lambda at: grad_ref[at, :], grad_held, rows)
    key_turned[...] = key_held[...].astype(jnp.float32).T.astype(jnp.bfloat16)
    lanes = lax.broadcasted_iota(jnp.int32, (SHORT, 128), 1)
    earlier = lax.broadcasted_iota(jnp.int32, (SHORT, SHORT), 0) <= lax.broadcasted_iota(
        jnp.int32, (SHORT, SHORT), 1
    )
    blocks = qkv_ref.shape[1] // SHORT
    for query in range(blocks):
        at_query = slice(query * SHORT, (query + 1) * SHORT)
        query_rows = query_held[at_query, :]
        grad_rows = grad_held[at_query, :]
        turned_grads = []
        for head in range(2):
            query_head = masked_heads(query_rows, lanes, head, HEAD_DIM**-0.5)
            grad_head = masked_heads(grad_rows, lanes, head, 1.0)
            scores, biases = [], []
            for key in range(query + 1):
                score = lax.dot_general(
                    key_held[key * SHORT : (key + 1) * SHORT, :],
                    query_head,
                    (((1,), (1,)), ((), ())),
                    preferred_element_type=jnp.float32,
                )
                scores.append(jnp.where(earlier, score, -1e30) if key == query else score)
                biases.append(block_bias(info_ref, query, key))
            top = scores[query].max(axis=0, keepdims=True)
            for score, bias in zip(scores[:query], biases):
                top = jnp.maximum(top, score.max(axis=0, keepdims=True) + bias)
            mass = jnp.zeros_like(top)
            inner = jnp.zeros_like(top)
            chances, slopes = [], []
            for key in range(query + 1):
                slope = lax.dot_general(
                    value_held[key * SHORT : (key + 1) * SHORT, :],
                    grad_head,
                    (((1,), (1,)), ((), ())),
                    preferred_element_type=jnp.float32,
                )
                chance = jnp.exp(scores[key] - (top - biases[key]))
                mass = mass + chance.sum(axis=0, keepdims=True)
                inner = inner + (chance * slope).sum(axis=0, keepdims=True)
                chances.append(chance)
                slopes.append(slope)
            share = 1.0 / mass
            inner = inner * share
            total = None
            for key in range(query + 1):
                at_key = slice(key * SHORT, (key + 1) * SHORT)
                probs = chances[key] * share
                grad_scores = (probs * (slopes[key] - inner)).astype(jnp.bfloat16)
                value_part = jnp.dot(
                    probs.astype(jnp.bfloat16), grad_head, preferred_element_type=jnp.float32
                )
                key_part = jnp.dot(grad_scores, query_head, preferred_element_type=jnp.float32)
                if head == 0 and key == query:
                    value_grad[at_key, :] = value_part
                    key_grad[at_key, :] = key_part
                else:
                    value_grad[at_key, :] += value_part
                    key_grad[at_key, :] += key_part
                part = jnp.dot(
                    key_turned[head * HEAD_DIM : (head + 1) * HEAD_DIM, at_key],
                    grad_scores,
                    preferred_element_type=jnp.float32,
                )
                total = part if total is None else total + part
            turned_grads.append(total)
        turned = jnp.concatenate(turned_grads, axis=0)
        query_grad[at_query, :] = turned.T * (HEAD_DIM**-0.5)

    for part, held in enumerate((query_grad, key_grad, value_grad)):

        def store(at, values_in, part=part):
            out_ref[part, at, :] = values_in.astype(jnp.bfloat16)

        out_of_order(info_ref, held, store, rows)


def attend(info, qkv):
    _, rows, width = qkv.shape
    held = pltpu.VMEM((rows, 128), jnp.bfloat16)
    return pl.pallas_call(
        forward_kernel,
        grid_spec=pltpu.PrefetchScalarGridSpec(
            num_scalar_prefetch=1,
            grid=(width // 128,),
            in_specs=[pl.BlockSpec((3, rows, 128), lambda pair, info_ref: (0, 0, pair))],
            out_specs=pl.BlockSpec((rows, 128), lambda pair, info_ref: (0, pair)),
            scratch_shapes=[held] * 4,
        ),
        out_shape=jax.ShapeDtypeStruct((rows, width), jnp.bfloat16),
        compiler_params=pltpu.CompilerParams(vmem_limit_bytes=48 * 1024 * 1024),
        cost_estimate=pl.CostEstimate(flops=1_000_000, bytes_accessed=100_000, transcendentals=0),
    )(info, qkv)


def attend_back(info, qkv, grad_heads, pair, earlier):
    _, rows, width = qkv.shape
    extra = [] if earlier is None else [pl.BlockSpec(memory_space=pl.ANY)]

    def kernel(info_ref, qkv_ref, grad_ref, *others):
        backward_kernel(info_ref, qkv_ref, grad_ref, *others[len(extra) :])

    return pl.pallas_call(
        kernel,
        grid_spec=pltpu.PrefetchScalarGridSpec(
            num_scalar_prefetch=1,
            grid=(1,),
            in_specs=[
                pl.BlockSpec((3, rows, 128), lambda step, info_ref: (0, 0, pair)),
                pl.BlockSpec((rows, 128), lambda step, info_ref: (0, pair)),
            ]
            + extra,
            out_specs=pl.BlockSpec((3, rows, 128), lambda step, info_ref: (0, 0, pair)),
            scratch_shapes=[pltpu.VMEM((rows, 128), jnp.bfloat16)] * 4
            + [pltpu.VMEM((128, rows), jnp.bfloat16)]
            + [pltpu.VMEM((rows, 128), jnp.float32)] * 3,
        ),
        out_shape=jax.ShapeDtypeStruct(qkv.shape, jnp.bfloat16),
        input_output_aliases={} if earlier is None else {3: 0},
        compiler_params=pltpu.CompilerParams(vmem_limit_bytes=48 * 1024 * 1024),
        cost_estimate=pl.CostEstimate(flops=1_000_000, bytes_accessed=100_000, transcendentals=0),
    )(info, qkv, grad_heads, *([] if earlier is None else [earlier]))


def regrouped(
    tokens_in,
    lm_grad,
    lm_logprob,
    targets,
    neighbor_ids,
    nearby_entry_gaps,
    seq_lengths,
    attn_weights,
    ffn_weights,
    attn_left,
    attn_right,
    ffn_left,
    ffn_right,
    attn_left_root,
    attn_right_root,
    ffn_left_root,
    ffn_right_root,
    norm_params,
    norm_moment1,
    norm_moment2,
    blending_coefficients,
    knn_moment1,
    knn_moment2,
):
    low = jnp.bfloat16
    rows = tokens_in.shape[0]
    group_rows = 4 * rows
    dp_index, tensor_index = lax.axis_index("dp"), lax.axis_index("tensor")
    place = {
        "line": tensor_index & 1,
        "half": tensor_index >> 1,
        "core": dp_index & 1,
        "x": (dp_index >> 1) & 1,
        "y": dp_index >> 2,
        "chip": dp_index >> 1,
    }
    me = place["core"] * 2 + place["line"]
    chip, core = place["chip"], place["core"]
    staying = core == place["half"]

    where = jnp.stack(
        [
            chip,
            core,
            tensor_index,
            place["line"],
            place["half"],
            place["line"] ^ place["x"],
            place["y"],
        ]
    ).astype(jnp.int32)
    tokens_one = swap_or_near(tokens_in)
    wa_mine, wa_theirs = halve(where, attn_weights)
    wa = unite(where, wa_mine, flip(wa_theirs, CORE_BIT))
    wa, ffn_weights_in, nearby_entry_gaps, lengths_in = together(
        wa, ffn_weights, nearby_entry_gaps, seq_lengths
    )
    wa_other = flip(wa, HALF_BIT)
    wf_mine, wf_theirs = halve(where, ffn_weights_in)
    wf = unite(where, wf_mine, flip(wf_theirs, CORE_BIT))
    other_lengths = flip(lengths_in.astype(jnp.float32), CORE_BIT).astype(jnp.int32)
    lengths = jnp.where(staying, seq_lengths, other_lengths)
    params = by_chip(norm_params, chip)
    block_begins = first_blocks(lengths, group_rows, SHORT) * SHORT
    info = jnp.concatenate([me[None].astype(jnp.int32), block_begins.astype(jnp.int32)])
    cot_low, knn_sums = neighbours(
        where,
        blending_coefficients,
        nearby_entry_gaps,
        neighbor_ids,
        targets,
        lm_logprob,
        lm_grad,
    )
    tokens_one, wf, params, info, wa_other, cot_low = together(
        tokens_one, wf, params, info, wa_other, cot_low
    )
    tokens_two = near_of_moved(tokens_one)
    wa = weight_halves(wa, wa_other, place)
    wa_first = cross_one(wa)
    wf_other = flip(wf, HALF_BIT)
    tokens_one, tokens_two, wa_first, cot_low = together(tokens_one, tokens_two, wa_first, cot_low)
    pair1 = jnp.concatenate(
        [
            jnp.where(staying, tokens_in, tokens_one),
            jnp.where(staying, tokens_one, tokens_two),
        ],
        axis=0,
    )
    far1 = flip(pair1, CORE_BIT)
    wa_pair = cross_two(jnp.stack([wa, wa_first]))
    cot_one = swap_or_near(cot_low)
    far1, pair1 = together(far1, pair1)
    normed1_all, own_low = normalize(where, pair1, far1, params)
    resid = own_low.astype(jnp.float32)
    normed1_all, wa_pair = together(normed1_all, wa_pair)
    wa_all = by_rel(core, wa, wa_first, wa_pair, 1)
    proj_in, proj_out = wa_all[:3], wa_all[3]

    qkv = dot32("rd,sdc->src", normed1_all, proj_in).astype(low)
    heads_flat = attend(info, qkv)
    heads_flat, wf_other, wf, cot_one = together(heads_flat, wf_other, wf, cot_one)

    def out_rows(a, b):
        return dot32("rc,dc->rd", heads_flat[a:b], proj_out)

    sent4 = out_rows(2 * rows, 4 * rows).astype(low)
    sent4, wf, heads_flat = together(sent4, weight_halves(wf, wf_other, place), heads_flat)
    received4 = flip(sent4, CORE_BIT)
    wf_first = cross_one(wf)
    near4 = (out_rows(rows, 2 * rows) + received4[rows:].astype(jnp.float32)).astype(low)
    near4, cot_one, heads_flat = together(near4, cot_one, heads_flat)
    from_near4 = flip(near4, LINE_BIT)
    cot_two = near_of_moved(cot_one)
    attn_out = out_rows(0, rows) + received4[:rows].astype(jnp.float32)
    attn_out, from_near4, wf_first, cot_two = together(attn_out, from_near4, wf_first, cot_two)
    middle = resid + attn_out + from_near4.astype(jnp.float32)
    normed2, norm2_back = jax.vjp(layer_norm, middle, params[2], params[3])
    normed2_low = normed2.astype(low)
    normed2_low, cot_two = together(normed2_low, cot_two)
    near2 = flip(normed2_low, LINE_BIT)
    wf_pair = cross_two(jnp.stack([wf, wf_first]))
    cot_moved = jnp.where(staying, cot_low, cot_one)
    pair_cot = jnp.concatenate([cot_moved, jnp.where(staying, cot_one, cot_two)], axis=0)
    far_cot = flip(pair_cot, CORE_BIT)
    cotangent = cot_moved.astype(jnp.float32)
    near2, far_cot, cotangent, normed2_low, wf_pair = together(
        near2, far_cot, cotangent, normed2_low, wf_pair
    )
    pair2 = jnp.concatenate([normed2_low, near2], axis=0)
    far2 = flip(pair2, CORE_BIT)
    wf_all = by_rel(core, wf, wf_first, wf_pair, 1)
    w_up, w_down = wf_all[0], wf_all[1]

    far2, w_up, w_down = together(far2, w_up, w_down)
    act_low, grad_pre_low = ffn_middle((pair2, far2), (pair_cot, far_cot), w_up, w_down)

    def back_rows(a, b):
        return dot32("rf,df->rd", grad_pre_low[a:b], w_up)

    sent2 = back_rows(2 * rows, 4 * rows).astype(low)
    sent2, pair2, far2, pair_cot, far_cot, act_low = together(
        sent2, pair2, far2, pair_cot, far_cot, act_low
    )
    normed2_all = jnp.concatenate([pair2, far2], axis=0)
    cot_all = jnp.concatenate([pair_cot, far_cot], axis=0)
    received2 = flip(sent2, CORE_BIT)
    cut = ffn_weights.shape[2] // 2
    up_halves = [
        dot32("rd,rf->df", normed2_all, grad_pre_low[:, :cut]).astype(low),
        dot32("rd,rf->df", normed2_all, grad_pre_low[:, cut:]).astype(low),
    ]
    near2 = back_rows(rows, 2 * rows) + received2[rows:].astype(jnp.float32)
    near2, act_low = together(near2.astype(low), act_low)
    from_near2 = flip(near2, LINE_BIT)
    own2 = back_rows(0, rows) + received2[:rows].astype(jnp.float32)
    down_halves = [
        dot32("rd,rf->df", cot_all, act_low[:, :cut]).astype(low),
        dot32("rd,rf->df", cot_all, act_low[:, cut:]).astype(low),
    ]
    ffn_kept, ffn_sent = scatter_parts(core, up_halves + down_halves)
    ffn_got = cross_one(ffn_sent)
    own2, from_near2 = together(own2, from_near2)
    grad_normed2 = own2 + from_near2.astype(jnp.float32)
    mid_norm_grad, gain2_grad, shift2_grad = norm2_back(grad_normed2)
    grad_middle = cotangent + mid_norm_grad
    mid_low, act_low = together(grad_middle.astype(low), act_low)
    near_mid = flip(mid_low, LINE_BIT)
    out_sent = dot32("rf,df->rd", act_low[2 * rows :], w_down).astype(low)
    ffn_got, ffn_kept, out_sent, act_low = together(ffn_got, ffn_kept, out_sent, act_low)
    ffn_kept = add_low(ffn_kept, ffn_got)
    ffn_got = cross_two(ffn_kept[:, 1])
    out_received = flip(out_sent, CORE_BIT)
    out_near = dot32("rf,df->rd", act_low[rows : 2 * rows], w_down) + out_received[rows:].astype(
        jnp.float32
    )
    ffn_out = dot32("rf,df->rd", act_low[:rows], w_down) + out_received[:rows].astype(jnp.float32)
    near_mid, ffn_got, out_near, ffn_out, mid_low = together(
        near_mid, ffn_got, out_near.astype(low), ffn_out, mid_low
    )
    pair_mid = jnp.concatenate([mid_low, near_mid], axis=0)
    far_mid = flip(pair_mid, CORE_BIT)
    ffn_part = add_low(ffn_kept[:, 0], ffn_got)
    ffn_other = flip(ffn_part, HALF_BIT)
    out_from_near = flip(out_near, LINE_BIT)

    grad_heads = jnp.concatenate(
        [dot32("rd,dc->rc", part, proj_out).astype(low) for part in (pair_mid, far_mid)], axis=0
    )
    grad_half = attend_back(info, qkv, grad_heads, 0, None)
    grad_half, pair_mid, far_mid = together(grad_half, pair_mid, far_mid)
    grad_out_proj = dot32("rd,rc->dc", pair_mid, heads_flat[: 2 * rows]) + dot32(
        "rd,rc->dc", far_mid, heads_flat[2 * rows :]
    )
    grad_out_proj = grad_out_proj.astype(low)
    grad_qkv = attend_back(info, qkv, grad_heads, 1, grad_half)
    grad_qkv, grad_out_proj = together(grad_qkv, grad_out_proj)

    def back_in(a, b):
        return dot32("src,sdc->rd", grad_qkv[:, a:b], proj_in)

    grad_parts = [
        dot32("rd,rc->dc", normed1_all, grad_qkv[part]).astype(low) for part in range(3)
    ] + [grad_out_proj]
    attn_kept, attn_sent = scatter_parts(core, grad_parts)
    sent1 = back_in(2 * rows, 4 * rows).astype(low)
    attn_kept, attn_sent, sent1, grad_qkv, ffn_other, out_from_near = together(
        attn_kept, attn_sent, sent1, grad_qkv, ffn_other, out_from_near
    )

    attn_got = cross_one(attn_sent)
    received1 = flip(sent1, CORE_BIT)
    ffn_own = add_low(ffn_part, ffn_other)
    ffn_near = flip(ffn_own, LINE_BIT)
    near3 = back_in(rows, 2 * rows) + received1[rows:].astype(jnp.float32)
    near3, grad_qkv = together(near3.astype(low), grad_qkv)
    from_near3 = flip(near3, LINE_BIT)
    own3 = back_in(0, rows) + received1[:rows].astype(jnp.float32)
    attn_got, attn_kept, own3, ffn_out = together(attn_got, attn_kept, own3, ffn_out)

    attn_kept = add_low(attn_kept, attn_got)
    attn_kept, own3, ffn_out = together(attn_kept, own3, ffn_out)
    attn_got = cross_two(attn_kept[:, 1])
    ffn_out = ffn_out + out_from_near.astype(jnp.float32)
    mixed = by_chip((middle + ffn_out).astype(low), chip)
    attn_got, attn_kept, own3, ffn_near, ffn_own, mixed = together(
        attn_got, attn_kept, own3, ffn_near, ffn_own, mixed
    )

    attn_part = add_low(attn_kept[:, 0], attn_got)
    ffn_line = jnp.stack([ffn_own, ffn_near])
    attn_part, own3, ffn_line, mixed = together(attn_part, own3, ffn_line, mixed)
    attn_other = flip(attn_part, HALF_BIT)
    ffn_first = cross_one(ffn_line)
    attn_other, attn_part, ffn_first, ffn_line, own3, mixed = together(
        attn_other, attn_part, ffn_first, ffn_line, own3, mixed
    )

    attn_own = add_low(attn_part, attn_other)
    ffn_two = jnp.stack([ffn_line, ffn_first])
    attn_own, own3, ffn_two, from_near3 = together(attn_own, own3, ffn_two, from_near3)
    attn_near = flip(attn_own, LINE_BIT)
    ffn_pair = cross_two(ffn_two)
    input_grad, gain_sums = norm_back(
        where, own3, from_near3, own_low, grad_middle, params[0:1]
    )
    attn_near, attn_own, gain_sums, input_grad, mixed = together(
        attn_near, attn_own, gain_sums, input_grad, mixed
    )

    attn_line = jnp.stack([attn_own, attn_near])
    norm_grads = jnp.concatenate([gain_sums, gain2_grad[None], shift2_grad[None]], axis=0)
    small = jnp.concatenate([by_chip(norm_grads, chip), knn_sums], axis=0)
    left_low = jnp.concatenate([attn_left_root.astype(low), ffn_left_root.astype(low)], axis=0)
    left_low = jnp.concatenate([left_low, flip(left_low, CORE_BIT)], axis=1)
    attn_line, small, attn_left_low, ffn_left_low, mixed, input_grad = together(
        attn_line, small, left_low[:4], left_low[4:], mixed, input_grad
    )
    attn_first = cross_one(attn_line)
    mixed = swap_core_half(mixed)
    input_grad = swap_core_half(input_grad)
    small = small + flip(small, CORE_BIT)
    attn_first, attn_line, small, mixed, input_grad = together(
        attn_first, attn_line, small, mixed, input_grad
    )

    attn_pair = cross_two(jnp.stack([attn_line, attn_first]))
    small = small + flip(small, HALF_BIT)
    ffn_pair, small = together(ffn_pair, small)
    small = small + flip(small, LINE_BIT)
    ffn_pieces = (ffn_line, ffn_first, ffn_pair)
    ffn_own, ffn_sent = updates(where, ffn_left_low, ffn_pieces, ffn_right_root, True)
    attn_pair, attn_first, attn_line, ffn_own, ffn_sent, ffn_line, ffn_first, ffn_pair, small = (
        together(
            attn_pair,
            attn_first,
            attn_line,
            ffn_own,
            ffn_sent,
            ffn_line,
            ffn_first,
            ffn_pair,
            small,
        )
    )

    ffn_pieces = (ffn_line, ffn_first, ffn_pair)
    attn_pieces = (attn_line, attn_first, attn_pair)
    attn_cols = column_block(attn_pieces, None, place["half"], False, core)
    ffn_cols = column_block(ffn_pieces, None, place["half"], True, core)
    attn_cols_other = flip(attn_cols, CORE_BIT)
    ffn_cols_other = flip(ffn_cols, CORE_BIT)
    ffn_received = flip(ffn_sent, CORE_BIT)
    attn_own, attn_sent = updates(where, attn_left_low, attn_pieces, attn_right_root, False)
    small = small + flip(small, X_BIT)
    attn_sent, small = together(attn_sent, small)
    attn_received = flip(attn_sent, CORE_BIT)
    summed = small + flip(small, Y_BIT)
    ffn_right_new, ffn_grad = right_statistics_new(
        where, ffn_pieces, ffn_cols_other, ffn_right, ffn_weights.shape[1], True
    )
    attn_right_new, attn_grad = right_statistics_new(
        where, attn_pieces, attn_cols_other, attn_right, attn_weights.shape[1], False
    )
    summed, ffn_right_new, attn_right_new = together(summed, ffn_right_new, attn_right_new)
    ffn_left_new, ffn_new = shampoo_left(ffn_own, ffn_received, ffn_left, ffn_weights)
    attn_left_new, attn_new = shampoo_left(attn_own, attn_received, attn_left, attn_weights)
    input_grad = input_grad.astype(jnp.float32)
    norm_total = summed[:4]
    knn_total = summed[4, :2]
    loss = summed[4, 2] / (group_rows * 8)
    norm_m1, norm_m2, norm_new = adamw_step(norm_params, norm_total, norm_moment1, norm_moment2)
    knn_m1, knn_m2, knn_new = adamw_step(blending_coefficients, knn_total, knn_moment1, knn_moment2)
    return (
        mixed,
        input_grad,
        loss,
        attn_grad,
        attn_left_new,
        attn_right_new,
        attn_new,
        ffn_grad,
        ffn_left_new,
        ffn_right_new,
        ffn_new,
        norm_m1,
        norm_m2,
        norm_new,
        knn_m1,
        knn_m2,
        knn_new,
    )


def solution(mesh):
    sized = (mesh.shape["dp"], mesh.shape["tensor"]) == (8, 4)
    placed = (
        P(("dp", "tensor"), None),
        P(("dp", "tensor"), None),
        P(("dp", "tensor")),
        P(("dp", "tensor")),
        P(("dp", "tensor"), None),
        P(("dp", "tensor"), None),
        P("dp", None),
        P(None, "dp", "tensor"),
        P(None, "dp", "tensor"),
        P(None, "dp", "tensor"),
        P(None, "tensor", "dp"),
        P(None, "dp", "tensor"),
        P(None, "tensor", "dp"),
        P(None, "dp", None),
        P(None, None, "tensor"),
        P(None, "dp", None),
        P(None, None, "tensor"),
        P(),
        P(),
        P(),
        P(),
        P(),
        P(),
    )
    return jax.shard_map(
        regrouped if sized else local,
        mesh=mesh,
        in_specs=placed,
        out_specs=(
            P(("dp", "tensor"), None),
            P(("dp", "tensor"), None),
            P(),
            P(None, "dp", "tensor"),
            P(None, "dp", "tensor"),
            P(None, "tensor", "dp"),
            P(None, "dp", "tensor"),
            P(None, "dp", "tensor"),
            P(None, "dp", "tensor"),
            P(None, "tensor", "dp"),
            P(None, "dp", "tensor"),
            P(),
            P(),
            P(),
            P(),
            P(),
            P(),
        ),
        check_vma=False,
    )
```

```python
import jax
import jax.numpy as jnp
from jax import lax
from jax.experimental import pallas as pl
from jax.experimental.pallas import tpu as pltpu
from jax.sharding import PartitionSpec as P

SHORT = 512
STEP = 10
HEAD_DIM = 64


adam_rate = 0.3
shampoo_rate = 0.5
shampoo_decay = 0.01
norm_eps = 1e-05


def layer_norm(values_in, gain, shift):
    centre = jnp.mean(values_in, axis=-1, keepdims=True)
    centred = values_in - centre
    spread_sq = jnp.mean(centred * centred, axis=-1, keepdims=True)
    return centred * lax.rsqrt(spread_sq + norm_eps) * gain + shift


def gelu_tanh(values_in):
    return jax.nn.gelu(values_in, approximate=True)


def spread_rows(local_low):
    return lax.all_gather(local_low, "tensor", axis=0, tiled=True)


def spread_again(local_low):
    return lax.all_gather(local_low, "tensor", axis=0, tiled=True)


def spread_grads(local_low):
    return lax.all_gather(local_low, "tensor", axis=0, tiled=True)


def branch_total(left_rows, right_mat):
    return lax.psum_scatter(
        jnp.einsum("rc,dc->rd", left_rows, right_mat, preferred_element_type=jnp.float32),
        "tensor",
        scatter_dimension=0,
        tiled=True,
    )


def input_total(left_rows, right_mat):
    return lax.psum_scatter(
        jnp.einsum("rc,dc->rd", left_rows, right_mat, preferred_element_type=jnp.float32),
        "tensor",
        scatter_dimension=0,
        tiled=True,
    )


def first_blocks(seq_lengths, group_rows, block_rows):
    lengths = seq_lengths[0]
    seq_ends = jnp.cumsum(lengths)
    seq_begins = seq_ends - lengths
    block_begins = jnp.arange(group_rows // block_rows, dtype=jnp.int32) * block_rows
    inside = (seq_begins[None, :] <= block_begins[:, None]) & (lengths[None, :] > 0)
    return jnp.max(jnp.where(inside, seq_begins[None, :], 0), axis=1) // block_rows


def block_scores(query_rows, key_rows, query_block, key_block, block_rows, score_scale):
    scores = (
        jnp.einsum("qhd,khd->hqk", query_rows, key_rows, preferred_element_type=jnp.float32)
        * score_scale
    )
    query_pos = query_block * block_rows + jnp.arange(block_rows, dtype=jnp.int32)
    key_pos = key_block * block_rows + jnp.arange(block_rows, dtype=jnp.int32)
    allowed = key_pos[None, :] <= query_pos[:, None]
    return jnp.where(allowed[None], scores, -1e30)


def attend_forward(query_all, key_all, value_all, first_block, block_rows, score_scale):
    group_rows, head_count, head_width = query_all.shape

    def one_block(query_block):
        query_rows = lax.dynamic_slice_in_dim(query_all, query_block * block_rows, block_rows, 0)

        def peak_step(key_block, loop_state):
            running_top, running_mass = loop_state
            key_rows = lax.dynamic_slice_in_dim(key_all, key_block * block_rows, block_rows, 0)
            scores = block_scores(
                query_rows, key_rows, query_block, key_block, block_rows, score_scale
            )
            new_top = jnp.maximum(running_top, jnp.max(scores, axis=2))
            new_mass = running_mass * jnp.exp(running_top - new_top) + jnp.sum(
                jnp.exp(scores - new_top[:, :, None]), axis=2
            )
            return (new_top, new_mass)

        start_state = (
            jnp.full((head_count, block_rows), -1e30, jnp.float32),
            jnp.zeros((head_count, block_rows), jnp.float32),
        )
        final_top, final_mass = lax.fori_loop(
            first_block[query_block], query_block + 1, peak_step, start_state
        )
        log_mass = final_top + jnp.log(final_mass)

        def value_step(key_block, out_acc):
            key_rows = lax.dynamic_slice_in_dim(key_all, key_block * block_rows, block_rows, 0)
            value_rows = lax.dynamic_slice_in_dim(value_all, key_block * block_rows, block_rows, 0)
            scores = block_scores(
                query_rows, key_rows, query_block, key_block, block_rows, score_scale
            )
            attn_probs = jnp.exp(scores - log_mass[:, :, None]).astype(jnp.bfloat16)
            return out_acc + jnp.einsum(
                "hqk,khd->qhd", attn_probs, value_rows, preferred_element_type=jnp.float32
            )

        out_rows = lax.fori_loop(
            first_block[query_block],
            query_block + 1,
            value_step,
            jnp.zeros((block_rows, head_count, head_width), jnp.float32),
        )
        return (out_rows.astype(jnp.bfloat16), log_mass)

    outs, log_masses = lax.map(one_block, jnp.arange(group_rows // block_rows, dtype=jnp.int32))
    return (outs.reshape(group_rows, head_count, head_width), log_masses)


def attend_backward(
    query_all, key_all, value_all, grad_out, log_masses, first_block, block_rows, score_scale
):
    group_rows, head_count, head_width = query_all.shape

    def one_block(query_block, loop_carry):
        grad_keys, grad_values, grad_query = loop_carry
        query_rows = lax.dynamic_slice_in_dim(query_all, query_block * block_rows, block_rows, 0)
        grad_rows = lax.dynamic_slice_in_dim(grad_out, query_block * block_rows, block_rows, 0)
        log_mass = log_masses[query_block]

        def chances(key_block):
            key_rows = lax.dynamic_slice_in_dim(key_all, key_block * block_rows, block_rows, 0)
            value_rows = lax.dynamic_slice_in_dim(value_all, key_block * block_rows, block_rows, 0)
            scores = block_scores(
                query_rows, key_rows, query_block, key_block, block_rows, score_scale
            )
            attn_probs = jnp.exp(scores - log_mass[:, :, None])
            likelihood_cotangent = jnp.einsum(
                "qhd,khd->hqk", grad_rows, value_rows, preferred_element_type=jnp.float32
            )
            return (key_rows, attn_probs, likelihood_cotangent)

        def inner_step(key_block, inner_acc):
            _, attn_probs, likelihood_cotangent = chances(key_block)
            return inner_acc + jnp.sum(attn_probs * likelihood_cotangent, axis=2)

        row_inner = lax.fori_loop(
            first_block[query_block],
            query_block + 1,
            inner_step,
            jnp.zeros((head_count, block_rows), jnp.float32),
        )

        def grad_step(key_block, loop_state):
            query_acc, keys_acc, values_acc = loop_state
            key_rows, attn_probs, likelihood_cotangent = chances(key_block)
            grad_scores = (attn_probs * (likelihood_cotangent - row_inner[:, :, None])).astype(
                jnp.bfloat16
            )
            query_acc = (
                query_acc
                + jnp.einsum(
                    "hqk,khd->qhd", grad_scores, key_rows, preferred_element_type=jnp.float32
                )
                * score_scale
            )
            key_part = (
                jnp.einsum(
                    "hqk,qhd->khd", grad_scores, query_rows, preferred_element_type=jnp.float32
                )
                * score_scale
            )
            value_part = jnp.einsum(
                "hqk,qhd->khd",
                attn_probs.astype(jnp.bfloat16),
                grad_rows,
                preferred_element_type=jnp.float32,
            )
            key_start = key_block * block_rows
            keys_acc = lax.dynamic_update_slice_in_dim(
                keys_acc,
                lax.dynamic_slice_in_dim(keys_acc, key_start, block_rows, 0) + key_part,
                key_start,
                0,
            )
            values_acc = lax.dynamic_update_slice_in_dim(
                values_acc,
                lax.dynamic_slice_in_dim(values_acc, key_start, block_rows, 0) + value_part,
                key_start,
                0,
            )
            return (query_acc, keys_acc, values_acc)

        query_acc, grad_keys, grad_values = lax.fori_loop(
            first_block[query_block],
            query_block + 1,
            grad_step,
            (jnp.zeros((block_rows, head_count, head_width), jnp.float32), grad_keys, grad_values),
        )
        grad_query = lax.dynamic_update_slice_in_dim(
            grad_query, query_acc, query_block * block_rows, 0
        )
        return (grad_keys, grad_values, grad_query)

    zeros_all = jnp.zeros((group_rows, head_count, head_width), jnp.float32)
    return lax.fori_loop(0, group_rows // block_rows, one_block, (zeros_all, zeros_all, zeros_all))


def right_statistics(attn_part_grad, ffn_part_grad, attn_rows, ffn_rows):
    attn_part = jnp.einsum(
        "sri,srj->sij", attn_part_grad, attn_rows, precision=lax.Precision.HIGHEST
    )
    ffn_part = jnp.einsum("sri,srj->sij", ffn_part_grad, ffn_rows, precision=lax.Precision.HIGHEST)
    return (
        lax.psum_scatter(
            attn_part.astype(jnp.bfloat16), "dp", scatter_dimension=2, tiled=True
        ).astype(jnp.float32),
        lax.psum_scatter(
            ffn_part.astype(jnp.bfloat16), "dp", scatter_dimension=2, tiled=True
        ).astype(jnp.float32),
    )


def left_statistics(attn_part_grad, ffn_part_grad, attn_cols, ffn_cols):
    attn_part = jnp.einsum(
        "sri,sqi->srq", attn_part_grad, attn_cols, precision=lax.Precision.HIGHEST
    )
    ffn_part = jnp.einsum("sri,sqi->srq", ffn_part_grad, ffn_cols, precision=lax.Precision.HIGHEST)
    return (
        lax.psum_scatter(
            attn_part.astype(jnp.bfloat16), "tensor", scatter_dimension=2, tiled=True
        ).astype(jnp.float32),
        lax.psum_scatter(
            ffn_part.astype(jnp.bfloat16), "tensor", scatter_dimension=2, tiled=True
        ).astype(jnp.float32),
    )


def adamw_step(params_in, grads_in, first_in, second_in):
    first_new = 0.9 * first_in + 0.1 * grads_in
    second_new = 0.999 * second_in + 0.001 * grads_in * grads_in
    first_hat = first_new / (1.0 - 0.9**STEP)
    second_hat = second_new / (1.0 - 0.999**STEP)
    return (
        first_new,
        second_new,
        params_in - adam_rate * first_hat / (jnp.sqrt(second_hat) + 1e-08),
    )


def local(
    tokens_in,
    lm_grad,
    lm_logprob,
    targets,
    neighbor_ids,
    nearby_entry_gaps,
    seq_lengths,
    attn_weights,
    ffn_weights,
    attn_left,
    attn_right,
    ffn_left,
    ffn_right,
    attn_left_root,
    attn_right_root,
    ffn_left_root,
    ffn_right_root,
    norm_params,
    norm_moment1,
    norm_moment2,
    blending_coefficients,
    knn_moment1,
    knn_moment2,
):
    local_rows = tokens_in.shape[0]
    group_rows = local_rows * lax.axis_size("tensor")
    block_rows = SHORT
    score_scale = HEAD_DIM ** (-0.5)
    attn_full, ffn_full = (
        lax.all_gather(attn_weights.astype(jnp.bfloat16), "dp", axis=1, tiled=True),
        lax.all_gather(ffn_weights.astype(jnp.bfloat16), "dp", axis=1, tiled=True),
    )
    proj_in = jnp.concatenate([attn_full[0], attn_full[1], attn_full[2]], axis=1)
    proj_out = attn_full[3]
    head_cols = proj_out.shape[1]
    head_count = head_cols // HEAD_DIM
    first_block = first_blocks(seq_lengths, group_rows, block_rows)
    resid = tokens_in.astype(jnp.float32)
    normed1, norm1_back = jax.vjp(layer_norm, resid, norm_params[0], norm_params[1])
    normed1_low = normed1.astype(jnp.bfloat16)
    normed1_all = spread_rows(normed1_low)
    qkv_low = jnp.dot(normed1_all, proj_in, preferred_element_type=jnp.float32).astype(jnp.bfloat16)
    query_all = qkv_low[:, :head_cols].reshape(group_rows, head_count, HEAD_DIM)
    key_all = qkv_low[:, head_cols : 2 * head_cols].reshape(group_rows, head_count, HEAD_DIM)
    value_all = qkv_low[:, 2 * head_cols :].reshape(group_rows, head_count, HEAD_DIM)
    heads_out, log_masses = attend_forward(
        query_all, key_all, value_all, first_block, block_rows, score_scale
    )
    heads_flat = heads_out.reshape(group_rows, head_cols)
    attn_out = branch_total(heads_flat, proj_out)
    middle = resid + attn_out
    normed2, norm2_back = jax.vjp(layer_norm, middle, norm_params[2], norm_params[3])
    normed2_low = normed2.astype(jnp.bfloat16)
    w_up = ffn_full[0]
    w_down = ffn_full[1]
    normed2_all = spread_rows(normed2_low)
    hidden_pre = jnp.dot(normed2_all, w_up, preferred_element_type=jnp.float32)
    hidden_act, gelu_back = jax.vjp(gelu_tanh, hidden_pre)
    act_low = hidden_act.astype(jnp.bfloat16)
    ffn_out = branch_total(act_low, w_down)
    mixed = (middle + ffn_out).astype(jnp.bfloat16)
    sharpness_divisor = jnp.exp(blending_coefficients[0])
    interp = jax.nn.sigmoid(blending_coefficients[1])
    nearby_entry_logits = -nearby_entry_gaps / sharpness_divisor
    near_top = jnp.max(nearby_entry_logits, axis=1, keepdims=True)
    near_exp = jnp.exp(nearby_entry_logits - near_top)
    nearby_entry_shares = near_exp / jnp.sum(near_exp, axis=1, keepdims=True)
    target_matches = (neighbor_ids == targets[:, None]).astype(jnp.float32)
    retrieval_probability = jnp.sum(nearby_entry_shares * target_matches, axis=1)
    lm_prob = jnp.exp(lm_logprob)
    mixture = interp * retrieval_probability + (1.0 - interp) * lm_prob
    token_loss = -jnp.log(mixture)
    lm_weight = -(1.0 - interp) * lm_prob / mixture
    temp_terms = (
        jnp.sum(
            nearby_entry_shares
            * (target_matches - retrieval_probability[:, None])
            * nearby_entry_gaps,
            axis=1,
        )
        / sharpness_divisor
    )
    temp_grad = jnp.sum(-(interp / mixture) * temp_terms)
    interp_grad = jnp.sum(-interp * (1.0 - interp) * (retrieval_probability - lm_prob) / mixture)
    knn_grads = jnp.stack([temp_grad, interp_grad])
    cotangent = lm_weight[:, None] * lm_grad.astype(jnp.float32)
    cot_all = spread_grads(cotangent.astype(jnp.bfloat16))
    grad_act = jnp.dot(cot_all, w_down, preferred_element_type=jnp.float32)
    grad_pre_low = gelu_back(grad_act)[0].astype(jnp.bfloat16)
    normed2_used = spread_again(normed2_low)
    grad_up = jnp.einsum(
        "rd,rf->df", normed2_used, grad_pre_low, preferred_element_type=jnp.float32
    )
    grad_down = jnp.einsum("rd,rf->df", cot_all, act_low, preferred_element_type=jnp.float32)
    ffn_local = jnp.stack([grad_up, grad_down])
    grad_normed2 = input_total(grad_pre_low, w_up)
    mid_norm_grad, gain2_grad, shift2_grad = norm2_back(grad_normed2)
    grad_middle = cotangent + mid_norm_grad
    grad_mid_all = spread_grads(grad_middle.astype(jnp.bfloat16))
    grad_heads = jnp.dot(grad_mid_all, proj_out, preferred_element_type=jnp.float32).astype(
        jnp.bfloat16
    )
    grad_out_proj = jnp.einsum(
        "rd,rc->dc", grad_mid_all, heads_flat, preferred_element_type=jnp.float32
    )
    grad_keys, grad_values, grad_query = attend_backward(
        query_all,
        key_all,
        value_all,
        grad_heads.reshape(group_rows, head_count, HEAD_DIM),
        log_masses,
        first_block,
        block_rows,
        score_scale,
    )
    grad_qkv = jnp.concatenate(
        [
            grad_query.reshape(group_rows, head_cols),
            grad_keys.reshape(group_rows, head_cols),
            grad_values.reshape(group_rows, head_cols),
        ],
        axis=1,
    ).astype(jnp.bfloat16)
    normed1_used = spread_again(normed1_low)
    grad_proj_in = jnp.einsum(
        "rd,rc->dc", normed1_used, grad_qkv, preferred_element_type=jnp.float32
    )
    grad_normed1 = input_total(grad_qkv, proj_in)
    res_norm_grad, gain1_grad, bias_first_cotangent = norm1_back(grad_normed1)
    input_grad = grad_middle + res_norm_grad
    norm_grads = jnp.stack([gain1_grad, bias_first_cotangent, gain2_grad, shift2_grad])
    norm_total, knn_total, loss_total = lax.psum(
        (norm_grads, knn_grads, jnp.sum(token_loss)), ("dp", "tensor")
    )
    token_count = group_rows * lax.axis_size("dp")
    attn_local = jnp.stack(
        [
            grad_proj_in[:, :head_cols],
            grad_proj_in[:, head_cols : 2 * head_cols],
            grad_proj_in[:, 2 * head_cols :],
            grad_out_proj,
        ]
    )
    attn_grad, ffn_grad = (
        lax.psum_scatter(attn_local, "dp", scatter_dimension=1, tiled=True),
        lax.psum_scatter(ffn_local, "dp", scatter_dimension=1, tiled=True),
    )
    attn_rows, ffn_rows = (
        lax.all_gather(attn_grad.astype(jnp.bfloat16), "tensor", axis=2, tiled=True).astype(
            attn_grad.dtype
        ),
        lax.all_gather(ffn_grad.astype(jnp.bfloat16), "tensor", axis=2, tiled=True).astype(
            ffn_grad.dtype
        ),
    )
    attn_right_sum, ffn_right_sum = right_statistics(attn_grad, ffn_grad, attn_rows, ffn_rows)
    attn_turned = jnp.einsum(
        "sri,sij->srj", attn_rows, attn_right_root, precision=lax.Precision.HIGHEST
    )
    ffn_turned = jnp.einsum(
        "sri,sij->srj", ffn_rows, ffn_right_root, precision=lax.Precision.HIGHEST
    )
    attn_cols, ffn_cols, attn_turned_cols, ffn_turned_cols = (
        lax.all_gather(attn_grad.astype(jnp.bfloat16), "dp", axis=1, tiled=True).astype(
            attn_grad.dtype
        ),
        lax.all_gather(ffn_grad.astype(jnp.bfloat16), "dp", axis=1, tiled=True).astype(
            ffn_grad.dtype
        ),
        lax.all_gather(attn_turned.astype(jnp.bfloat16), "dp", axis=1, tiled=True).astype(
            attn_turned.dtype
        ),
        lax.all_gather(ffn_turned.astype(jnp.bfloat16), "dp", axis=1, tiled=True).astype(
            ffn_turned.dtype
        ),
    )
    attn_left_sum, ffn_left_sum = left_statistics(attn_grad, ffn_grad, attn_cols, ffn_cols)
    attn_update = jnp.einsum(
        "srq,sqi->sri", attn_left_root, attn_turned_cols, precision=lax.Precision.HIGHEST
    )
    ffn_update = jnp.einsum(
        "srq,sqi->sri", ffn_left_root, ffn_turned_cols, precision=lax.Precision.HIGHEST
    )
    attn_left_new = 0.5 * attn_left + 0.5 * attn_left_sum
    attn_right_new = 0.5 * attn_right + 0.5 * attn_right_sum
    ffn_left_new = 0.5 * ffn_left + 0.5 * ffn_left_sum
    ffn_right_new = 0.5 * ffn_right + 0.5 * ffn_right_sum
    attn_new = attn_weights - shampoo_rate * (attn_update + shampoo_decay * attn_weights)
    ffn_new = ffn_weights - shampoo_rate * (ffn_update + shampoo_decay * ffn_weights)
    norm_m1, norm_m2, norm_new = adamw_step(norm_params, norm_total, norm_moment1, norm_moment2)
    knn_m1, knn_m2, knn_new = adamw_step(blending_coefficients, knn_total, knn_moment1, knn_moment2)
    return (
        mixed,
        input_grad,
        loss_total / token_count,
        attn_grad,
        attn_left_new,
        attn_right_new,
        attn_new,
        ffn_grad,
        ffn_left_new,
        ffn_right_new,
        ffn_new,
        norm_m1,
        norm_m2,
        norm_new,
        knn_m1,
        knn_m2,
        knn_new,
    )


LINE_BIT, HALF_BIT, CORE_BIT, X_BIT, Y_BIT = 1, 2, 4, 8, 16


def send_by(values_in, target):
    return lax.ppermute(values_in, ("dp", "tensor"), [(index, target(index)) for index in range(32)])


def flip(values_in, mask):
    return send_by(values_in, lambda index: index ^ mask)


def moves(index):
    return ((index >> 2) ^ (index >> 1)) & 1 == 1


def swapped(index):
    return index ^ (CORE_BIT | HALF_BIT) if moves(index) else index


def swap_core_half(values_in):
    return send_by(values_in, swapped)


def swap_or_near(values_in):
    return send_by(
        values_in, lambda index: swapped(index) if moves(index) else index ^ LINE_BIT
    )


def near_of_moved(values_in):
    pairs = [(index, index ^ LINE_BIT) for index in range(32) if moves(index)]
    return lax.ppermute(values_in, ("dp", "tensor"), pairs)


def cross_one(values_in):
    return send_by(values_in, lambda index: index ^ (Y_BIT if index & CORE_BIT else X_BIT))


def cross_two(values_in):
    return send_by(values_in, lambda index: index ^ (X_BIT if index & CORE_BIT else Y_BIT))


def pick(values_in, index, axis):
    return lax.dynamic_index_in_dim(values_in, index, axis, keepdims=False)


def ordered_pair(own, other, bit, axis):
    return jnp.where(
        bit == 0, jnp.stack([own, other], axis=axis), jnp.stack([other, own], axis=axis)
    )


def together(*values_in):
    return lax.optimization_barrier(values_in)


def by_chip(values_in, chip):
    width = values_in.shape[-1] // 4
    return jnp.concatenate(
        [
            lax.dynamic_slice_in_dim(values_in, (chip ^ block) * width, width, values_in.ndim - 1)
            for block in range(4)
        ],
        axis=-1,
    )


def add_far(pair):
    return jnp.concatenate([pair, flip(pair, CORE_BIT)], axis=0)


def weight_core(local_low, place):
    width = local_low.shape[2] // 2
    mine = lax.dynamic_slice_in_dim(local_low, place["core"] * width, width, 2)
    theirs = lax.dynamic_slice_in_dim(local_low, (1 - place["core"]) * width, width, 2)
    both = ordered_pair(mine, flip(theirs, CORE_BIT), place["core"], 1)
    return both.reshape(local_low.shape[0], 2 * local_low.shape[1], width)


def weight_halves(own, other, place):
    return jnp.where(
        place["half"] == 0,
        jnp.concatenate([own, other], axis=2),
        jnp.concatenate([other, own], axis=2),
    )


def by_core(core, own, other, axis):
    return jnp.where(
        core == 0,
        jnp.concatenate([own, other], axis=axis),
        jnp.concatenate([other, own], axis=axis),
    )


def by_rel(core, own, first, pair, axis):
    middle = jnp.where(
        core == 0,
        jnp.concatenate([first, pair[0]], axis=axis),
        jnp.concatenate([pair[0], first], axis=axis),
    )
    return jnp.concatenate([own, middle, pair[1]], axis=axis)


def scatter_parts(core, partials):
    parts = [partial.reshape(2, 2, -1, partial.shape[1]) for partial in partials]
    kept = [jnp.where(core == 0, part[:, 0], part[0]) for part in parts]
    sent = [jnp.where(core == 0, part[:, 1], part[1]) for part in parts]
    return jnp.stack(kept), jnp.stack(sent)


def add_low(left_part, right_part):
    return (left_part.astype(jnp.float32) + right_part.astype(jnp.float32)).astype(jnp.bfloat16)


def dot32(spec, left_mat, right_mat):
    return jnp.einsum(spec, left_mat, right_mat, preferred_element_type=jnp.float32)


def update_kernel(
    info_ref, left_ref, line_ref, first_ref, pair_ref, root_ref, own_ref, sent_ref, update_acc, gram_acc
):
    step = pl.program_id(1)
    steps = pl.num_programs(1)
    chip, core, tensor, line_bit = info_ref[0], info_ref[1], info_ref[2], info_ref[3]
    block = left_ref.shape[2] // 4
    own_rows = block // 2
    cols = update_acc.shape[1]

    @pl.when(step == 0)
    def _():
        update_acc[...] = jnp.zeros_like(update_acc)
        gram_acc[...] = jnp.zeros_like(gram_acc)

    rels = (0, 1 + core, 2 - core, 3)
    lefts = [
        left_ref[0, :, pl.ds(pl.multiple_of((chip ^ rel) * block, block), block)] for rel in rels
    ]
    total = None
    for line in range(2):
        pieces = (
            line_ref[line, 0],
            first_ref[line, 0],
            pair_ref[0, line, 0],
            pair_ref[1, line, 0],
        )
        turned = None
        for left, piece in zip(lefts, pieces):
            part = jnp.dot(left, piece, preferred_element_type=jnp.float32)
            turned = part if turned is None else turned + part
        root = root_ref[0, :, line_bit ^ line, 0].reshape(-1, cols).astype(jnp.bfloat16)
        part = jnp.dot(turned.astype(jnp.bfloat16), root, preferred_element_type=jnp.float32)
        total = part if total is None else total + part
        for rel, piece in zip(rels, pieces):

            @pl.when((chip ^ tensor) == rel)
            def _(own=pieces[0], piece=piece):
                gram_acc[...] += lax.dot_general(
                    own, piece, (((1,), (1,)), ((), ())), preferred_element_type=jnp.float32
                )

    update_acc[...] += total

    @pl.when(step == steps - 1)
    def _():
        own_ref[0, :, :cols] = update_acc[:own_rows]
        sent_ref[0, :, :cols] = update_acc[own_rows:].astype(jnp.bfloat16)
        gram_own = gram_acc[pl.ds(pl.multiple_of(core * own_rows, own_rows), own_rows), :]
        gram_sent = gram_acc[pl.ds(pl.multiple_of((1 - core) * own_rows, own_rows), own_rows), :]
        own_ref[0, :, cols:] = gram_own
        sent_ref[0, :, cols:] = gram_sent.astype(jnp.bfloat16)


def updates(info, left_low, pieces, root, split):
    line, first, pair = pieces
    _, lead, rows, width = line.shape
    count = lead // 2 if split else lead
    cols = root.shape[2]
    root_rows = root.shape[1] // 8
    root = root.reshape(root.shape[0], 2, 2, 2, root_rows, cols)
    steps = 2 if split else 1
    if split:
        root_spec = pl.BlockSpec(
            (1, 1, 2, 1, root_rows, cols),
            lambda m, k, info_ref: (m, k, 0, info_ref[1], 0, 0),
        )
    else:
        root_spec = pl.BlockSpec(
            (1, 2, 2, 1, root_rows, cols),
            lambda m, k, info_ref: (m, 0, 0, info_ref[1], 0, 0),
        )

    def place_of(m, k):
        return 2 * m + k if split else m

    out_shape = (count, rows // 2, cols + rows)
    out_spec = pl.BlockSpec((1, rows // 2, cols + rows), lambda m, k, info_ref: (m, 0, 0))
    piece_spec = pl.BlockSpec(
        (2, 1, rows, width), lambda m, k, info_ref: (0, place_of(m, k), 0, 0)
    )
    return pl.pallas_call(
        update_kernel,
        grid_spec=pltpu.PrefetchScalarGridSpec(
            num_scalar_prefetch=1,
            grid=(count, steps),
            in_specs=[
                pl.BlockSpec((1, rows, 4 * rows), lambda m, k, info_ref: (m, 0, 0)),
                piece_spec,
                piece_spec,
                pl.BlockSpec(
                    (2, 2, 1, rows, width), lambda m, k, info_ref: (0, 0, place_of(m, k), 0, 0)
                ),
                root_spec,
            ],
            out_specs=[out_spec, out_spec],
            scratch_shapes=[
                pltpu.VMEM((rows, cols), jnp.float32),
                pltpu.VMEM((rows, rows), jnp.float32),
            ],
        ),
        out_shape=(
            jax.ShapeDtypeStruct(out_shape, jnp.float32),
            jax.ShapeDtypeStruct(out_shape, jnp.bfloat16),
        ),
        compiler_params=pltpu.CompilerParams(vmem_limit_bytes=48 * 1024 * 1024),
        cost_estimate=pl.CostEstimate(flops=1_000_000, bytes_accessed=100_000, transcendentals=0),
    )(info, left_low, line, first, pair, root)


def column_block(pieces, line_rel, half, split, core):
    line, first, pair = pieces

    def cut(piece):
        piece = piece[0] if line_rel is None else pick(piece, line_rel, 0)
        if split:
            return pick(piece.reshape(-1, 2, *piece.shape[1:]), half, 1)
        width = piece.shape[2] // 2
        return lax.dynamic_slice_in_dim(piece, half * width, width, 2)

    return by_rel(core, cut(line), cut(first), (cut(pair[0]), cut(pair[1])), 1)


def right_kernel(
    info_ref,
    line_t,
    first_t,
    pair_t,
    line_c,
    first_c,
    pair_c,
    other_ref,
    right_in_ref,
    right_ref,
    grad_ref,
):
    core = info_ref[1]
    half = other_ref.shape[2]
    chip_rows = other_ref.shape[1] // 4
    own_rows = chip_rows // 2
    own = (line_t[0, 0], first_t[0, 0], pair_t[0, 0, 0], pair_t[1, 0, 0])
    cols = (line_c[0, 0], first_c[0, 0], pair_c[0, 0, 0], pair_c[1, 0, 0])
    rels = (0, 1 + core, 2 - core, 3)
    sums = [None, None]
    for rel, own_piece, col_piece in zip(rels, own, cols):
        other_piece = other_ref[0, pl.ds(pl.multiple_of(rel * chip_rows, chip_rows), chip_rows), :]
        for at, piece in enumerate((own_piece, other_piece)):
            part = lax.dot_general(
                piece, col_piece, (((0,), (0,)), ((), ())), preferred_element_type=jnp.float32
            )
            sums[at] = part if sums[at] is None else sums[at] + part
    row = pl.ds(pl.multiple_of(core * own_rows, own_rows), own_rows)
    grads = (line_t[0, 0, row, :], other_ref[0, row, :])
    for at in range(2):
        block = core if at == 0 else 1 - core
        rows = pl.ds(pl.multiple_of(block * half, half), half)
        right_ref[0, rows, :] = 0.5 * right_in_ref[0, rows, :] + 0.5 * sums[at]
        grad_ref[0, :, rows] = grads[at].astype(jnp.float32)


def right_statistics_new(info, pieces, other_cols, right_in, own_rows, split):
    line, first, pair = pieces
    _, lead, rows, width = line.shape
    count = right_in.shape[0]
    half = other_cols.shape[2]
    cols = right_in.shape[2]
    if split:

        def own(m, info_ref):
            return (0, 2 * m + info_ref[4], 0, 0)

        def col(m, info_ref):
            return (info_ref[5], 2 * m + info_ref[6], 0, 0)

    else:

        def own(m, info_ref):
            return (0, m, 0, info_ref[4])

        def col(m, info_ref):
            return (info_ref[5], m, 0, info_ref[6])

    def specs(place_of):
        one = pl.BlockSpec((1, 1, rows, half), place_of)
        two = pl.BlockSpec((2, 1, 1, rows, half), lambda m, info_ref: (0,) + place_of(m, info_ref))
        return [one, one, two]

    return pl.pallas_call(
        right_kernel,
        grid_spec=pltpu.PrefetchScalarGridSpec(
            num_scalar_prefetch=1,
            grid=(count,),
            in_specs=specs(own)
            + specs(col)
            + [
                pl.BlockSpec((1, 4 * rows, half), lambda m, info_ref: (m, 0, 0)),
                pl.BlockSpec((1, 2 * half, cols), lambda m, info_ref: (m, 0, 0)),
            ],
            out_specs=[
                pl.BlockSpec((1, 2 * half, cols), lambda m, info_ref: (m, 0, 0)),
                pl.BlockSpec((1, own_rows, 2 * half), lambda m, info_ref: (m, 0, 0)),
            ],
        ),
        out_shape=(
            jax.ShapeDtypeStruct(right_in.shape, jnp.float32),
            jax.ShapeDtypeStruct((count, own_rows, 2 * half), jnp.float32),
        ),
        compiler_params=pltpu.CompilerParams(vmem_limit_bytes=48 * 1024 * 1024),
        cost_estimate=pl.CostEstimate(flops=1_000_000, bytes_accessed=100_000, transcendentals=0),
    )(info, line, first, pair, line, first, pair, other_cols, right_in)


def shampoo_left(own, received, left_in, weights_in):
    total = own + received.astype(jnp.float32)
    cols = weights_in.shape[2]
    return (
        0.5 * left_in + 0.5 * total[:, :, cols:],
        weights_in - shampoo_rate * (total[:, :, :cols] + shampoo_decay * weights_in),
    )


def halve_kernel(info_ref, weights_ref, mine_ref, theirs_ref):
    core = info_ref[1]
    width = mine_ref.shape[2]
    mine = pl.ds(pl.multiple_of(core * width, width), width)
    theirs = pl.ds(pl.multiple_of((1 - core) * width, width), width)
    mine_ref[...] = weights_ref[:, :, mine].astype(mine_ref.dtype)
    theirs_ref[...] = weights_ref[:, :, theirs].astype(theirs_ref.dtype)


def halve(where, weights):
    count, rows, width = weights.shape
    shape = jax.ShapeDtypeStruct((count, rows, width // 2), jnp.bfloat16)
    return pl.pallas_call(
        halve_kernel,
        grid_spec=pltpu.PrefetchScalarGridSpec(
            num_scalar_prefetch=1,
            grid=(1,),
            in_specs=[pl.BlockSpec(weights.shape, lambda step, info_ref: (0, 0, 0))],
            out_specs=[pl.BlockSpec(shape.shape, lambda step, info_ref: (0, 0, 0))] * 2,
        ),
        out_shape=(shape, shape),
        compiler_params=pltpu.CompilerParams(vmem_limit_bytes=32 * 1024 * 1024),
        cost_estimate=pl.CostEstimate(flops=1_000_000, bytes_accessed=100_000, transcendentals=0),
    )(where, weights)


def unite_kernel(info_ref, mine_ref, other_ref, out_ref):
    core = info_ref[1]
    rows = mine_ref.shape[1]
    out_ref[:, pl.ds(pl.multiple_of(core * rows, rows), rows), :] = mine_ref[...]
    out_ref[:, pl.ds(pl.multiple_of((1 - core) * rows, rows), rows), :] = other_ref[...]


def unite(where, mine, other):
    count, rows, width = mine.shape
    spec = pl.BlockSpec(mine.shape, lambda step, info_ref: (0, 0, 0))
    out = (count, 2 * rows, width)
    return pl.pallas_call(
        unite_kernel,
        grid_spec=pltpu.PrefetchScalarGridSpec(
            num_scalar_prefetch=1,
            grid=(1,),
            in_specs=[spec, spec],
            out_specs=pl.BlockSpec(out, lambda step, info_ref: (0, 0, 0)),
        ),
        out_shape=jax.ShapeDtypeStruct(out, mine.dtype),
        compiler_params=pltpu.CompilerParams(vmem_limit_bytes=32 * 1024 * 1024),
        cost_estimate=pl.CostEstimate(flops=1_000_000, bytes_accessed=100_000, transcendentals=0),
    )(where, mine, other)


def knn_kernel(
    info_ref, blend_ref, gaps_ref, ids_ref, targets_ref, logprob_ref, lm_ref, cot_ref, sums_ref
):
    step = pl.program_id(0)
    chip = info_ref[0]
    log_temperature = blend_ref[0:1, 0:1]
    sharpness_divisor = jnp.exp(log_temperature)
    interp = 1.0 / (1.0 + jnp.exp(-blend_ref[0:1, 1:2]))
    gaps = gaps_ref[...]
    logits = -gaps / sharpness_divisor
    near_exp = jnp.exp(logits - jnp.max(logits, axis=1, keepdims=True))
    mass = jnp.sum(near_exp, axis=1, keepdims=True)
    hits = ids_ref[...] == targets_ref[...]
    hit_exp = jnp.where(hits, near_exp, 0.0)
    retrieval = jnp.sum(hit_exp, axis=1, keepdims=True) / mass
    hit_gaps = jnp.sum(hit_exp * gaps, axis=1, keepdims=True) / mass
    all_gaps = jnp.sum(near_exp * gaps, axis=1, keepdims=True) / mass
    temp_terms = (hit_gaps - retrieval * all_gaps) / sharpness_divisor
    lm_prob = jnp.exp(logprob_ref[...])
    mixture = interp * retrieval + (1.0 - interp) * lm_prob
    lm_weight = -(1.0 - interp) * lm_prob / mixture
    temp_grad = jnp.sum(-(interp / mixture) * temp_terms, axis=0, keepdims=True)
    interp_grad = jnp.sum(
        -interp * (1.0 - interp) * (retrieval - lm_prob) / mixture, axis=0, keepdims=True
    )
    loss = jnp.sum(-jnp.log(mixture), axis=0, keepdims=True)
    lane = lax.broadcasted_iota(jnp.int32, sums_ref.shape, 1)
    sums = jnp.where(lane == 0, temp_grad, jnp.where(lane == 1, interp_grad, 0.0))
    sums = jnp.where(lane == 2, loss, sums)

    @pl.when(step == 0)
    def _():
        sums_ref[...] = jnp.zeros_like(sums_ref)

    sums_ref[...] += sums
    block = lm_ref.shape[1] // 4
    for rel in range(4):
        start = pl.multiple_of((chip ^ rel) * block, block)
        part = lm_weight * lm_ref[:, pl.ds(start, block)].astype(jnp.float32)
        cot_ref[:, rel * block : (rel + 1) * block] = part.astype(cot_ref.dtype)


def neighbours(where, blend, gaps, ids, targets, logprob, lm_grad):
    rows, width = gaps.shape
    step_rows = rows // 3
    wide = pl.BlockSpec((step_rows, width), lambda r, info_ref: (r, 0))
    thin = pl.BlockSpec((step_rows, 1), lambda r, info_ref: (r, 0))
    cot, sums = pl.pallas_call(
        knn_kernel,
        grid_spec=pltpu.PrefetchScalarGridSpec(
            num_scalar_prefetch=1,
            grid=(3,),
            in_specs=[
                pl.BlockSpec((1, 2), lambda r, info_ref: (0, 0)),
                wide,
                wide,
                thin,
                thin,
                wide,
            ],
            out_specs=[wide, pl.BlockSpec((8, width), lambda r, info_ref: (0, 0))],
        ),
        out_shape=(
            jax.ShapeDtypeStruct((rows, width), jnp.bfloat16),
            jax.ShapeDtypeStruct((8, width), jnp.float32),
        ),
        compiler_params=pltpu.CompilerParams(vmem_limit_bytes=32 * 1024 * 1024),
        cost_estimate=pl.CostEstimate(flops=1_000_000, bytes_accessed=100_000, transcendentals=0),
    )(where, blend[None], gaps, ids, targets[:, None], logprob[:, None], lm_grad)
    return cot, sums[:1]


def normalize_kernel(info_ref, pair_ref, far_ref, params_ref, out_ref, own_ref):
    step = pl.program_id(0)
    chip = info_ref[0]
    block = out_ref.shape[1] // 4

    def work(rows_ref):
        values_in = rows_ref[...].astype(jnp.float32)
        centre = jnp.mean(values_in, axis=-1, keepdims=True)
        spread_sq = jnp.mean((values_in - centre) ** 2, axis=-1, keepdims=True)
        scale = lax.rsqrt(spread_sq + norm_eps)
        for rel in range(4):
            start = pl.multiple_of((chip ^ rel) * block, block)
            own = slice(rel * block, (rel + 1) * block)
            part = rows_ref[:, pl.ds(start, block)].astype(jnp.float32)
            normed = (part - centre) * scale * params_ref[0:1, own] + params_ref[1:2, own]
            out_ref[:, own] = normed.astype(out_ref.dtype)

    @pl.when(step < 2)
    def _():
        work(pair_ref)

    @pl.when(step >= 2)
    def _():
        work(far_ref)

    @pl.when(step == 0)
    def _():
        for rel in range(4):
            start = pl.multiple_of((chip ^ rel) * block, block)
            own_ref[:, rel * block : (rel + 1) * block] = pair_ref[:, pl.ds(start, block)]


def normalize(where, pair, far, params):
    rows, width = pair.shape
    step_rows = rows // 2
    pair_spec = pl.BlockSpec((step_rows, width), lambda r, info_ref: (jnp.minimum(r, 1), 0))
    far_spec = pl.BlockSpec((step_rows, width), lambda r, info_ref: (jnp.maximum(r - 2, 0), 0))
    return pl.pallas_call(
        normalize_kernel,
        grid_spec=pltpu.PrefetchScalarGridSpec(
            num_scalar_prefetch=1,
            grid=(4,),
            in_specs=[
                pair_spec,
                far_spec,
                pl.BlockSpec(params.shape, lambda r, info_ref: (0, 0)),
            ],
            out_specs=[
                pl.BlockSpec((step_rows, width), lambda r, info_ref: (r, 0)),
                pl.BlockSpec((step_rows, width), lambda r, info_ref: (0, 0)),
            ],
        ),
        out_shape=(
            jax.ShapeDtypeStruct((2 * rows, width), pair.dtype),
            jax.ShapeDtypeStruct((step_rows, width), pair.dtype),
        ),
        compiler_params=pltpu.CompilerParams(vmem_limit_bytes=32 * 1024 * 1024),
        cost_estimate=pl.CostEstimate(flops=1_000_000, bytes_accessed=100_000, transcendentals=0),
    )(where, pair, far, params)


def norm_back_kernel(
    info_ref, own_ref, near_ref, rows_ref, later_ref, gain_ref, out_ref, sums_ref
):
    chip = info_ref[0]
    grads = own_ref[...] + near_ref[...].astype(jnp.float32)
    values_in = rows_ref[...].astype(jnp.float32)
    centred = values_in - jnp.mean(values_in, axis=-1, keepdims=True)
    spread_sq = jnp.mean(centred * centred, axis=-1, keepdims=True)
    scale = lax.rsqrt(spread_sq + norm_eps)
    normed = centred * scale
    sums_ref[0:1, :] = jnp.sum(grads * normed, axis=0, keepdims=True)
    sums_ref[1:2, :] = jnp.sum(grads, axis=0, keepdims=True)
    sloped = grads * gain_ref[0:1, :]
    along = jnp.mean(sloped * normed, axis=-1, keepdims=True)
    back = (sloped - jnp.mean(sloped, axis=-1, keepdims=True) - normed * along) * scale
    result = (later_ref[...] + back).astype(out_ref.dtype)
    block = out_ref.shape[1] // 4
    for rel in range(4):
        start = pl.multiple_of((chip ^ rel) * block, block)
        out_ref[:, pl.ds(start, block)] = result[:, rel * block : (rel + 1) * block]


def norm_back(where, own, near, rows_low, later, gain):
    rows, width = own.shape

    def whole(shape):
        return pl.BlockSpec(shape, lambda step, info_ref: (0, 0))

    return pl.pallas_call(
        norm_back_kernel,
        grid_spec=pltpu.PrefetchScalarGridSpec(
            num_scalar_prefetch=1,
            grid=(1,),
            in_specs=[whole(own.shape)] * 4 + [whole((1, width))],
            out_specs=[whole(own.shape), whole((2, width))],
        ),
        out_shape=(
            jax.ShapeDtypeStruct((rows, width), jnp.bfloat16),
            jax.ShapeDtypeStruct((2, width), jnp.float32),
        ),
        compiler_params=pltpu.CompilerParams(vmem_limit_bytes=40 * 1024 * 1024),
        cost_estimate=pl.CostEstimate(flops=1_000_000, bytes_accessed=100_000, transcendentals=0),
    )(where, own, near, rows_low, later, gain)


def ffn_kernel(normed_a, normed_b, cot_a, cot_b, up_ref, down_ref, act_ref, grad_ref):
    def work(normed_ref, cot_ref):
        pre = jnp.dot(normed_ref[...], up_ref[0], preferred_element_type=jnp.float32)
        grad_act = jnp.dot(cot_ref[...], down_ref[0], preferred_element_type=jnp.float32)
        scale = 0.7978845608028654
        square = pre * pre
        turn = jnp.tanh(pre * (scale + (scale * 0.044715) * square))
        gate = 0.5 + 0.5 * turn
        act_ref[...] = (pre * gate).astype(jnp.bfloat16)
        slope = gate + 0.5 * pre * (1.0 - turn * turn) * (scale + (3.0 * scale * 0.044715) * square)
        grad_ref[...] = (grad_act * slope).astype(jnp.bfloat16)

    @pl.when(pl.program_id(1) < 2)
    def _():
        work(normed_a, cot_a)

    @pl.when(pl.program_id(1) >= 2)
    def _():
        work(normed_b, cot_b)


def ffn_middle(normed, cot, weights):
    rows, width = normed[0].shape
    hidden = weights.shape[2]
    step_rows, step_cols = rows // 2, hidden // 2
    pair_spec = pl.BlockSpec((step_rows, width), lambda f, r: (jnp.minimum(r, 1), 0))
    far_spec = pl.BlockSpec((step_rows, width), lambda f, r: (jnp.maximum(r - 2, 0), 0))
    up_spec = pl.BlockSpec((1, width, step_cols), lambda f, r: (0, 0, f))
    down_spec = pl.BlockSpec((1, width, step_cols), lambda f, r: (1, 0, f))
    out_spec = pl.BlockSpec((step_rows, step_cols), lambda f, r: (r, f))
    shape = jax.ShapeDtypeStruct((2 * rows, hidden), jnp.bfloat16)
    return pl.pallas_call(
        ffn_kernel,
        grid=(2, 4),
        in_specs=[pair_spec, far_spec, pair_spec, far_spec, up_spec, down_spec],
        out_specs=[out_spec, out_spec],
        out_shape=(shape, shape),
        compiler_params=pltpu.CompilerParams(vmem_limit_bytes=48 * 1024 * 1024),
        cost_estimate=pl.CostEstimate(flops=1_000_000, bytes_accessed=100_000, transcendentals=0),
    )(*normed, *cot, weights, weights)


def masked_heads(values_in, lanes, head, scale):
    keep = (lanes >= head * HEAD_DIM) & (lanes < (head + 1) * HEAD_DIM)
    return jnp.where(keep, values_in * scale, jnp.zeros_like(values_in))


def in_order(info_ref, source, held, rows):
    for piece in range(4):
        start = pl.multiple_of((info_ref[0] ^ piece) * rows, rows)
        held[piece * rows : (piece + 1) * rows, :] = source(pl.ds(start, rows))


def out_of_order(info_ref, held, store, rows):
    for piece in range(4):
        start = pl.multiple_of((info_ref[0] ^ piece) * rows, rows)
        store(pl.ds(start, rows), held[piece * rows : (piece + 1) * rows, :])


def block_bias(info_ref, query, key):
    return jnp.where(info_ref[1 + query] <= key * SHORT, 0.0, -1e30).astype(jnp.float32)


def forward_kernel(info_ref, qkv_ref, out_ref, query_held, key_held, value_held, out_held):
    rows = qkv_ref.shape[1] // 4
    for part, held in enumerate((query_held, key_held, value_held)):
        in_order(info_ref, lambda at, part=part: qkv_ref[part, at, :], held, rows)
    lanes = lax.broadcasted_iota(jnp.int32, (SHORT, 128), 1)
    earlier = lax.broadcasted_iota(jnp.int32, (SHORT, SHORT), 1) <= lax.broadcasted_iota(
        jnp.int32, (SHORT, SHORT), 0
    )
    for query in range(qkv_ref.shape[1] // SHORT):
        query_rows = query_held[query * SHORT : (query + 1) * SHORT, :]
        outs = []
        for head in range(2):
            query_head = masked_heads(query_rows, lanes, head, HEAD_DIM**-0.5)
            scores, biases = [], []
            for key in range(query + 1):
                score = lax.dot_general(
                    query_head,
                    key_held[key * SHORT : (key + 1) * SHORT, :],
                    (((1,), (1,)), ((), ())),
                    preferred_element_type=jnp.float32,
                )
                scores.append(jnp.where(earlier, score, -1e30) if key == query else score)
                biases.append(block_bias(info_ref, query, key))
            top = scores[query].max(axis=1, keepdims=True)
            for score, bias in zip(scores[:query], biases):
                top = jnp.maximum(top, score.max(axis=1, keepdims=True) + bias)
            mass = jnp.zeros_like(top)
            total = jnp.zeros((SHORT, 128), jnp.float32)
            for key in range(query + 1):
                chance = jnp.exp(scores[key] - (top - biases[key]))
                mass = mass + chance.sum(axis=1, keepdims=True)
                total = total + jnp.dot(
                    chance.astype(jnp.bfloat16),
                    value_held[key * SHORT : (key + 1) * SHORT, :],
                    preferred_element_type=jnp.float32,
                )
            outs.append(total / mass)
        out = jnp.where(lanes < HEAD_DIM, outs[0], outs[1])
        out_held[query * SHORT : (query + 1) * SHORT, :] = out.astype(jnp.bfloat16)

    def store(at, values_in):
        out_ref[at, :] = values_in

    out_of_order(info_ref, out_held, store, rows)


def backward_kernel(
    info_ref,
    qkv_ref,
    grad_ref,
    out_ref,
    query_held,
    key_held,
    value_held,
    grad_held,
    key_turned,
    query_grad,
    key_grad,
    value_grad,
):
    rows = qkv_ref.shape[1] // 4
    for part, held in enumerate((query_held, key_held, value_held)):
        in_order(info_ref, lambda at, part=part: qkv_ref[part, at, :], held, rows)
    in_order(info_ref, lambda at: grad_ref[at, :], grad_held, rows)
    key_turned[...] = key_held[...].astype(jnp.float32).T.astype(jnp.bfloat16)
    lanes = lax.broadcasted_iota(jnp.int32, (SHORT, 128), 1)
    earlier = lax.broadcasted_iota(jnp.int32, (SHORT, SHORT), 0) <= lax.broadcasted_iota(
        jnp.int32, (SHORT, SHORT), 1
    )
    blocks = qkv_ref.shape[1] // SHORT
    for query in range(blocks):
        at_query = slice(query * SHORT, (query + 1) * SHORT)
        query_rows = query_held[at_query, :]
        grad_rows = grad_held[at_query, :]
        turned_grads = []
        for head in range(2):
            query_head = masked_heads(query_rows, lanes, head, HEAD_DIM**-0.5)
            grad_head = masked_heads(grad_rows, lanes, head, 1.0)
            scores, biases = [], []
            for key in range(query + 1):
                score = lax.dot_general(
                    key_held[key * SHORT : (key + 1) * SHORT, :],
                    query_head,
                    (((1,), (1,)), ((), ())),
                    preferred_element_type=jnp.float32,
                )
                scores.append(jnp.where(earlier, score, -1e30) if key == query else score)
                biases.append(block_bias(info_ref, query, key))
            top = scores[query].max(axis=0, keepdims=True)
            for score, bias in zip(scores[:query], biases):
                top = jnp.maximum(top, score.max(axis=0, keepdims=True) + bias)
            mass = jnp.zeros_like(top)
            inner = jnp.zeros_like(top)
            chances, slopes = [], []
            for key in range(query + 1):
                slope = lax.dot_general(
                    value_held[key * SHORT : (key + 1) * SHORT, :],
                    grad_head,
                    (((1,), (1,)), ((), ())),
                    preferred_element_type=jnp.float32,
                )
                chance = jnp.exp(scores[key] - (top - biases[key]))
                mass = mass + chance.sum(axis=0, keepdims=True)
                inner = inner + (chance * slope).sum(axis=0, keepdims=True)
                chances.append(chance)
                slopes.append(slope)
            share = 1.0 / mass
            inner = inner * share
            total = None
            for key in range(query + 1):
                at_key = slice(key * SHORT, (key + 1) * SHORT)
                probs = chances[key] * share
                grad_scores = (probs * (slopes[key] - inner)).astype(jnp.bfloat16)
                value_part = jnp.dot(
                    probs.astype(jnp.bfloat16), grad_head, preferred_element_type=jnp.float32
                )
                key_part = jnp.dot(grad_scores, query_head, preferred_element_type=jnp.float32)
                if head == 0 and key == query:
                    value_grad[at_key, :] = value_part
                    key_grad[at_key, :] = key_part
                else:
                    value_grad[at_key, :] += value_part
                    key_grad[at_key, :] += key_part
                part = jnp.dot(
                    key_turned[head * HEAD_DIM : (head + 1) * HEAD_DIM, at_key],
                    grad_scores,
                    preferred_element_type=jnp.float32,
                )
                total = part if total is None else total + part
            turned_grads.append(total)
        turned = jnp.concatenate(turned_grads, axis=0)
        query_grad[at_query, :] = turned.T * (HEAD_DIM**-0.5)

    for part, held in enumerate((query_grad, key_grad, value_grad)):

        def store(at, values_in, part=part):
            out_ref[part, at, :] = values_in.astype(jnp.bfloat16)

        out_of_order(info_ref, held, store, rows)


def attend(info, qkv):
    _, rows, width = qkv.shape
    held = pltpu.VMEM((rows, 128), jnp.bfloat16)
    return pl.pallas_call(
        forward_kernel,
        grid_spec=pltpu.PrefetchScalarGridSpec(
            num_scalar_prefetch=1,
            grid=(width // 128,),
            in_specs=[pl.BlockSpec((3, rows, 128), lambda pair, info_ref: (0, 0, pair))],
            out_specs=pl.BlockSpec((rows, 128), lambda pair, info_ref: (0, pair)),
            scratch_shapes=[held] * 4,
        ),
        out_shape=jax.ShapeDtypeStruct((rows, width), jnp.bfloat16),
        compiler_params=pltpu.CompilerParams(vmem_limit_bytes=48 * 1024 * 1024),
        cost_estimate=pl.CostEstimate(flops=1_000_000, bytes_accessed=100_000, transcendentals=0),
    )(info, qkv)


def attend_back(info, qkv, grad_heads, pair, earlier):
    _, rows, width = qkv.shape
    extra = [] if earlier is None else [pl.BlockSpec(memory_space=pl.ANY)]

    def kernel(info_ref, qkv_ref, grad_ref, *others):
        backward_kernel(info_ref, qkv_ref, grad_ref, *others[len(extra) :])

    return pl.pallas_call(
        kernel,
        grid_spec=pltpu.PrefetchScalarGridSpec(
            num_scalar_prefetch=1,
            grid=(1,),
            in_specs=[
                pl.BlockSpec((3, rows, 128), lambda step, info_ref: (0, 0, pair)),
                pl.BlockSpec((rows, 128), lambda step, info_ref: (0, pair)),
            ]
            + extra,
            out_specs=pl.BlockSpec((3, rows, 128), lambda step, info_ref: (0, 0, pair)),
            scratch_shapes=[pltpu.VMEM((rows, 128), jnp.bfloat16)] * 4
            + [pltpu.VMEM((128, rows), jnp.bfloat16)]
            + [pltpu.VMEM((rows, 128), jnp.float32)] * 3,
        ),
        out_shape=jax.ShapeDtypeStruct(qkv.shape, jnp.bfloat16),
        input_output_aliases={} if earlier is None else {3: 0},
        compiler_params=pltpu.CompilerParams(vmem_limit_bytes=48 * 1024 * 1024),
        cost_estimate=pl.CostEstimate(flops=1_000_000, bytes_accessed=100_000, transcendentals=0),
    )(info, qkv, grad_heads, *([] if earlier is None else [earlier]))


def regrouped(
    tokens_in,
    lm_grad,
    lm_logprob,
    targets,
    neighbor_ids,
    nearby_entry_gaps,
    seq_lengths,
    attn_weights,
    ffn_weights,
    attn_left,
    attn_right,
    ffn_left,
    ffn_right,
    attn_left_root,
    attn_right_root,
    ffn_left_root,
    ffn_right_root,
    norm_params,
    norm_moment1,
    norm_moment2,
    blending_coefficients,
    knn_moment1,
    knn_moment2,
):
    low = jnp.bfloat16
    rows = tokens_in.shape[0]
    group_rows = 4 * rows
    dp_index, tensor_index = lax.axis_index("dp"), lax.axis_index("tensor")
    place = {
        "line": tensor_index & 1,
        "half": tensor_index >> 1,
        "core": dp_index & 1,
        "x": (dp_index >> 1) & 1,
        "y": dp_index >> 2,
        "chip": dp_index >> 1,
    }
    me = place["core"] * 2 + place["line"]
    chip, core = place["chip"], place["core"]
    staying = core == place["half"]

    where = jnp.stack(
        [
            chip,
            core,
            tensor_index,
            place["line"],
            place["half"],
            place["line"] ^ place["x"],
            place["y"],
        ]
    ).astype(jnp.int32)
    tokens_one = swap_or_near(tokens_in)
    wa_mine, wa_theirs = halve(where, attn_weights)
    wa = unite(where, wa_mine, flip(wa_theirs, CORE_BIT))
    wa, ffn_weights_in, nearby_entry_gaps, lengths_in = together(
        wa, ffn_weights, nearby_entry_gaps, seq_lengths
    )
    wa_other = flip(wa, HALF_BIT)
    wf_mine, wf_theirs = halve(where, ffn_weights_in)
    wf = unite(where, wf_mine, flip(wf_theirs, CORE_BIT))
    other_lengths = flip(lengths_in.astype(jnp.float32), CORE_BIT).astype(jnp.int32)
    lengths = jnp.where(staying, seq_lengths, other_lengths)
    params = by_chip(norm_params, chip)
    block_begins = first_blocks(lengths, group_rows, SHORT) * SHORT
    info = jnp.concatenate([me[None].astype(jnp.int32), block_begins.astype(jnp.int32)])
    cot_low, knn_sums = neighbours(
        where,
        blending_coefficients,
        nearby_entry_gaps,
        neighbor_ids,
        targets,
        lm_logprob,
        lm_grad,
    )
    tokens_one, wf, params, info, wa_other, cot_low = together(
        tokens_one, wf, params, info, wa_other, cot_low
    )
    tokens_two = near_of_moved(tokens_one)
    wa = weight_halves(wa, wa_other, place)
    wa_first = cross_one(wa)
    wf_other = flip(wf, HALF_BIT)
    tokens_one, tokens_two, wa_first, cot_low = together(tokens_one, tokens_two, wa_first, cot_low)
    pair1 = jnp.concatenate(
        [
            jnp.where(staying, tokens_in, tokens_one),
            jnp.where(staying, tokens_one, tokens_two),
        ],
        axis=0,
    )
    far1 = flip(pair1, CORE_BIT)
    wa_pair = cross_two(jnp.stack([wa, wa_first]))
    cot_one = swap_or_near(cot_low)
    far1, pair1 = together(far1, pair1)
    normed1_all, own_low = normalize(where, pair1, far1, params)
    resid = own_low.astype(jnp.float32)
    normed1_all, wa_pair = together(normed1_all, wa_pair)
    wa_all = by_rel(core, wa, wa_first, wa_pair, 1)
    proj_in, proj_out = wa_all[:3], wa_all[3]

    qkv = dot32("rd,sdc->src", normed1_all, proj_in).astype(low)
    heads_flat = attend(info, qkv)
    heads_flat, wf_other, wf, cot_one = together(heads_flat, wf_other, wf, cot_one)

    def out_rows(a, b):
        return dot32("rc,dc->rd", heads_flat[a:b], proj_out)

    sent4 = out_rows(2 * rows, 4 * rows).astype(low)
    sent4, wf, heads_flat = together(sent4, weight_halves(wf, wf_other, place), heads_flat)
    received4 = flip(sent4, CORE_BIT)
    wf_first = cross_one(wf)
    near4 = (out_rows(rows, 2 * rows) + received4[rows:].astype(jnp.float32)).astype(low)
    near4, heads_flat = together(near4, heads_flat)
    from_near4 = flip(near4, LINE_BIT)
    attn_out = out_rows(0, rows) + received4[:rows].astype(jnp.float32)
    attn_out, cot_one = together(attn_out, cot_one)
    cot_two = near_of_moved(cot_one)
    attn_out, from_near4, wf_first = together(attn_out, from_near4, wf_first)
    middle = resid + attn_out + from_near4.astype(jnp.float32)
    normed2, norm2_back = jax.vjp(layer_norm, middle, params[2], params[3])
    normed2_low = normed2.astype(low)
    near2 = flip(normed2_low, LINE_BIT)
    wf_pair = cross_two(jnp.stack([wf, wf_first]))
    near2, cot_one, cot_two, normed2_low = together(near2, cot_one, cot_two, normed2_low)
    cot_moved = jnp.where(staying, cot_low, cot_one)
    pair_cot = jnp.concatenate([cot_moved, jnp.where(staying, cot_one, cot_two)], axis=0)
    cotangent = cot_moved.astype(jnp.float32)
    pair2 = jnp.concatenate([normed2_low, near2], axis=0)
    far2 = flip(pair2, CORE_BIT)
    far_cot = flip(pair_cot, CORE_BIT)
    wf_all = by_rel(core, wf, wf_first, wf_pair, 1)

    far2, wf_all = together(far2, wf_all)
    act_low, grad_pre_low = ffn_middle((pair2, far2), (pair_cot, far_cot), wf_all)

    def back_rows(a, b):
        return dot32("rf,df->rd", grad_pre_low[a:b], wf_all[0])

    sent2 = back_rows(2 * rows, 4 * rows).astype(low)
    sent2, pair2, far2, pair_cot, far_cot, act_low = together(
        sent2, pair2, far2, pair_cot, far_cot, act_low
    )
    normed2_all = jnp.concatenate([pair2, far2], axis=0)
    cot_all = jnp.concatenate([pair_cot, far_cot], axis=0)
    received2 = flip(sent2, CORE_BIT)
    cut = ffn_weights.shape[2] // 2
    up_halves = [
        dot32("rd,rf->df", normed2_all, grad_pre_low[:, :cut]).astype(low),
        dot32("rd,rf->df", normed2_all, grad_pre_low[:, cut:]).astype(low),
    ]
    up_kept, up_sent = scatter_parts(core, up_halves)
    up_got = cross_one(up_sent)
    near2 = back_rows(rows, 2 * rows) + received2[rows:].astype(jnp.float32)
    near2, act_low = together(near2.astype(low), act_low)
    from_near2 = flip(near2, LINE_BIT)
    own2 = back_rows(0, rows) + received2[:rows].astype(jnp.float32)
    down_halves = [
        dot32("rd,rf->df", cot_all, act_low[:, :cut]).astype(low),
        dot32("rd,rf->df", cot_all, act_low[:, cut:]).astype(low),
    ]
    down_kept, down_sent = scatter_parts(core, down_halves)
    down_got = cross_one(down_sent)
    own2, from_near2 = together(own2, from_near2)
    grad_normed2 = own2 + from_near2.astype(jnp.float32)
    mid_norm_grad, gain2_grad, shift2_grad = norm2_back(grad_normed2)
    grad_middle = cotangent + mid_norm_grad
    mid_low, act_low = together(grad_middle.astype(low), act_low)
    near_mid = flip(mid_low, LINE_BIT)
    out_sent = dot32("rf,df->rd", act_low[2 * rows :], wf_all[1]).astype(low)
    up_got, down_got, out_sent, act_low = together(up_got, down_got, out_sent, act_low)
    ffn_kept = jnp.concatenate([add_low(up_kept, up_got), add_low(down_kept, down_got)], axis=0)
    ffn_got = cross_two(ffn_kept[:, 1])
    out_received = flip(out_sent, CORE_BIT)
    out_near = dot32("rf,df->rd", act_low[rows : 2 * rows], wf_all[1]) + out_received[rows:].astype(
        jnp.float32
    )
    ffn_out = dot32("rf,df->rd", act_low[:rows], wf_all[1]) + out_received[:rows].astype(jnp.float32)
    near_mid, ffn_got, out_near, ffn_out, mid_low = together(
        near_mid, ffn_got, out_near.astype(low), ffn_out, mid_low
    )
    pair_mid = jnp.concatenate([mid_low, near_mid], axis=0)
    far_mid = flip(pair_mid, CORE_BIT)
    ffn_part = add_low(ffn_kept[:, 0], ffn_got)
    ffn_other = flip(ffn_part, HALF_BIT)
    out_from_near = flip(out_near, LINE_BIT)

    grad_heads = jnp.concatenate(
        [dot32("rd,dc->rc", part, proj_out).astype(low) for part in (pair_mid, far_mid)], axis=0
    )
    grad_half = attend_back(info, qkv, grad_heads, 0, None)
    grad_half, pair_mid, far_mid = together(grad_half, pair_mid, far_mid)
    grad_out_proj = dot32("rd,rc->dc", pair_mid, heads_flat[: 2 * rows]) + dot32(
        "rd,rc->dc", far_mid, heads_flat[2 * rows :]
    )
    grad_out_proj = grad_out_proj.astype(low)
    grad_qkv = attend_back(info, qkv, grad_heads, 1, grad_half)
    grad_qkv, grad_out_proj = together(grad_qkv, grad_out_proj)

    def back_in(a, b):
        return dot32("src,sdc->rd", grad_qkv[:, a:b], proj_in)

    grad_parts = [
        dot32("rd,rc->dc", normed1_all, grad_qkv[part]).astype(low) for part in range(3)
    ] + [grad_out_proj]
    attn_kept, attn_sent = scatter_parts(core, grad_parts)
    sent1 = back_in(2 * rows, 4 * rows).astype(low)
    attn_kept, attn_sent, sent1, grad_qkv, ffn_other, out_from_near = together(
        attn_kept, attn_sent, sent1, grad_qkv, ffn_other, out_from_near
    )

    attn_got = cross_one(attn_sent)
    received1 = flip(sent1, CORE_BIT)
    ffn_own = add_low(ffn_part, ffn_other)
    ffn_near = flip(ffn_own, LINE_BIT)
    near3 = back_in(rows, 2 * rows) + received1[rows:].astype(jnp.float32)
    near3, grad_qkv = together(near3.astype(low), grad_qkv)
    from_near3 = flip(near3, LINE_BIT)
    own3 = back_in(0, rows) + received1[:rows].astype(jnp.float32)
    attn_got, attn_kept, own3, ffn_out = together(attn_got, attn_kept, own3, ffn_out)

    attn_kept = add_low(attn_kept, attn_got)
    attn_kept, own3, ffn_out = together(attn_kept, own3, ffn_out)
    attn_got = cross_two(attn_kept[:, 1])
    ffn_out = ffn_out + out_from_near.astype(jnp.float32)
    mixed = by_chip((middle + ffn_out).astype(low), chip)
    attn_got, attn_kept, own3, ffn_near, ffn_own, mixed = together(
        attn_got, attn_kept, own3, ffn_near, ffn_own, mixed
    )

    attn_part = add_low(attn_kept[:, 0], attn_got)
    ffn_line = jnp.stack([ffn_own, ffn_near])
    attn_part, own3, ffn_line, mixed = together(attn_part, own3, ffn_line, mixed)
    attn_other = flip(attn_part, HALF_BIT)
    ffn_first = cross_one(ffn_line)
    attn_other, attn_part, ffn_first, ffn_line, own3, mixed = together(
        attn_other, attn_part, ffn_first, ffn_line, own3, mixed
    )

    attn_own = add_low(attn_part, attn_other)
    ffn_two = jnp.stack([ffn_line, ffn_first])
    attn_own, own3, ffn_two = together(attn_own, own3, ffn_two)
    attn_near = flip(attn_own, LINE_BIT)
    ffn_pair = cross_two(ffn_two)
    input_grad, gain_sums = norm_back(
        where, own3, from_near3, own_low, grad_middle, params[0:1]
    )
    attn_near, attn_own, gain_sums, input_grad, mixed = together(
        attn_near, attn_own, gain_sums, input_grad, mixed
    )

    attn_line = jnp.stack([attn_own, attn_near])
    norm_grads = jnp.concatenate([gain_sums, gain2_grad[None], shift2_grad[None]], axis=0)
    small = jnp.concatenate([by_chip(norm_grads, chip), knn_sums], axis=0)
    left_low = jnp.concatenate([attn_left_root.astype(low), ffn_left_root.astype(low)], axis=0)
    left_low = jnp.concatenate([left_low, flip(left_low, CORE_BIT)], axis=1)
    attn_line, small, attn_left_low, ffn_left_low, mixed, input_grad = together(
        attn_line, small, left_low[:4], left_low[4:], mixed, input_grad
    )
    attn_first = cross_one(attn_line)
    mixed = swap_core_half(mixed)
    input_grad = swap_core_half(input_grad)
    small = small + flip(small, CORE_BIT)
    attn_first, attn_line, small, mixed, input_grad = together(
        attn_first, attn_line, small, mixed, input_grad
    )

    attn_pair = cross_two(jnp.stack([attn_line, attn_first]))
    small = small + flip(small, HALF_BIT)
    ffn_pair, small = together(ffn_pair, small)
    small = small + flip(small, LINE_BIT)
    ffn_pieces = (ffn_line, ffn_first, ffn_pair)
    ffn_own, ffn_sent = updates(where, ffn_left_low, ffn_pieces, ffn_right_root, True)
    attn_pair, attn_first, attn_line, ffn_own, ffn_sent, ffn_line, ffn_first, ffn_pair, small = (
        together(
            attn_pair,
            attn_first,
            attn_line,
            ffn_own,
            ffn_sent,
            ffn_line,
            ffn_first,
            ffn_pair,
            small,
        )
    )

    ffn_pieces = (ffn_line, ffn_first, ffn_pair)
    attn_pieces = (attn_line, attn_first, attn_pair)
    attn_cols = column_block(attn_pieces, None, place["half"], False, core)
    ffn_cols = column_block(ffn_pieces, None, place["half"], True, core)
    attn_cols_other = flip(attn_cols, CORE_BIT)
    ffn_cols_other = flip(ffn_cols, CORE_BIT)
    ffn_received = flip(ffn_sent, CORE_BIT)
    attn_own, attn_sent = updates(where, attn_left_low, attn_pieces, attn_right_root, False)
    small = small + flip(small, X_BIT)
    attn_sent, small = together(attn_sent, small)
    attn_received = flip(attn_sent, CORE_BIT)
    summed = small + flip(small, Y_BIT)
    ffn_right_new, ffn_grad = right_statistics_new(
        where, ffn_pieces, ffn_cols_other, ffn_right, ffn_weights.shape[1], True
    )
    attn_right_new, attn_grad = right_statistics_new(
        where, attn_pieces, attn_cols_other, attn_right, attn_weights.shape[1], False
    )
    summed, ffn_right_new, attn_right_new = together(summed, ffn_right_new, attn_right_new)
    ffn_left_new, ffn_new = shampoo_left(ffn_own, ffn_received, ffn_left, ffn_weights)
    attn_left_new, attn_new = shampoo_left(attn_own, attn_received, attn_left, attn_weights)
    input_grad = input_grad.astype(jnp.float32)
    norm_total = summed[:4]
    knn_total = summed[4, :2]
    loss = summed[4, 2] / (group_rows * 8)
    norm_m1, norm_m2, norm_new = adamw_step(norm_params, norm_total, norm_moment1, norm_moment2)
    knn_m1, knn_m2, knn_new = adamw_step(blending_coefficients, knn_total, knn_moment1, knn_moment2)
    return (
        mixed,
        input_grad,
        loss,
        attn_grad,
        attn_left_new,
        attn_right_new,
        attn_new,
        ffn_grad,
        ffn_left_new,
        ffn_right_new,
        ffn_new,
        norm_m1,
        norm_m2,
        norm_new,
        knn_m1,
        knn_m2,
        knn_new,
    )


def solution(mesh):
    sized = (mesh.shape["dp"], mesh.shape["tensor"]) == (8, 4)
    placed = (
        P(("dp", "tensor"), None),
        P(("dp", "tensor"), None),
        P(("dp", "tensor")),
        P(("dp", "tensor")),
        P(("dp", "tensor"), None),
        P(("dp", "tensor"), None),
        P("dp", None),
        P(None, "dp", "tensor"),
        P(None, "dp", "tensor"),
        P(None, "dp", "tensor"),
        P(None, "tensor", "dp"),
        P(None, "dp", "tensor"),
        P(None, "tensor", "dp"),
        P(None, "dp", None),
        P(None, None, "tensor"),
        P(None, "dp", None),
        P(None, None, "tensor"),
        P(),
        P(),
        P(),
        P(),
        P(),
        P(),
    )
    return jax.shard_map(
        regrouped if sized else local,
        mesh=mesh,
        in_specs=placed,
        out_specs=(
            P(("dp", "tensor"), None),
            P(("dp", "tensor"), None),
            P(),
            P(None, "dp", "tensor"),
            P(None, "dp", "tensor"),
            P(None, "tensor", "dp"),
            P(None, "dp", "tensor"),
            P(None, "dp", "tensor"),
            P(None, "dp", "tensor"),
            P(None, "tensor", "dp"),
            P(None, "dp", "tensor"),
            P(),
            P(),
            P(),
            P(),
            P(),
            P(),
        ),
        check_vma=False,
    )
```

```python
import jax
import jax.numpy as jnp
from jax import lax
from jax.experimental import pallas as pl
from jax.experimental.pallas import tpu as pltpu
from jax.sharding import PartitionSpec as P

SHORT = 512
STEP = 10
HEAD_DIM = 64


adam_rate = 0.3
shampoo_rate = 0.5
shampoo_decay = 0.01
norm_eps = 1e-05


def layer_norm(values_in, gain, shift):
    centre = jnp.mean(values_in, axis=-1, keepdims=True)
    centred = values_in - centre
    spread_sq = jnp.mean(centred * centred, axis=-1, keepdims=True)
    return centred * lax.rsqrt(spread_sq + norm_eps) * gain + shift


def gelu_tanh(values_in):
    return jax.nn.gelu(values_in, approximate=True)


def spread_rows(local_low):
    return lax.all_gather(local_low, "tensor", axis=0, tiled=True)


def spread_again(local_low):
    return lax.all_gather(local_low, "tensor", axis=0, tiled=True)


def spread_grads(local_low):
    return lax.all_gather(local_low, "tensor", axis=0, tiled=True)


def branch_total(left_rows, right_mat):
    return lax.psum_scatter(
        jnp.einsum("rc,dc->rd", left_rows, right_mat, preferred_element_type=jnp.float32),
        "tensor",
        scatter_dimension=0,
        tiled=True,
    )


def input_total(left_rows, right_mat):
    return lax.psum_scatter(
        jnp.einsum("rc,dc->rd", left_rows, right_mat, preferred_element_type=jnp.float32),
        "tensor",
        scatter_dimension=0,
        tiled=True,
    )


def first_blocks(seq_lengths, group_rows, block_rows):
    lengths = seq_lengths[0]
    seq_ends = jnp.cumsum(lengths)
    seq_begins = seq_ends - lengths
    block_begins = jnp.arange(group_rows // block_rows, dtype=jnp.int32) * block_rows
    inside = (seq_begins[None, :] <= block_begins[:, None]) & (lengths[None, :] > 0)
    return jnp.max(jnp.where(inside, seq_begins[None, :], 0), axis=1) // block_rows


def block_scores(query_rows, key_rows, query_block, key_block, block_rows, score_scale):
    scores = (
        jnp.einsum("qhd,khd->hqk", query_rows, key_rows, preferred_element_type=jnp.float32)
        * score_scale
    )
    query_pos = query_block * block_rows + jnp.arange(block_rows, dtype=jnp.int32)
    key_pos = key_block * block_rows + jnp.arange(block_rows, dtype=jnp.int32)
    allowed = key_pos[None, :] <= query_pos[:, None]
    return jnp.where(allowed[None], scores, -1e30)


def attend_forward(query_all, key_all, value_all, first_block, block_rows, score_scale):
    group_rows, head_count, head_width = query_all.shape

    def one_block(query_block):
        query_rows = lax.dynamic_slice_in_dim(query_all, query_block * block_rows, block_rows, 0)

        def peak_step(key_block, loop_state):
            running_top, running_mass = loop_state
            key_rows = lax.dynamic_slice_in_dim(key_all, key_block * block_rows, block_rows, 0)
            scores = block_scores(
                query_rows, key_rows, query_block, key_block, block_rows, score_scale
            )
            new_top = jnp.maximum(running_top, jnp.max(scores, axis=2))
            new_mass = running_mass * jnp.exp(running_top - new_top) + jnp.sum(
                jnp.exp(scores - new_top[:, :, None]), axis=2
            )
            return (new_top, new_mass)

        start_state = (
            jnp.full((head_count, block_rows), -1e30, jnp.float32),
            jnp.zeros((head_count, block_rows), jnp.float32),
        )
        final_top, final_mass = lax.fori_loop(
            first_block[query_block], query_block + 1, peak_step, start_state
        )
        log_mass = final_top + jnp.log(final_mass)

        def value_step(key_block, out_acc):
            key_rows = lax.dynamic_slice_in_dim(key_all, key_block * block_rows, block_rows, 0)
            value_rows = lax.dynamic_slice_in_dim(value_all, key_block * block_rows, block_rows, 0)
            scores = block_scores(
                query_rows, key_rows, query_block, key_block, block_rows, score_scale
            )
            attn_probs = jnp.exp(scores - log_mass[:, :, None]).astype(jnp.bfloat16)
            return out_acc + jnp.einsum(
                "hqk,khd->qhd", attn_probs, value_rows, preferred_element_type=jnp.float32
            )

        out_rows = lax.fori_loop(
            first_block[query_block],
            query_block + 1,
            value_step,
            jnp.zeros((block_rows, head_count, head_width), jnp.float32),
        )
        return (out_rows.astype(jnp.bfloat16), log_mass)

    outs, log_masses = lax.map(one_block, jnp.arange(group_rows // block_rows, dtype=jnp.int32))
    return (outs.reshape(group_rows, head_count, head_width), log_masses)


def attend_backward(
    query_all, key_all, value_all, grad_out, log_masses, first_block, block_rows, score_scale
):
    group_rows, head_count, head_width = query_all.shape

    def one_block(query_block, loop_carry):
        grad_keys, grad_values, grad_query = loop_carry
        query_rows = lax.dynamic_slice_in_dim(query_all, query_block * block_rows, block_rows, 0)
        grad_rows = lax.dynamic_slice_in_dim(grad_out, query_block * block_rows, block_rows, 0)
        log_mass = log_masses[query_block]

        def chances(key_block):
            key_rows = lax.dynamic_slice_in_dim(key_all, key_block * block_rows, block_rows, 0)
            value_rows = lax.dynamic_slice_in_dim(value_all, key_block * block_rows, block_rows, 0)
            scores = block_scores(
                query_rows, key_rows, query_block, key_block, block_rows, score_scale
            )
            attn_probs = jnp.exp(scores - log_mass[:, :, None])
            likelihood_cotangent = jnp.einsum(
                "qhd,khd->hqk", grad_rows, value_rows, preferred_element_type=jnp.float32
            )
            return (key_rows, attn_probs, likelihood_cotangent)

        def inner_step(key_block, inner_acc):
            _, attn_probs, likelihood_cotangent = chances(key_block)
            return inner_acc + jnp.sum(attn_probs * likelihood_cotangent, axis=2)

        row_inner = lax.fori_loop(
            first_block[query_block],
            query_block + 1,
            inner_step,
            jnp.zeros((head_count, block_rows), jnp.float32),
        )

        def grad_step(key_block, loop_state):
            query_acc, keys_acc, values_acc = loop_state
            key_rows, attn_probs, likelihood_cotangent = chances(key_block)
            grad_scores = (attn_probs * (likelihood_cotangent - row_inner[:, :, None])).astype(
                jnp.bfloat16
            )
            query_acc = (
                query_acc
                + jnp.einsum(
                    "hqk,khd->qhd", grad_scores, key_rows, preferred_element_type=jnp.float32
                )
                * score_scale
            )
            key_part = (
                jnp.einsum(
                    "hqk,qhd->khd", grad_scores, query_rows, preferred_element_type=jnp.float32
                )
                * score_scale
            )
            value_part = jnp.einsum(
                "hqk,qhd->khd",
                attn_probs.astype(jnp.bfloat16),
                grad_rows,
                preferred_element_type=jnp.float32,
            )
            key_start = key_block * block_rows
            keys_acc = lax.dynamic_update_slice_in_dim(
                keys_acc,
                lax.dynamic_slice_in_dim(keys_acc, key_start, block_rows, 0) + key_part,
                key_start,
                0,
            )
            values_acc = lax.dynamic_update_slice_in_dim(
                values_acc,
                lax.dynamic_slice_in_dim(values_acc, key_start, block_rows, 0) + value_part,
                key_start,
                0,
            )
            return (query_acc, keys_acc, values_acc)

        query_acc, grad_keys, grad_values = lax.fori_loop(
            first_block[query_block],
            query_block + 1,
            grad_step,
            (jnp.zeros((block_rows, head_count, head_width), jnp.float32), grad_keys, grad_values),
        )
        grad_query = lax.dynamic_update_slice_in_dim(
            grad_query, query_acc, query_block * block_rows, 0
        )
        return (grad_keys, grad_values, grad_query)

    zeros_all = jnp.zeros((group_rows, head_count, head_width), jnp.float32)
    return lax.fori_loop(0, group_rows // block_rows, one_block, (zeros_all, zeros_all, zeros_all))


def right_statistics(attn_part_grad, ffn_part_grad, attn_rows, ffn_rows):
    attn_part = jnp.einsum(
        "sri,srj->sij", attn_part_grad, attn_rows, precision=lax.Precision.HIGHEST
    )
    ffn_part = jnp.einsum("sri,srj->sij", ffn_part_grad, ffn_rows, precision=lax.Precision.HIGHEST)
    return (
        lax.psum_scatter(
            attn_part.astype(jnp.bfloat16), "dp", scatter_dimension=2, tiled=True
        ).astype(jnp.float32),
        lax.psum_scatter(
            ffn_part.astype(jnp.bfloat16), "dp", scatter_dimension=2, tiled=True
        ).astype(jnp.float32),
    )


def left_statistics(attn_part_grad, ffn_part_grad, attn_cols, ffn_cols):
    attn_part = jnp.einsum(
        "sri,sqi->srq", attn_part_grad, attn_cols, precision=lax.Precision.HIGHEST
    )
    ffn_part = jnp.einsum("sri,sqi->srq", ffn_part_grad, ffn_cols, precision=lax.Precision.HIGHEST)
    return (
        lax.psum_scatter(
            attn_part.astype(jnp.bfloat16), "tensor", scatter_dimension=2, tiled=True
        ).astype(jnp.float32),
        lax.psum_scatter(
            ffn_part.astype(jnp.bfloat16), "tensor", scatter_dimension=2, tiled=True
        ).astype(jnp.float32),
    )


def adamw_step(params_in, grads_in, first_in, second_in):
    first_new = 0.9 * first_in + 0.1 * grads_in
    second_new = 0.999 * second_in + 0.001 * grads_in * grads_in
    first_hat = first_new / (1.0 - 0.9**STEP)
    second_hat = second_new / (1.0 - 0.999**STEP)
    return (
        first_new,
        second_new,
        params_in - adam_rate * first_hat / (jnp.sqrt(second_hat) + 1e-08),
    )


def local(
    tokens_in,
    lm_grad,
    lm_logprob,
    targets,
    neighbor_ids,
    nearby_entry_gaps,
    seq_lengths,
    attn_weights,
    ffn_weights,
    attn_left,
    attn_right,
    ffn_left,
    ffn_right,
    attn_left_root,
    attn_right_root,
    ffn_left_root,
    ffn_right_root,
    norm_params,
    norm_moment1,
    norm_moment2,
    blending_coefficients,
    knn_moment1,
    knn_moment2,
):
    local_rows = tokens_in.shape[0]
    group_rows = local_rows * lax.axis_size("tensor")
    block_rows = SHORT
    score_scale = HEAD_DIM ** (-0.5)
    attn_full, ffn_full = (
        lax.all_gather(attn_weights.astype(jnp.bfloat16), "dp", axis=1, tiled=True),
        lax.all_gather(ffn_weights.astype(jnp.bfloat16), "dp", axis=1, tiled=True),
    )
    proj_in = jnp.concatenate([attn_full[0], attn_full[1], attn_full[2]], axis=1)
    proj_out = attn_full[3]
    head_cols = proj_out.shape[1]
    head_count = head_cols // HEAD_DIM
    first_block = first_blocks(seq_lengths, group_rows, block_rows)
    resid = tokens_in.astype(jnp.float32)
    normed1, norm1_back = jax.vjp(layer_norm, resid, norm_params[0], norm_params[1])
    normed1_low = normed1.astype(jnp.bfloat16)
    normed1_all = spread_rows(normed1_low)
    qkv_low = jnp.dot(normed1_all, proj_in, preferred_element_type=jnp.float32).astype(jnp.bfloat16)
    query_all = qkv_low[:, :head_cols].reshape(group_rows, head_count, HEAD_DIM)
    key_all = qkv_low[:, head_cols : 2 * head_cols].reshape(group_rows, head_count, HEAD_DIM)
    value_all = qkv_low[:, 2 * head_cols :].reshape(group_rows, head_count, HEAD_DIM)
    heads_out, log_masses = attend_forward(
        query_all, key_all, value_all, first_block, block_rows, score_scale
    )
    heads_flat = heads_out.reshape(group_rows, head_cols)
    attn_out = branch_total(heads_flat, proj_out)
    middle = resid + attn_out
    normed2, norm2_back = jax.vjp(layer_norm, middle, norm_params[2], norm_params[3])
    normed2_low = normed2.astype(jnp.bfloat16)
    w_up = ffn_full[0]
    w_down = ffn_full[1]
    normed2_all = spread_rows(normed2_low)
    hidden_pre = jnp.dot(normed2_all, w_up, preferred_element_type=jnp.float32)
    hidden_act, gelu_back = jax.vjp(gelu_tanh, hidden_pre)
    act_low = hidden_act.astype(jnp.bfloat16)
    ffn_out = branch_total(act_low, w_down)
    mixed = (middle + ffn_out).astype(jnp.bfloat16)
    sharpness_divisor = jnp.exp(blending_coefficients[0])
    interp = jax.nn.sigmoid(blending_coefficients[1])
    nearby_entry_logits = -nearby_entry_gaps / sharpness_divisor
    near_top = jnp.max(nearby_entry_logits, axis=1, keepdims=True)
    near_exp = jnp.exp(nearby_entry_logits - near_top)
    nearby_entry_shares = near_exp / jnp.sum(near_exp, axis=1, keepdims=True)
    target_matches = (neighbor_ids == targets[:, None]).astype(jnp.float32)
    retrieval_probability = jnp.sum(nearby_entry_shares * target_matches, axis=1)
    lm_prob = jnp.exp(lm_logprob)
    mixture = interp * retrieval_probability + (1.0 - interp) * lm_prob
    token_loss = -jnp.log(mixture)
    lm_weight = -(1.0 - interp) * lm_prob / mixture
    temp_terms = (
        jnp.sum(
            nearby_entry_shares
            * (target_matches - retrieval_probability[:, None])
            * nearby_entry_gaps,
            axis=1,
        )
        / sharpness_divisor
    )
    temp_grad = jnp.sum(-(interp / mixture) * temp_terms)
    interp_grad = jnp.sum(-interp * (1.0 - interp) * (retrieval_probability - lm_prob) / mixture)
    knn_grads = jnp.stack([temp_grad, interp_grad])
    cotangent = lm_weight[:, None] * lm_grad.astype(jnp.float32)
    cot_all = spread_grads(cotangent.astype(jnp.bfloat16))
    grad_act = jnp.dot(cot_all, w_down, preferred_element_type=jnp.float32)
    grad_pre_low = gelu_back(grad_act)[0].astype(jnp.bfloat16)
    normed2_used = spread_again(normed2_low)
    grad_up = jnp.einsum(
        "rd,rf->df", normed2_used, grad_pre_low, preferred_element_type=jnp.float32
    )
    grad_down = jnp.einsum("rd,rf->df", cot_all, act_low, preferred_element_type=jnp.float32)
    ffn_local = jnp.stack([grad_up, grad_down])
    grad_normed2 = input_total(grad_pre_low, w_up)
    mid_norm_grad, gain2_grad, shift2_grad = norm2_back(grad_normed2)
    grad_middle = cotangent + mid_norm_grad
    grad_mid_all = spread_grads(grad_middle.astype(jnp.bfloat16))
    grad_heads = jnp.dot(grad_mid_all, proj_out, preferred_element_type=jnp.float32).astype(
        jnp.bfloat16
    )
    grad_out_proj = jnp.einsum(
        "rd,rc->dc", grad_mid_all, heads_flat, preferred_element_type=jnp.float32
    )
    grad_keys, grad_values, grad_query = attend_backward(
        query_all,
        key_all,
        value_all,
        grad_heads.reshape(group_rows, head_count, HEAD_DIM),
        log_masses,
        first_block,
        block_rows,
        score_scale,
    )
    grad_qkv = jnp.concatenate(
        [
            grad_query.reshape(group_rows, head_cols),
            grad_keys.reshape(group_rows, head_cols),
            grad_values.reshape(group_rows, head_cols),
        ],
        axis=1,
    ).astype(jnp.bfloat16)
    normed1_used = spread_again(normed1_low)
    grad_proj_in = jnp.einsum(
        "rd,rc->dc", normed1_used, grad_qkv, preferred_element_type=jnp.float32
    )
    grad_normed1 = input_total(grad_qkv, proj_in)
    res_norm_grad, gain1_grad, bias_first_cotangent = norm1_back(grad_normed1)
    input_grad = grad_middle + res_norm_grad
    norm_grads = jnp.stack([gain1_grad, bias_first_cotangent, gain2_grad, shift2_grad])
    norm_total, knn_total, loss_total = lax.psum(
        (norm_grads, knn_grads, jnp.sum(token_loss)), ("dp", "tensor")
    )
    token_count = group_rows * lax.axis_size("dp")
    attn_local = jnp.stack(
        [
            grad_proj_in[:, :head_cols],
            grad_proj_in[:, head_cols : 2 * head_cols],
            grad_proj_in[:, 2 * head_cols :],
            grad_out_proj,
        ]
    )
    attn_grad, ffn_grad = (
        lax.psum_scatter(attn_local, "dp", scatter_dimension=1, tiled=True),
        lax.psum_scatter(ffn_local, "dp", scatter_dimension=1, tiled=True),
    )
    attn_rows, ffn_rows = (
        lax.all_gather(attn_grad.astype(jnp.bfloat16), "tensor", axis=2, tiled=True).astype(
            attn_grad.dtype
        ),
        lax.all_gather(ffn_grad.astype(jnp.bfloat16), "tensor", axis=2, tiled=True).astype(
            ffn_grad.dtype
        ),
    )
    attn_right_sum, ffn_right_sum = right_statistics(attn_grad, ffn_grad, attn_rows, ffn_rows)
    attn_turned = jnp.einsum(
        "sri,sij->srj", attn_rows, attn_right_root, precision=lax.Precision.HIGHEST
    )
    ffn_turned = jnp.einsum(
        "sri,sij->srj", ffn_rows, ffn_right_root, precision=lax.Precision.HIGHEST
    )
    attn_cols, ffn_cols, attn_turned_cols, ffn_turned_cols = (
        lax.all_gather(attn_grad.astype(jnp.bfloat16), "dp", axis=1, tiled=True).astype(
            attn_grad.dtype
        ),
        lax.all_gather(ffn_grad.astype(jnp.bfloat16), "dp", axis=1, tiled=True).astype(
            ffn_grad.dtype
        ),
        lax.all_gather(attn_turned.astype(jnp.bfloat16), "dp", axis=1, tiled=True).astype(
            attn_turned.dtype
        ),
        lax.all_gather(ffn_turned.astype(jnp.bfloat16), "dp", axis=1, tiled=True).astype(
            ffn_turned.dtype
        ),
    )
    attn_left_sum, ffn_left_sum = left_statistics(attn_grad, ffn_grad, attn_cols, ffn_cols)
    attn_update = jnp.einsum(
        "srq,sqi->sri", attn_left_root, attn_turned_cols, precision=lax.Precision.HIGHEST
    )
    ffn_update = jnp.einsum(
        "srq,sqi->sri", ffn_left_root, ffn_turned_cols, precision=lax.Precision.HIGHEST
    )
    attn_left_new = 0.5 * attn_left + 0.5 * attn_left_sum
    attn_right_new = 0.5 * attn_right + 0.5 * attn_right_sum
    ffn_left_new = 0.5 * ffn_left + 0.5 * ffn_left_sum
    ffn_right_new = 0.5 * ffn_right + 0.5 * ffn_right_sum
    attn_new = attn_weights - shampoo_rate * (attn_update + shampoo_decay * attn_weights)
    ffn_new = ffn_weights - shampoo_rate * (ffn_update + shampoo_decay * ffn_weights)
    norm_m1, norm_m2, norm_new = adamw_step(norm_params, norm_total, norm_moment1, norm_moment2)
    knn_m1, knn_m2, knn_new = adamw_step(blending_coefficients, knn_total, knn_moment1, knn_moment2)
    return (
        mixed,
        input_grad,
        loss_total / token_count,
        attn_grad,
        attn_left_new,
        attn_right_new,
        attn_new,
        ffn_grad,
        ffn_left_new,
        ffn_right_new,
        ffn_new,
        norm_m1,
        norm_m2,
        norm_new,
        knn_m1,
        knn_m2,
        knn_new,
    )


LINE_BIT, HALF_BIT, CORE_BIT, X_BIT, Y_BIT = 1, 2, 4, 8, 16


def send_by(values_in, target):
    return lax.ppermute(values_in, ("dp", "tensor"), [(index, target(index)) for index in range(32)])


def flip(values_in, mask):
    return send_by(values_in, lambda index: index ^ mask)


def moves(index):
    return ((index >> 2) ^ (index >> 1)) & 1 == 1


def swapped(index):
    return index ^ (CORE_BIT | HALF_BIT) if moves(index) else index


def swap_core_half(values_in):
    return send_by(values_in, swapped)


def swap_or_near(values_in):
    return send_by(
        values_in, lambda index: swapped(index) if moves(index) else index ^ LINE_BIT
    )


def near_of_moved(values_in):
    pairs = [(index, index ^ LINE_BIT) for index in range(32) if moves(index)]
    return lax.ppermute(values_in, ("dp", "tensor"), pairs)


def cross_one(values_in):
    return send_by(values_in, lambda index: index ^ (Y_BIT if index & CORE_BIT else X_BIT))


def cross_two(values_in):
    return send_by(values_in, lambda index: index ^ (X_BIT if index & CORE_BIT else Y_BIT))


def pick(values_in, index, axis):
    return lax.dynamic_index_in_dim(values_in, index, axis, keepdims=False)


def ordered_pair(own, other, bit, axis):
    return jnp.where(
        bit == 0, jnp.stack([own, other], axis=axis), jnp.stack([other, own], axis=axis)
    )


def together(*values_in):
    return lax.optimization_barrier(values_in)


def by_chip(values_in, chip):
    width = values_in.shape[-1] // 4
    return jnp.concatenate(
        [
            lax.dynamic_slice_in_dim(values_in, (chip ^ block) * width, width, values_in.ndim - 1)
            for block in range(4)
        ],
        axis=-1,
    )


def add_far(pair):
    return jnp.concatenate([pair, flip(pair, CORE_BIT)], axis=0)


def weight_core(local_low, place):
    width = local_low.shape[2] // 2
    mine = lax.dynamic_slice_in_dim(local_low, place["core"] * width, width, 2)
    theirs = lax.dynamic_slice_in_dim(local_low, (1 - place["core"]) * width, width, 2)
    both = ordered_pair(mine, flip(theirs, CORE_BIT), place["core"], 1)
    return both.reshape(local_low.shape[0], 2 * local_low.shape[1], width)


def weight_halves(own, other, place):
    return jnp.where(
        place["half"] == 0,
        jnp.concatenate([own, other], axis=2),
        jnp.concatenate([other, own], axis=2),
    )


def by_core(core, own, other, axis):
    return jnp.where(
        core == 0,
        jnp.concatenate([own, other], axis=axis),
        jnp.concatenate([other, own], axis=axis),
    )


def by_rel(core, own, first, pair, axis):
    middle = jnp.where(
        core == 0,
        jnp.concatenate([first, pair[0]], axis=axis),
        jnp.concatenate([pair[0], first], axis=axis),
    )
    return jnp.concatenate([own, middle, pair[1]], axis=axis)


def scatter_parts(core, partials):
    parts = [partial.reshape(2, 2, -1, partial.shape[1]) for partial in partials]
    kept = [jnp.where(core == 0, part[:, 0], part[0]) for part in parts]
    sent = [jnp.where(core == 0, part[:, 1], part[1]) for part in parts]
    return jnp.stack(kept), jnp.stack(sent)


def add_low(left_part, right_part):
    return (left_part.astype(jnp.float32) + right_part.astype(jnp.float32)).astype(jnp.bfloat16)


def dot32(spec, left_mat, right_mat):
    return jnp.einsum(spec, left_mat, right_mat, preferred_element_type=jnp.float32)


def update_kernel(
    info_ref, left_ref, line_ref, first_ref, pair_ref, root_ref, own_ref, sent_ref, update_acc, gram_acc
):
    step = pl.program_id(1)
    steps = pl.num_programs(1)
    chip, core, tensor, line_bit = info_ref[0], info_ref[1], info_ref[2], info_ref[3]
    block = left_ref.shape[2] // 4
    own_rows = block // 2
    cols = update_acc.shape[1]

    @pl.when(step == 0)
    def _():
        update_acc[...] = jnp.zeros_like(update_acc)
        gram_acc[...] = jnp.zeros_like(gram_acc)

    rels = (0, 1 + core, 2 - core, 3)
    lefts = [
        left_ref[0, :, pl.ds(pl.multiple_of((chip ^ rel) * block, block), block)] for rel in rels
    ]
    total = None
    for line in range(2):
        pieces = (
            line_ref[line, 0],
            first_ref[line, 0],
            pair_ref[0, line, 0],
            pair_ref[1, line, 0],
        )
        turned = None
        for left, piece in zip(lefts, pieces):
            part = jnp.dot(left, piece, preferred_element_type=jnp.float32)
            turned = part if turned is None else turned + part
        root = root_ref[0, :, line_bit ^ line, 0].reshape(-1, cols).astype(jnp.bfloat16)
        part = jnp.dot(turned.astype(jnp.bfloat16), root, preferred_element_type=jnp.float32)
        total = part if total is None else total + part
        for rel, piece in zip(rels, pieces):

            @pl.when((chip ^ tensor) == rel)
            def _(own=pieces[0], piece=piece):
                gram_acc[...] += lax.dot_general(
                    own, piece, (((1,), (1,)), ((), ())), preferred_element_type=jnp.float32
                )

    update_acc[...] += total

    @pl.when(step == steps - 1)
    def _():
        own_ref[0, :, :cols] = update_acc[:own_rows]
        sent_ref[0, :, :cols] = update_acc[own_rows:].astype(jnp.bfloat16)
        gram_own = gram_acc[pl.ds(pl.multiple_of(core * own_rows, own_rows), own_rows), :]
        gram_sent = gram_acc[pl.ds(pl.multiple_of((1 - core) * own_rows, own_rows), own_rows), :]
        own_ref[0, :, cols:] = gram_own
        sent_ref[0, :, cols:] = gram_sent.astype(jnp.bfloat16)


def updates(info, left_low, pieces, root, split):
    line, first, pair = pieces
    _, lead, rows, width = line.shape
    count = lead // 2 if split else lead
    cols = root.shape[2]
    root_rows = root.shape[1] // 8
    root = root.reshape(root.shape[0], 2, 2, 2, root_rows, cols)
    steps = 2 if split else 1
    if split:
        root_spec = pl.BlockSpec(
            (1, 1, 2, 1, root_rows, cols),
            lambda m, k, info_ref: (m, k, 0, info_ref[1], 0, 0),
        )
    else:
        root_spec = pl.BlockSpec(
            (1, 2, 2, 1, root_rows, cols),
            lambda m, k, info_ref: (m, 0, 0, info_ref[1], 0, 0),
        )

    def place_of(m, k):
        return 2 * m + k if split else m

    out_shape = (count, rows // 2, cols + rows)
    out_spec = pl.BlockSpec((1, rows // 2, cols + rows), lambda m, k, info_ref: (m, 0, 0))
    piece_spec = pl.BlockSpec(
        (2, 1, rows, width), lambda m, k, info_ref: (0, place_of(m, k), 0, 0)
    )
    return pl.pallas_call(
        update_kernel,
        grid_spec=pltpu.PrefetchScalarGridSpec(
            num_scalar_prefetch=1,
            grid=(count, steps),
            in_specs=[
                pl.BlockSpec((1, rows, 4 * rows), lambda m, k, info_ref: (m, 0, 0)),
                piece_spec,
                piece_spec,
                pl.BlockSpec(
                    (2, 2, 1, rows, width), lambda m, k, info_ref: (0, 0, place_of(m, k), 0, 0)
                ),
                root_spec,
            ],
            out_specs=[out_spec, out_spec],
            scratch_shapes=[
                pltpu.VMEM((rows, cols), jnp.float32),
                pltpu.VMEM((rows, rows), jnp.float32),
            ],
        ),
        out_shape=(
            jax.ShapeDtypeStruct(out_shape, jnp.float32),
            jax.ShapeDtypeStruct(out_shape, jnp.bfloat16),
        ),
        compiler_params=pltpu.CompilerParams(vmem_limit_bytes=48 * 1024 * 1024),
        cost_estimate=pl.CostEstimate(flops=1_000_000, bytes_accessed=100_000, transcendentals=0),
    )(info, left_low, line, first, pair, root)


def column_block(pieces, line_rel, half, split):
    line, first, pair = pieces

    def cut(piece):
        piece = piece[0] if line_rel is None else pick(piece, line_rel, 0)
        if split:
            return pick(piece.reshape(-1, 2, *piece.shape[1:]), half, 1)
        width = piece.shape[2] // 2
        return lax.dynamic_slice_in_dim(piece, half * width, width, 2)

    return jnp.concatenate([cut(line), cut(first), cut(pair[0]), cut(pair[1])], axis=1)


def right_kernel(
    info_ref,
    line_t,
    first_t,
    pair_t,
    line_c,
    first_c,
    pair_c,
    other_ref,
    right_in_ref,
    right_ref,
    grad_ref,
):
    core = info_ref[1]
    half = other_ref.shape[2]
    chip_rows = other_ref.shape[1] // 4
    own_rows = chip_rows // 2
    own = (line_t[0, 0], first_t[0, 0], pair_t[0, 0, 0], pair_t[1, 0, 0])
    cols = (line_c[0, 0], first_c[0, 0], pair_c[0, 0, 0], pair_c[1, 0, 0])
    sums = [None, None]
    for place, own_piece, col_piece in zip((0, 2, 1, 3), own, cols):
        other_piece = other_ref[0, place * chip_rows : (place + 1) * chip_rows, :]
        for at, piece in enumerate((own_piece, other_piece)):
            part = lax.dot_general(
                piece, col_piece, (((0,), (0,)), ((), ())), preferred_element_type=jnp.float32
            )
            sums[at] = part if sums[at] is None else sums[at] + part
    row = pl.ds(pl.multiple_of(core * own_rows, own_rows), own_rows)
    grads = (line_t[0, 0, row, :], other_ref[0, row, :])
    for at in range(2):
        block = core if at == 0 else 1 - core
        rows = pl.ds(pl.multiple_of(block * half, half), half)
        right_ref[0, rows, :] = 0.5 * right_in_ref[0, rows, :] + 0.5 * sums[at]
        grad_ref[0, :, rows] = grads[at].astype(jnp.float32)


def right_statistics_new(info, pieces, other_cols, right_in, own_rows, split):
    line, first, pair = pieces
    _, lead, rows, width = line.shape
    count = right_in.shape[0]
    half = other_cols.shape[2]
    cols = right_in.shape[2]
    if split:

        def own(m, info_ref):
            return (0, 2 * m + info_ref[4], 0, 0)

        def col(m, info_ref):
            return (info_ref[5], 2 * m + info_ref[6], 0, 0)

    else:

        def own(m, info_ref):
            return (0, m, 0, info_ref[4])

        def col(m, info_ref):
            return (info_ref[5], m, 0, info_ref[6])

    def specs(place_of):
        one = pl.BlockSpec((1, 1, rows, half), place_of)
        two = pl.BlockSpec((2, 1, 1, rows, half), lambda m, info_ref: (0,) + place_of(m, info_ref))
        return [one, one, two]

    return pl.pallas_call(
        right_kernel,
        grid_spec=pltpu.PrefetchScalarGridSpec(
            num_scalar_prefetch=1,
            grid=(count,),
            in_specs=specs(own)
            + specs(col)
            + [
                pl.BlockSpec((1, 4 * rows, half), lambda m, info_ref: (m, 0, 0)),
                pl.BlockSpec((1, 2 * half, cols), lambda m, info_ref: (m, 0, 0)),
            ],
            out_specs=[
                pl.BlockSpec((1, 2 * half, cols), lambda m, info_ref: (m, 0, 0)),
                pl.BlockSpec((1, own_rows, 2 * half), lambda m, info_ref: (m, 0, 0)),
            ],
        ),
        out_shape=(
            jax.ShapeDtypeStruct(right_in.shape, jnp.float32),
            jax.ShapeDtypeStruct((count, own_rows, 2 * half), jnp.float32),
        ),
        compiler_params=pltpu.CompilerParams(vmem_limit_bytes=48 * 1024 * 1024),
        cost_estimate=pl.CostEstimate(flops=1_000_000, bytes_accessed=100_000, transcendentals=0),
    )(info, line, first, pair, line, first, pair, other_cols, right_in)


def product_of(pieces, cols):
    total = None
    for piece, col_piece in zip(pieces, cols):
        part = lax.dot_general(
            piece, col_piece, (((0,), (0,)), ((), ())), preferred_element_type=jnp.float32
        )
        total = part if total is None else total + part
    return total


def right_own_kernel(
    info_ref, line_t, first_t, pair_t, line_c, first_c, pair_c, right_in_ref, right_ref, grad_ref
):
    own_rows = grad_ref.shape[1]
    own = (line_t[0, 0], first_t[0, 0], pair_t[0, 0, 0], pair_t[1, 0, 0])
    cols = (line_c[0, 0], first_c[0, 0], pair_c[0, 0, 0], pair_c[1, 0, 0])
    right_ref[0] = 0.5 * right_in_ref[0] + 0.5 * product_of(own, cols)
    row = pl.ds(pl.multiple_of(info_ref[1] * own_rows, own_rows), own_rows)
    grad_ref[0] = line_t[0, 0, row, :].astype(jnp.float32)


def right_other_kernel(
    info_ref, line_c, first_c, pair_c, other_ref, right_in_ref, kept_a, kept_b, right_ref, grad_ref
):
    own_rows = grad_ref.shape[1]
    chip_rows = other_ref.shape[1] // 4
    others = [other_ref[0, at * chip_rows : (at + 1) * chip_rows, :] for at in (0, 2, 1, 3)]
    cols = (line_c[0, 0], first_c[0, 0], pair_c[0, 0, 0], pair_c[1, 0, 0])
    right_ref[0] = 0.5 * right_in_ref[0] + 0.5 * product_of(others, cols)
    row = pl.ds(pl.multiple_of(info_ref[1] * own_rows, own_rows), own_rows)
    grad_ref[0] = other_ref[0, row, :].astype(jnp.float32)


def right_half(info, pieces, other_cols, right_in, own_rows, earlier):
    line, first, pair = pieces
    rows, half = line.shape[2:]
    count, _, cols = right_in.shape
    mine = other_cols is None

    def block(info_ref):
        return info_ref[1] if mine else 1 - info_ref[1]

    def specs(place_of):
        one = pl.BlockSpec((1, 1, rows, half), place_of)
        two = pl.BlockSpec((2, 1, 1, rows, half), lambda m, info_ref: (0,) + place_of(m, info_ref))
        return [one, one, two]

    right_spec = pl.BlockSpec((1, half, cols), lambda m, info_ref: (m, block(info_ref), 0))
    grad_spec = pl.BlockSpec((1, own_rows, half), lambda m, info_ref: (m, 0, block(info_ref)))
    col_specs = specs(lambda m, info_ref: (info_ref[5], 2 * m + info_ref[6], 0, 0))
    if mine:
        in_specs = specs(lambda m, info_ref: (0, 2 * m + info_ref[4], 0, 0)) + col_specs
        in_specs = in_specs + [right_spec]
        operands = (line, first, pair, line, first, pair, right_in)
    else:
        other_spec = pl.BlockSpec((1, 4 * rows, half), lambda m, info_ref: (m, 0, 0))
        kept = [pl.BlockSpec(memory_space=pl.ANY)] * 2
        in_specs = col_specs + [other_spec, right_spec] + kept
        operands = (line, first, pair, other_cols, right_in) + earlier
    return pl.pallas_call(
        right_own_kernel if mine else right_other_kernel,
        grid_spec=pltpu.PrefetchScalarGridSpec(
            num_scalar_prefetch=1,
            grid=(count,),
            in_specs=in_specs,
            out_specs=[right_spec, grad_spec],
        ),
        out_shape=(
            jax.ShapeDtypeStruct(right_in.shape, jnp.float32),
            jax.ShapeDtypeStruct((count, own_rows, 2 * half), jnp.float32),
        ),
        input_output_aliases={} if mine else {6: 0, 7: 1},
        compiler_params=pltpu.CompilerParams(vmem_limit_bytes=48 * 1024 * 1024),
        cost_estimate=pl.CostEstimate(flops=1_000_000, bytes_accessed=100_000, transcendentals=0),
    )(info, *operands)


def shampoo_left(own, received, left_in, weights_in):
    total = own + received.astype(jnp.float32)
    cols = weights_in.shape[2]
    return (
        0.5 * left_in + 0.5 * total[:, :, cols:],
        weights_in - shampoo_rate * (total[:, :, :cols] + shampoo_decay * weights_in),
    )


def halve_kernel(info_ref, weights_ref, mine_ref, theirs_ref):
    core = info_ref[1]
    width = mine_ref.shape[2]
    mine = pl.ds(pl.multiple_of(core * width, width), width)
    theirs = pl.ds(pl.multiple_of((1 - core) * width, width), width)
    mine_ref[...] = weights_ref[:, :, mine].astype(mine_ref.dtype)
    theirs_ref[...] = weights_ref[:, :, theirs].astype(theirs_ref.dtype)


def halve(where, weights):
    count, rows, width = weights.shape
    shape = jax.ShapeDtypeStruct((count, rows, width // 2), jnp.bfloat16)
    return pl.pallas_call(
        halve_kernel,
        grid_spec=pltpu.PrefetchScalarGridSpec(
            num_scalar_prefetch=1,
            grid=(1,),
            in_specs=[pl.BlockSpec(weights.shape, lambda step, info_ref: (0, 0, 0))],
            out_specs=[pl.BlockSpec(shape.shape, lambda step, info_ref: (0, 0, 0))] * 2,
        ),
        out_shape=(shape, shape),
        compiler_params=pltpu.CompilerParams(vmem_limit_bytes=32 * 1024 * 1024),
        cost_estimate=pl.CostEstimate(flops=1_000_000, bytes_accessed=100_000, transcendentals=0),
    )(where, weights)


def unite_kernel(info_ref, mine_ref, other_ref, out_ref):
    core = info_ref[1]
    rows = mine_ref.shape[1]
    out_ref[:, pl.ds(pl.multiple_of(core * rows, rows), rows), :] = mine_ref[...]
    out_ref[:, pl.ds(pl.multiple_of((1 - core) * rows, rows), rows), :] = other_ref[...]


def unite(where, mine, other):
    count, rows, width = mine.shape
    spec = pl.BlockSpec(mine.shape, lambda step, info_ref: (0, 0, 0))
    out = (count, 2 * rows, width)
    return pl.pallas_call(
        unite_kernel,
        grid_spec=pltpu.PrefetchScalarGridSpec(
            num_scalar_prefetch=1,
            grid=(1,),
            in_specs=[spec, spec],
            out_specs=pl.BlockSpec(out, lambda step, info_ref: (0, 0, 0)),
        ),
        out_shape=jax.ShapeDtypeStruct(out, mine.dtype),
        compiler_params=pltpu.CompilerParams(vmem_limit_bytes=32 * 1024 * 1024),
        cost_estimate=pl.CostEstimate(flops=1_000_000, bytes_accessed=100_000, transcendentals=0),
    )(where, mine, other)


def knn_kernel(
    info_ref, blend_ref, gaps_ref, ids_ref, targets_ref, logprob_ref, lm_ref, cot_ref, sums_ref
):
    step = pl.program_id(0)
    chip = info_ref[0]
    log_temperature = blend_ref[0:1, 0:1]
    sharpness_divisor = jnp.exp(log_temperature)
    interp = 1.0 / (1.0 + jnp.exp(-blend_ref[0:1, 1:2]))
    gaps = gaps_ref[...]
    logits = -gaps / sharpness_divisor
    near_exp = jnp.exp(logits - jnp.max(logits, axis=1, keepdims=True))
    mass = jnp.sum(near_exp, axis=1, keepdims=True)
    hits = ids_ref[...] == targets_ref[...]
    hit_exp = jnp.where(hits, near_exp, 0.0)
    retrieval = jnp.sum(hit_exp, axis=1, keepdims=True) / mass
    hit_gaps = jnp.sum(hit_exp * gaps, axis=1, keepdims=True) / mass
    all_gaps = jnp.sum(near_exp * gaps, axis=1, keepdims=True) / mass
    temp_terms = (hit_gaps - retrieval * all_gaps) / sharpness_divisor
    lm_prob = jnp.exp(logprob_ref[...])
    mixture = interp * retrieval + (1.0 - interp) * lm_prob
    lm_weight = -(1.0 - interp) * lm_prob / mixture
    temp_grad = jnp.sum(-(interp / mixture) * temp_terms, axis=0, keepdims=True)
    interp_grad = jnp.sum(
        -interp * (1.0 - interp) * (retrieval - lm_prob) / mixture, axis=0, keepdims=True
    )
    loss = jnp.sum(-jnp.log(mixture), axis=0, keepdims=True)
    lane = lax.broadcasted_iota(jnp.int32, sums_ref.shape, 1)
    sums = jnp.where(lane == 0, temp_grad, jnp.where(lane == 1, interp_grad, 0.0))
    sums = jnp.where(lane == 2, loss, sums)

    @pl.when(step == 0)
    def _():
        sums_ref[...] = jnp.zeros_like(sums_ref)

    sums_ref[...] += sums
    block = lm_ref.shape[1] // 4
    for rel in range(4):
        start = pl.multiple_of((chip ^ rel) * block, block)
        part = lm_weight * lm_ref[:, pl.ds(start, block)].astype(jnp.float32)
        cot_ref[:, rel * block : (rel + 1) * block] = part.astype(cot_ref.dtype)


def neighbours(where, blend, gaps, ids, targets, logprob, lm_grad):
    rows, width = gaps.shape
    step_rows = rows // 3
    wide = pl.BlockSpec((step_rows, width), lambda r, info_ref: (r, 0))
    thin = pl.BlockSpec((step_rows, 1), lambda r, info_ref: (r, 0))
    cot, sums = pl.pallas_call(
        knn_kernel,
        grid_spec=pltpu.PrefetchScalarGridSpec(
            num_scalar_prefetch=1,
            grid=(3,),
            in_specs=[
                pl.BlockSpec((1, 2), lambda r, info_ref: (0, 0)),
                wide,
                wide,
                thin,
                thin,
                wide,
            ],
            out_specs=[wide, pl.BlockSpec((8, width), lambda r, info_ref: (0, 0))],
        ),
        out_shape=(
            jax.ShapeDtypeStruct((rows, width), jnp.bfloat16),
            jax.ShapeDtypeStruct((8, width), jnp.float32),
        ),
        compiler_params=pltpu.CompilerParams(vmem_limit_bytes=32 * 1024 * 1024),
        cost_estimate=pl.CostEstimate(flops=1_000_000, bytes_accessed=100_000, transcendentals=0),
    )(where, blend[None], gaps, ids, targets[:, None], logprob[:, None], lm_grad)
    return cot, sums[:1]


def normalize_kernel(info_ref, pair_ref, far_ref, params_ref, out_ref, own_ref):
    step = pl.program_id(0)
    chip = info_ref[0]
    block = out_ref.shape[1] // 4

    def work(rows_ref):
        values_in = rows_ref[...].astype(jnp.float32)
        centre = jnp.mean(values_in, axis=-1, keepdims=True)
        spread_sq = jnp.mean((values_in - centre) ** 2, axis=-1, keepdims=True)
        scale = lax.rsqrt(spread_sq + norm_eps)
        for rel in range(4):
            start = pl.multiple_of((chip ^ rel) * block, block)
            own = slice(rel * block, (rel + 1) * block)
            part = rows_ref[:, pl.ds(start, block)].astype(jnp.float32)
            normed = (part - centre) * scale * params_ref[0:1, own] + params_ref[1:2, own]
            out_ref[:, own] = normed.astype(out_ref.dtype)

    @pl.when(step < 2)
    def _():
        work(pair_ref)

    @pl.when(step >= 2)
    def _():
        work(far_ref)

    @pl.when(step == 0)
    def _():
        for rel in range(4):
            start = pl.multiple_of((chip ^ rel) * block, block)
            own_ref[:, rel * block : (rel + 1) * block] = pair_ref[:, pl.ds(start, block)]


def normalize(where, pair, far, params):
    rows, width = pair.shape
    step_rows = rows // 2
    pair_spec = pl.BlockSpec((step_rows, width), lambda r, info_ref: (jnp.minimum(r, 1), 0))
    far_spec = pl.BlockSpec((step_rows, width), lambda r, info_ref: (jnp.maximum(r - 2, 0), 0))
    return pl.pallas_call(
        normalize_kernel,
        grid_spec=pltpu.PrefetchScalarGridSpec(
            num_scalar_prefetch=1,
            grid=(4,),
            in_specs=[
                pair_spec,
                far_spec,
                pl.BlockSpec(params.shape, lambda r, info_ref: (0, 0)),
            ],
            out_specs=[
                pl.BlockSpec((step_rows, width), lambda r, info_ref: (r, 0)),
                pl.BlockSpec((step_rows, width), lambda r, info_ref: (0, 0)),
            ],
        ),
        out_shape=(
            jax.ShapeDtypeStruct((2 * rows, width), pair.dtype),
            jax.ShapeDtypeStruct((step_rows, width), pair.dtype),
        ),
        compiler_params=pltpu.CompilerParams(vmem_limit_bytes=32 * 1024 * 1024),
        cost_estimate=pl.CostEstimate(flops=1_000_000, bytes_accessed=100_000, transcendentals=0),
    )(where, pair, far, params)


def norm_back_kernel(
    info_ref, own_ref, near_ref, rows_ref, later_ref, gain_ref, out_ref, sums_ref
):
    chip = info_ref[0]
    grads = own_ref[...] + near_ref[...].astype(jnp.float32)
    values_in = rows_ref[...].astype(jnp.float32)
    centred = values_in - jnp.mean(values_in, axis=-1, keepdims=True)
    spread_sq = jnp.mean(centred * centred, axis=-1, keepdims=True)
    scale = lax.rsqrt(spread_sq + norm_eps)
    normed = centred * scale
    sums_ref[0:1, :] = jnp.sum(grads * normed, axis=0, keepdims=True)
    sums_ref[1:2, :] = jnp.sum(grads, axis=0, keepdims=True)
    sloped = grads * gain_ref[0:1, :]
    along = jnp.mean(sloped * normed, axis=-1, keepdims=True)
    back = (sloped - jnp.mean(sloped, axis=-1, keepdims=True) - normed * along) * scale
    result = (later_ref[...] + back).astype(out_ref.dtype)
    block = out_ref.shape[1] // 4
    for rel in range(4):
        start = pl.multiple_of((chip ^ rel) * block, block)
        out_ref[:, pl.ds(start, block)] = result[:, rel * block : (rel + 1) * block]


def norm_back(where, own, near, rows_low, later, gain):
    rows, width = own.shape

    def whole(shape):
        return pl.BlockSpec(shape, lambda step, info_ref: (0, 0))

    return pl.pallas_call(
        norm_back_kernel,
        grid_spec=pltpu.PrefetchScalarGridSpec(
            num_scalar_prefetch=1,
            grid=(1,),
            in_specs=[whole(own.shape)] * 4 + [whole((1, width))],
            out_specs=[whole(own.shape), whole((2, width))],
        ),
        out_shape=(
            jax.ShapeDtypeStruct((rows, width), jnp.bfloat16),
            jax.ShapeDtypeStruct((2, width), jnp.float32),
        ),
        compiler_params=pltpu.CompilerParams(vmem_limit_bytes=40 * 1024 * 1024),
        cost_estimate=pl.CostEstimate(flops=1_000_000, bytes_accessed=100_000, transcendentals=0),
    )(where, own, near, rows_low, later, gain)


def ffn_kernel(normed_a, normed_b, cot_a, cot_b, up_ref, down_ref, act_ref, grad_ref):
    def work(normed_ref, cot_ref):
        pre = jnp.dot(normed_ref[...], up_ref[0], preferred_element_type=jnp.float32)
        grad_act = jnp.dot(cot_ref[...], down_ref[0], preferred_element_type=jnp.float32)
        scale = 0.7978845608028654
        square = pre * pre
        turn = jnp.tanh(pre * (scale + (scale * 0.044715) * square))
        gate = 0.5 + 0.5 * turn
        act_ref[...] = (pre * gate).astype(jnp.bfloat16)
        slope = gate + 0.5 * pre * (1.0 - turn * turn) * (scale + (3.0 * scale * 0.044715) * square)
        grad_ref[...] = (grad_act * slope).astype(jnp.bfloat16)

    @pl.when(pl.program_id(1) < 2)
    def _():
        work(normed_a, cot_a)

    @pl.when(pl.program_id(1) >= 2)
    def _():
        work(normed_b, cot_b)


def ffn_middle(normed, cot, weights):
    rows, width = normed[0].shape
    hidden = weights.shape[2]
    step_rows, step_cols = rows // 2, hidden // 2
    pair_spec = pl.BlockSpec((step_rows, width), lambda f, r: (jnp.minimum(r, 1), 0))
    far_spec = pl.BlockSpec((step_rows, width), lambda f, r: (jnp.maximum(r - 2, 0), 0))
    up_spec = pl.BlockSpec((1, width, step_cols), lambda f, r: (0, 0, f))
    down_spec = pl.BlockSpec((1, width, step_cols), lambda f, r: (1, 0, f))
    out_spec = pl.BlockSpec((step_rows, step_cols), lambda f, r: (r, f))
    shape = jax.ShapeDtypeStruct((2 * rows, hidden), jnp.bfloat16)
    return pl.pallas_call(
        ffn_kernel,
        grid=(2, 4),
        in_specs=[pair_spec, far_spec, pair_spec, far_spec, up_spec, down_spec],
        out_specs=[out_spec, out_spec],
        out_shape=(shape, shape),
        compiler_params=pltpu.CompilerParams(vmem_limit_bytes=48 * 1024 * 1024),
        cost_estimate=pl.CostEstimate(flops=1_000_000, bytes_accessed=100_000, transcendentals=0),
    )(*normed, *cot, weights, weights)


def masked_heads(values_in, lanes, head, scale):
    keep = (lanes >= head * HEAD_DIM) & (lanes < (head + 1) * HEAD_DIM)
    return jnp.where(keep, values_in * scale, jnp.zeros_like(values_in))


def in_order(info_ref, source, held, rows):
    for piece in range(4):
        start = pl.multiple_of((info_ref[0] ^ piece) * rows, rows)
        held[piece * rows : (piece + 1) * rows, :] = source(pl.ds(start, rows))


def out_of_order(info_ref, held, store, rows):
    for piece in range(4):
        start = pl.multiple_of((info_ref[0] ^ piece) * rows, rows)
        store(pl.ds(start, rows), held[piece * rows : (piece + 1) * rows, :])


def block_bias(info_ref, query, key):
    return jnp.where(info_ref[1 + query] <= key * SHORT, 0.0, -1e30).astype(jnp.float32)


def forward_kernel(info_ref, qkv_ref, out_ref, query_held, key_held, value_held, out_held):
    rows = qkv_ref.shape[1] // 4
    for part, held in enumerate((query_held, key_held, value_held)):
        in_order(info_ref, lambda at, part=part: qkv_ref[part, at, :], held, rows)
    lanes = lax.broadcasted_iota(jnp.int32, (SHORT, 128), 1)
    earlier = lax.broadcasted_iota(jnp.int32, (SHORT, SHORT), 1) <= lax.broadcasted_iota(
        jnp.int32, (SHORT, SHORT), 0
    )
    for query in range(qkv_ref.shape[1] // SHORT):
        query_rows = query_held[query * SHORT : (query + 1) * SHORT, :]
        outs = []
        for head in range(2):
            query_head = masked_heads(query_rows, lanes, head, HEAD_DIM**-0.5)
            scores, biases = [], []
            for key in range(query + 1):
                score = lax.dot_general(
                    query_head,
                    key_held[key * SHORT : (key + 1) * SHORT, :],
                    (((1,), (1,)), ((), ())),
                    preferred_element_type=jnp.float32,
                )
                scores.append(jnp.where(earlier, score, -1e30) if key == query else score)
                biases.append(block_bias(info_ref, query, key))
            top = scores[query].max(axis=1, keepdims=True)
            for score, bias in zip(scores[:query], biases):
                top = jnp.maximum(top, score.max(axis=1, keepdims=True) + bias)
            mass = jnp.zeros_like(top)
            total = jnp.zeros((SHORT, 128), jnp.float32)
            for key in range(query + 1):
                chance = jnp.exp(scores[key] - (top - biases[key]))
                mass = mass + chance.sum(axis=1, keepdims=True)
                total = total + jnp.dot(
                    chance.astype(jnp.bfloat16),
                    value_held[key * SHORT : (key + 1) * SHORT, :],
                    preferred_element_type=jnp.float32,
                )
            outs.append(total / mass)
        out = jnp.where(lanes < HEAD_DIM, outs[0], outs[1])
        out_held[query * SHORT : (query + 1) * SHORT, :] = out.astype(jnp.bfloat16)

    def store(at, values_in):
        out_ref[at, :] = values_in

    out_of_order(info_ref, out_held, store, rows)


def backward_kernel(
    info_ref,
    qkv_ref,
    grad_ref,
    out_ref,
    query_held,
    key_held,
    value_held,
    grad_held,
    key_turned,
    query_grad,
    key_grad,
    value_grad,
):
    rows = qkv_ref.shape[1] // 4
    for part, held in enumerate((query_held, key_held, value_held)):
        in_order(info_ref, lambda at, part=part: qkv_ref[part, at, :], held, rows)
    in_order(info_ref, lambda at: grad_ref[at, :], grad_held, rows)
    key_turned[...] = key_held[...].astype(jnp.float32).T.astype(jnp.bfloat16)
    lanes = lax.broadcasted_iota(jnp.int32, (SHORT, 128), 1)
    earlier = lax.broadcasted_iota(jnp.int32, (SHORT, SHORT), 0) <= lax.broadcasted_iota(
        jnp.int32, (SHORT, SHORT), 1
    )
    blocks = qkv_ref.shape[1] // SHORT
    for query in range(blocks):
        at_query = slice(query * SHORT, (query + 1) * SHORT)
        query_rows = query_held[at_query, :]
        grad_rows = grad_held[at_query, :]
        turned_grads = []
        for head in range(2):
            query_head = masked_heads(query_rows, lanes, head, HEAD_DIM**-0.5)
            grad_head = masked_heads(grad_rows, lanes, head, 1.0)
            scores, biases = [], []
            for key in range(query + 1):
                score = lax.dot_general(
                    key_held[key * SHORT : (key + 1) * SHORT, :],
                    query_head,
                    (((1,), (1,)), ((), ())),
                    preferred_element_type=jnp.float32,
                )
                scores.append(jnp.where(earlier, score, -1e30) if key == query else score)
                biases.append(block_bias(info_ref, query, key))
            top = scores[query].max(axis=0, keepdims=True)
            for score, bias in zip(scores[:query], biases):
                top = jnp.maximum(top, score.max(axis=0, keepdims=True) + bias)
            mass = jnp.zeros_like(top)
            inner = jnp.zeros_like(top)
            chances, slopes = [], []
            for key in range(query + 1):
                slope = lax.dot_general(
                    value_held[key * SHORT : (key + 1) * SHORT, :],
                    grad_head,
                    (((1,), (1,)), ((), ())),
                    preferred_element_type=jnp.float32,
                )
                chance = jnp.exp(scores[key] - (top - biases[key]))
                mass = mass + chance.sum(axis=0, keepdims=True)
                inner = inner + (chance * slope).sum(axis=0, keepdims=True)
                chances.append(chance)
                slopes.append(slope)
            share = 1.0 / mass
            inner = inner * share
            total = None
            for key in range(query + 1):
                at_key = slice(key * SHORT, (key + 1) * SHORT)
                probs = chances[key] * share
                grad_scores = (probs * (slopes[key] - inner)).astype(jnp.bfloat16)
                value_part = jnp.dot(
                    probs.astype(jnp.bfloat16), grad_head, preferred_element_type=jnp.float32
                )
                key_part = jnp.dot(grad_scores, query_head, preferred_element_type=jnp.float32)
                if head == 0 and key == query:
                    value_grad[at_key, :] = value_part
                    key_grad[at_key, :] = key_part
                else:
                    value_grad[at_key, :] += value_part
                    key_grad[at_key, :] += key_part
                part = jnp.dot(
                    key_turned[head * HEAD_DIM : (head + 1) * HEAD_DIM, at_key],
                    grad_scores,
                    preferred_element_type=jnp.float32,
                )
                total = part if total is None else total + part
            turned_grads.append(total)
        turned = jnp.concatenate(turned_grads, axis=0)
        query_grad[at_query, :] = turned.T * (HEAD_DIM**-0.5)

    for part, held in enumerate((query_grad, key_grad, value_grad)):

        def store(at, values_in, part=part):
            out_ref[part, at, :] = values_in.astype(jnp.bfloat16)

        out_of_order(info_ref, held, store, rows)


def attend(info, qkv):
    _, rows, width = qkv.shape
    held = pltpu.VMEM((rows, 128), jnp.bfloat16)
    return pl.pallas_call(
        forward_kernel,
        grid_spec=pltpu.PrefetchScalarGridSpec(
            num_scalar_prefetch=1,
            grid=(width // 128,),
            in_specs=[pl.BlockSpec((3, rows, 128), lambda pair, info_ref: (0, 0, pair))],
            out_specs=pl.BlockSpec((rows, 128), lambda pair, info_ref: (0, pair)),
            scratch_shapes=[held] * 4,
        ),
        out_shape=jax.ShapeDtypeStruct((rows, width), jnp.bfloat16),
        compiler_params=pltpu.CompilerParams(vmem_limit_bytes=48 * 1024 * 1024),
        cost_estimate=pl.CostEstimate(flops=1_000_000, bytes_accessed=100_000, transcendentals=0),
    )(info, qkv)


def attend_back(info, qkv, grad_heads, pair, earlier):
    _, rows, width = qkv.shape
    extra = [] if earlier is None else [pl.BlockSpec(memory_space=pl.ANY)]

    def kernel(info_ref, qkv_ref, grad_ref, *others):
        backward_kernel(info_ref, qkv_ref, grad_ref, *others[len(extra) :])

    return pl.pallas_call(
        kernel,
        grid_spec=pltpu.PrefetchScalarGridSpec(
            num_scalar_prefetch=1,
            grid=(1,),
            in_specs=[
                pl.BlockSpec((3, rows, 128), lambda step, info_ref: (0, 0, pair)),
                pl.BlockSpec((rows, 128), lambda step, info_ref: (0, pair)),
            ]
            + extra,
            out_specs=pl.BlockSpec((3, rows, 128), lambda step, info_ref: (0, 0, pair)),
            scratch_shapes=[pltpu.VMEM((rows, 128), jnp.bfloat16)] * 4
            + [pltpu.VMEM((128, rows), jnp.bfloat16)]
            + [pltpu.VMEM((rows, 128), jnp.float32)] * 3,
        ),
        out_shape=jax.ShapeDtypeStruct(qkv.shape, jnp.bfloat16),
        input_output_aliases={} if earlier is None else {3: 0},
        compiler_params=pltpu.CompilerParams(vmem_limit_bytes=48 * 1024 * 1024),
        cost_estimate=pl.CostEstimate(flops=1_000_000, bytes_accessed=100_000, transcendentals=0),
    )(info, qkv, grad_heads, *([] if earlier is None else [earlier]))


def regrouped(
    tokens_in,
    lm_grad,
    lm_logprob,
    targets,
    neighbor_ids,
    nearby_entry_gaps,
    seq_lengths,
    attn_weights,
    ffn_weights,
    attn_left,
    attn_right,
    ffn_left,
    ffn_right,
    attn_left_root,
    attn_right_root,
    ffn_left_root,
    ffn_right_root,
    norm_params,
    norm_moment1,
    norm_moment2,
    blending_coefficients,
    knn_moment1,
    knn_moment2,
):
    low = jnp.bfloat16
    rows = tokens_in.shape[0]
    group_rows = 4 * rows
    dp_index, tensor_index = lax.axis_index("dp"), lax.axis_index("tensor")
    place = {
        "line": tensor_index & 1,
        "half": tensor_index >> 1,
        "core": dp_index & 1,
        "x": (dp_index >> 1) & 1,
        "y": dp_index >> 2,
        "chip": dp_index >> 1,
    }
    me = place["core"] * 2 + place["line"]
    chip, core = place["chip"], place["core"]
    staying = core == place["half"]

    where = jnp.stack(
        [
            chip,
            core,
            tensor_index,
            place["line"],
            place["half"],
            place["line"] ^ place["x"],
            place["y"],
        ]
    ).astype(jnp.int32)
    tokens_one = swap_or_near(tokens_in)
    wa_mine, wa_theirs = halve(where, attn_weights)
    wa = unite(where, wa_mine, flip(wa_theirs, CORE_BIT))
    wa, ffn_weights_in, nearby_entry_gaps, lengths_in = together(
        wa, ffn_weights, nearby_entry_gaps, seq_lengths
    )
    wa_other = flip(wa, HALF_BIT)
    wf_mine, wf_theirs = halve(where, ffn_weights_in)
    wf = unite(where, wf_mine, flip(wf_theirs, CORE_BIT))
    other_lengths = flip(lengths_in.astype(jnp.float32), CORE_BIT).astype(jnp.int32)
    lengths = jnp.where(staying, seq_lengths, other_lengths)
    params = by_chip(norm_params, chip)
    block_begins = first_blocks(lengths, group_rows, SHORT) * SHORT
    info = jnp.concatenate([me[None].astype(jnp.int32), block_begins.astype(jnp.int32)])
    cot_low, knn_sums = neighbours(
        where,
        blending_coefficients,
        nearby_entry_gaps,
        neighbor_ids,
        targets,
        lm_logprob,
        lm_grad,
    )
    tokens_one, wf, params, info, wa_other, cot_low = together(
        tokens_one, wf, params, info, wa_other, cot_low
    )
    tokens_two = near_of_moved(tokens_one)
    wa = weight_halves(wa, wa_other, place)
    wa_first = cross_one(wa)
    wf_other = flip(wf, HALF_BIT)
    tokens_one, tokens_two, wa_first, cot_low = together(tokens_one, tokens_two, wa_first, cot_low)
    pair1 = jnp.concatenate(
        [
            jnp.where(staying, tokens_in, tokens_one),
            jnp.where(staying, tokens_one, tokens_two),
        ],
        axis=0,
    )
    far1 = flip(pair1, CORE_BIT)
    wa_pair = cross_two(jnp.stack([wa, wa_first]))
    cot_one = swap_or_near(cot_low)
    far1, pair1 = together(far1, pair1)
    normed1_all, own_low = normalize(where, pair1, far1, params)
    resid = own_low.astype(jnp.float32)
    normed1_all, wa_pair = together(normed1_all, wa_pair)
    wa_all = by_rel(core, wa, wa_first, wa_pair, 1)
    proj_in, proj_out = wa_all[:3], wa_all[3]

    qkv = dot32("rd,sdc->src", normed1_all, proj_in).astype(low)
    heads_flat = attend(info, qkv)
    heads_flat, wf_other, wf, cot_one = together(heads_flat, wf_other, wf, cot_one)

    def out_rows(a, b):
        return dot32("rc,dc->rd", heads_flat[a:b], proj_out)

    sent4 = out_rows(2 * rows, 4 * rows).astype(low)
    sent4, wf, heads_flat = together(sent4, weight_halves(wf, wf_other, place), heads_flat)
    received4 = flip(sent4, CORE_BIT)
    wf_first = cross_one(wf)
    near4 = (out_rows(rows, 2 * rows) + received4[rows:].astype(jnp.float32)).astype(low)
    near4, heads_flat = together(near4, heads_flat)
    from_near4 = flip(near4, LINE_BIT)
    attn_out = out_rows(0, rows) + received4[:rows].astype(jnp.float32)
    attn_out, cot_one = together(attn_out, cot_one)
    cot_two = near_of_moved(cot_one)
    attn_out, from_near4, wf_first = together(attn_out, from_near4, wf_first)
    middle = resid + attn_out + from_near4.astype(jnp.float32)
    normed2, norm2_back = jax.vjp(layer_norm, middle, params[2], params[3])
    normed2_low = normed2.astype(low)
    near2 = flip(normed2_low, LINE_BIT)
    wf_pair = cross_two(jnp.stack([wf, wf_first]))
    near2, cot_one, cot_two, normed2_low = together(near2, cot_one, cot_two, normed2_low)
    cot_moved = jnp.where(staying, cot_low, cot_one)
    pair_cot = jnp.concatenate([cot_moved, jnp.where(staying, cot_one, cot_two)], axis=0)
    cotangent = cot_moved.astype(jnp.float32)
    pair2 = jnp.concatenate([normed2_low, near2], axis=0)
    far2 = flip(pair2, CORE_BIT)
    far_cot = flip(pair_cot, CORE_BIT)
    wf_all = by_rel(core, wf, wf_first, wf_pair, 1)

    far2, wf_all = together(far2, wf_all)
    act_low, grad_pre_low = ffn_middle((pair2, far2), (pair_cot, far_cot), wf_all)

    def back_rows(a, b):
        return dot32("rf,df->rd", grad_pre_low[a:b], wf_all[0])

    sent2 = back_rows(2 * rows, 4 * rows).astype(low)
    sent2, pair2, far2, pair_cot, far_cot, act_low = together(
        sent2, pair2, far2, pair_cot, far_cot, act_low
    )
    normed2_all = jnp.concatenate([pair2, far2], axis=0)
    cot_all = jnp.concatenate([pair_cot, far_cot], axis=0)
    received2 = flip(sent2, CORE_BIT)
    cut = ffn_weights.shape[2] // 2
    up_halves = [
        dot32("rd,rf->df", normed2_all, grad_pre_low[:, :cut]).astype(low),
        dot32("rd,rf->df", normed2_all, grad_pre_low[:, cut:]).astype(low),
    ]
    up_kept, up_sent = scatter_parts(core, up_halves)
    up_got = cross_one(up_sent)
    near2 = back_rows(rows, 2 * rows) + received2[rows:].astype(jnp.float32)
    near2, act_low = together(near2.astype(low), act_low)
    from_near2 = flip(near2, LINE_BIT)
    own2 = back_rows(0, rows) + received2[:rows].astype(jnp.float32)
    down_halves = [
        dot32("rd,rf->df", cot_all, act_low[:, :cut]).astype(low),
        dot32("rd,rf->df", cot_all, act_low[:, cut:]).astype(low),
    ]
    down_kept, down_sent = scatter_parts(core, down_halves)
    down_got = cross_one(down_sent)
    own2, from_near2 = together(own2, from_near2)
    grad_normed2 = own2 + from_near2.astype(jnp.float32)
    mid_norm_grad, gain2_grad, shift2_grad = norm2_back(grad_normed2)
    grad_middle = cotangent + mid_norm_grad
    mid_low, act_low = together(grad_middle.astype(low), act_low)
    near_mid = flip(mid_low, LINE_BIT)
    out_sent = dot32("rf,df->rd", act_low[2 * rows :], wf_all[1]).astype(low)
    up_got, down_got, out_sent, act_low = together(up_got, down_got, out_sent, act_low)
    ffn_kept = jnp.concatenate([add_low(up_kept, up_got), add_low(down_kept, down_got)], axis=0)
    ffn_got = cross_two(ffn_kept[:, 1])
    out_received = flip(out_sent, CORE_BIT)
    out_near = dot32("rf,df->rd", act_low[rows : 2 * rows], wf_all[1]) + out_received[rows:].astype(
        jnp.float32
    )
    ffn_out = dot32("rf,df->rd", act_low[:rows], wf_all[1]) + out_received[:rows].astype(jnp.float32)
    near_mid, ffn_got, out_near, ffn_out, mid_low = together(
        near_mid, ffn_got, out_near.astype(low), ffn_out, mid_low
    )
    pair_mid = jnp.concatenate([mid_low, near_mid], axis=0)
    far_mid = flip(pair_mid, CORE_BIT)
    ffn_part = add_low(ffn_kept[:, 0], ffn_got)
    ffn_other = flip(ffn_part, HALF_BIT)
    out_from_near = flip(out_near, LINE_BIT)

    grad_heads = jnp.concatenate(
        [dot32("rd,dc->rc", part, proj_out).astype(low) for part in (pair_mid, far_mid)], axis=0
    )
    grad_half = attend_back(info, qkv, grad_heads, 0, None)
    grad_half, pair_mid, far_mid = together(grad_half, pair_mid, far_mid)
    grad_out_proj = dot32("rd,rc->dc", pair_mid, heads_flat[: 2 * rows]) + dot32(
        "rd,rc->dc", far_mid, heads_flat[2 * rows :]
    )
    grad_out_proj = grad_out_proj.astype(low)
    grad_qkv = attend_back(info, qkv, grad_heads, 1, grad_half)
    grad_qkv, grad_out_proj = together(grad_qkv, grad_out_proj)

    def back_in(a, b):
        return dot32("src,sdc->rd", grad_qkv[:, a:b], proj_in)

    grad_parts = [
        dot32("rd,rc->dc", normed1_all, grad_qkv[part]).astype(low) for part in range(3)
    ] + [grad_out_proj]
    attn_kept, attn_sent = scatter_parts(core, grad_parts)
    sent1 = back_in(2 * rows, 4 * rows).astype(low)
    attn_kept, attn_sent, sent1, grad_qkv, ffn_other, out_from_near = together(
        attn_kept, attn_sent, sent1, grad_qkv, ffn_other, out_from_near
    )

    attn_got = cross_one(attn_sent)
    received1 = flip(sent1, CORE_BIT)
    ffn_own = add_low(ffn_part, ffn_other)
    ffn_near = flip(ffn_own, LINE_BIT)
    near3 = back_in(rows, 2 * rows) + received1[rows:].astype(jnp.float32)
    near3, grad_qkv = together(near3.astype(low), grad_qkv)
    from_near3 = flip(near3, LINE_BIT)
    own3 = back_in(0, rows) + received1[:rows].astype(jnp.float32)
    attn_got, attn_kept, own3, ffn_out = together(attn_got, attn_kept, own3, ffn_out)

    attn_kept = add_low(attn_kept, attn_got)
    attn_kept, own3, ffn_out = together(attn_kept, own3, ffn_out)
    attn_got = cross_two(attn_kept[:, 1])
    ffn_out = ffn_out + out_from_near.astype(jnp.float32)
    mixed = by_chip((middle + ffn_out).astype(low), chip)
    attn_got, attn_kept, own3, ffn_near, ffn_own, mixed = together(
        attn_got, attn_kept, own3, ffn_near, ffn_own, mixed
    )

    attn_part = add_low(attn_kept[:, 0], attn_got)
    ffn_line = jnp.stack([ffn_own, ffn_near])
    attn_part, own3, ffn_line, mixed = together(attn_part, own3, ffn_line, mixed)
    attn_other = flip(attn_part, HALF_BIT)
    ffn_first = cross_one(ffn_line)
    attn_other, attn_part, ffn_first, ffn_line, own3, mixed = together(
        attn_other, attn_part, ffn_first, ffn_line, own3, mixed
    )

    attn_own = add_low(attn_part, attn_other)
    ffn_two = jnp.stack([ffn_line, ffn_first])
    attn_own, own3, ffn_two = together(attn_own, own3, ffn_two)
    attn_near = flip(attn_own, LINE_BIT)
    ffn_pair = cross_two(ffn_two)
    input_grad, gain_sums = norm_back(
        where, own3, from_near3, own_low, grad_middle, params[0:1]
    )
    attn_near, attn_own, gain_sums, input_grad, mixed = together(
        attn_near, attn_own, gain_sums, input_grad, mixed
    )

    attn_line = jnp.stack([attn_own, attn_near])
    norm_grads = jnp.concatenate([gain_sums, gain2_grad[None], shift2_grad[None]], axis=0)
    small = jnp.concatenate([by_chip(norm_grads, chip), knn_sums], axis=0)
    left_low = jnp.concatenate([attn_left_root.astype(low), ffn_left_root.astype(low)], axis=0)
    left_low = jnp.concatenate([left_low, flip(left_low, CORE_BIT)], axis=1)
    attn_line, small, attn_left_low, ffn_left_low, mixed, input_grad = together(
        attn_line, small, left_low[:4], left_low[4:], mixed, input_grad
    )
    attn_first = cross_one(attn_line)
    mixed = swap_core_half(mixed)
    input_grad = swap_core_half(input_grad)
    small = small + flip(small, CORE_BIT)
    attn_first, attn_line, small, mixed, input_grad = together(
        attn_first, attn_line, small, mixed, input_grad
    )

    attn_pair = cross_two(jnp.stack([attn_line, attn_first]))
    small = small + flip(small, HALF_BIT)
    ffn_pair, small = together(ffn_pair, small)
    small = small + flip(small, LINE_BIT)
    ffn_pieces = (ffn_line, ffn_first, ffn_pair)
    ffn_own, ffn_sent = updates(where, ffn_left_low, ffn_pieces, ffn_right_root, True)
    ffn_half = tuple(right_half(where, ffn_pieces, None, ffn_right, ffn_weights.shape[1], None))
    ffn_own, ffn_half = together(ffn_own, ffn_half)
    attn_pair, attn_first, attn_line, ffn_own, ffn_sent, ffn_line, ffn_first, ffn_pair, small = (
        together(
            attn_pair,
            attn_first,
            attn_line,
            ffn_own,
            ffn_sent,
            ffn_line,
            ffn_first,
            ffn_pair,
            small,
        )
    )

    ffn_pieces = (ffn_line, ffn_first, ffn_pair)
    attn_pieces = (attn_line, attn_first, attn_pair)
    attn_cols = column_block(attn_pieces, None, place["half"], False)
    ffn_cols = column_block(ffn_pieces, None, place["half"], True)
    attn_cols_other = flip(attn_cols, CORE_BIT)
    ffn_cols_other = flip(ffn_cols, CORE_BIT)
    ffn_received = flip(ffn_sent, CORE_BIT)
    attn_own, attn_sent = updates(where, attn_left_low, attn_pieces, attn_right_root, False)
    small = small + flip(small, X_BIT)
    attn_sent, small = together(attn_sent, small)
    attn_received = flip(attn_sent, CORE_BIT)
    summed = small + flip(small, Y_BIT)
    ffn_right_new, ffn_grad = right_half(
        where, ffn_pieces, ffn_cols_other, ffn_right, ffn_weights.shape[1], ffn_half
    )
    attn_right_new, attn_grad = right_statistics_new(
        where, attn_pieces, attn_cols_other, attn_right, attn_weights.shape[1], False
    )
    summed, ffn_right_new, attn_right_new = together(summed, ffn_right_new, attn_right_new)
    ffn_left_new, ffn_new = shampoo_left(ffn_own, ffn_received, ffn_left, ffn_weights)
    attn_left_new, attn_new = shampoo_left(attn_own, attn_received, attn_left, attn_weights)
    input_grad = input_grad.astype(jnp.float32)
    norm_total = summed[:4]
    knn_total = summed[4, :2]
    loss = summed[4, 2] / (group_rows * 8)
    norm_m1, norm_m2, norm_new = adamw_step(norm_params, norm_total, norm_moment1, norm_moment2)
    knn_m1, knn_m2, knn_new = adamw_step(blending_coefficients, knn_total, knn_moment1, knn_moment2)
    return (
        mixed,
        input_grad,
        loss,
        attn_grad,
        attn_left_new,
        attn_right_new,
        attn_new,
        ffn_grad,
        ffn_left_new,
        ffn_right_new,
        ffn_new,
        norm_m1,
        norm_m2,
        norm_new,
        knn_m1,
        knn_m2,
        knn_new,
    )


def solution(mesh):
    sized = (mesh.shape["dp"], mesh.shape["tensor"]) == (8, 4)
    placed = (
        P(("dp", "tensor"), None),
        P(("dp", "tensor"), None),
        P(("dp", "tensor")),
        P(("dp", "tensor")),
        P(("dp", "tensor"), None),
        P(("dp", "tensor"), None),
        P("dp", None),
        P(None, "dp", "tensor"),
        P(None, "dp", "tensor"),
        P(None, "dp", "tensor"),
        P(None, "tensor", "dp"),
        P(None, "dp", "tensor"),
        P(None, "tensor", "dp"),
        P(None, "dp", None),
        P(None, None, "tensor"),
        P(None, "dp", None),
        P(None, None, "tensor"),
        P(),
        P(),
        P(),
        P(),
        P(),
        P(),
    )
    return jax.shard_map(
        regrouped if sized else local,
        mesh=mesh,
        in_specs=placed,
        out_specs=(
            P(("dp", "tensor"), None),
            P(("dp", "tensor"), None),
            P(),
            P(None, "dp", "tensor"),
            P(None, "dp", "tensor"),
            P(None, "tensor", "dp"),
            P(None, "dp", "tensor"),
            P(None, "dp", "tensor"),
            P(None, "dp", "tensor"),
            P(None, "tensor", "dp"),
            P(None, "dp", "tensor"),
            P(),
            P(),
            P(),
            P(),
            P(),
            P(),
        ),
        check_vma=False,
    )
```
